32 devices in a mesh: pix: 8 (over z, x), rep: 4 (over y, core).
Axes of the slice: x: 2, y: 2, z: 4, core: 2. Of those that a mesh axis runs over, the one named last changes fastest.
Arguments:
- tokens: bfloat16 [4096, 24, 128], P(('pix', 'rep')), may hold values from -6 to 6
- lengths: int32 [4096], P(('pix', 'rep')), may hold values from 3 to 24, as said below
- masked: int32 [4096, 24], P(('pix', 'rep')), may hold values from 0 to 1, as said below
- route_dev: int32 [4096], P(('pix', 'rep')), may hold values from 0 to 7, as said below
- route_slot: int32 [4096], P(('pix', 'rep')), may hold values from 0 to 127, as said below
- norm_gain: float32 [2, 2, 128], replicated, may hold values from 0.5 to 1.5
- norm_bias: float32 [2, 2, 128], replicated, may hold values from -1.75 to 1.75
- w_qkv: bfloat16 [2, 128, 384], replicated, may hold values from -0.5 to 0.5
- w_out: bfloat16 [2, 128, 128], replicated, may hold values from -1 to 1
- w_up: bfloat16 [2, 128, 512], replicated, may hold values from -0.5 to 0.5
- b_up: float32 [2, 512], replicated, may hold values from -1.75 to 1.75
- w_down: bfloat16 [2, 512, 128], replicated, may hold values from -0.25 to 0.25
- b_down: float32 [2, 128], replicated, may hold values from -1.75 to 1.75
- mask_token: float32 [128], replicated, may hold values from -6 to 6
- pos_table: float32 [24, 128], replicated, may hold values from -3 to 3
- cotangent: bfloat16 [4096, 24, 128], P(('pix', 'rep')), may hold values from -6 to 6
Outputs:
- dec_output: float32 [4096, 24, 128], P(('pix', 'rep'))
- grad_tokens: float32 [4096, 24, 128], P(('pix', 'rep'))
- grad_norm_gain: float32 [2, 2, 128], replicated
- grad_norm_bias: float32 [2, 2, 128], replicated
- grad_w_qkv: float32 [2, 128, 384], replicated
- grad_w_out: float32 [2, 128, 128], replicated
- grad_w_up: float32 [2, 128, 512], replicated
- grad_b_up: float32 [2, 512], replicated
- grad_w_down: float32 [2, 512, 128], replicated
- grad_b_down: float32 [2, 128], replicated
- grad_mask_token: float32 [128], replicated
- grad_pos_table: float32 [24, 128], replicated
The draws below stay inside these ranges and needn't reach their ends.
Inputs may be any that keep to these rules, and one draw needn't show every extreme that they name: `lengths`: the first series of every device has length 24. masked is 1 at and beyond the length; below it each series has 1 to 8 unmasked slots, exactly 8 in the first series of every device. Within each rep index the series form a one-to-one map onto decoder slots; route_dev minus the sender's pix index (modulo 8) and route_slot depend only on the series' slot and rep index; no device of pix sends more than 32 series to one device, and in each rep group some pair sends exactly 32. `route_slot`: every decoder slot of every device is named exactly once within its rep group.
All inputs are finite; a program needn't handle non-finite values.
Results may differ from the reference program's by a relative error of at most 0.014.
Values may be sent and summed in bfloat16 or wider, within the bound.
No kernel may reach another device: no remote copies, remote signals or barrier semaphores. Data moves between devices by JAX's collectives and lax.ppermute only.
A program may use at most 192 MiB of HBM per device.

```python
import math
import jax
import jax.numpy as jnp
from jax import lax

D = 128
HEADS = 8
HEAD_DIM = 16
FF = 512
SEQ = 24
VIS = 8
PIX_DEV = 128
CAP = 32
PIXELS = 4096
N_PIX = 8
N_REP = 4


def series_layout(key):
    len_key, count_key, order_key = jax.random.split(key, 3)
    pixel_ids = jnp.arange(PIXELS)
    leading = pixel_ids % PIX_DEV == 0
    lengths = jax.random.randint(len_key, (PIXELS,), 3, SEQ + 1)
    lengths = jnp.where(leading, SEQ, lengths)
    counts = jnp.minimum(jax.random.randint(count_key, (PIXELS,), 1, VIS + 1), lengths)
    counts = jnp.where(leading, VIS, counts)
    places = jnp.arange(SEQ)
    raw = jax.random.randint(order_key, (PIXELS, SEQ), 0, 1 << 20) * SEQ + places[None, :]
    outside = places[None, :] >= lengths[:, None]
    raw = jnp.where(outside, raw + (1 << 20) * SEQ, raw)
    ranking = jnp.argsort(jnp.argsort(raw, axis=1), axis=1)
    masked = jnp.where(ranking < counts[:, None], 0, 1).astype(jnp.int32)
    return (lengths.astype(jnp.int32), masked)


def route_layout(key):
    perm_key, pick_key, slot_key = jax.random.split(key, 3)
    tickets = N_PIX * CAP
    ticket_ids = jnp.arange(tickets)
    raw = jax.random.randint(perm_key, (N_REP, tickets), 0, 1 << 20) * tickets + ticket_ids[None, :]
    position = jnp.argsort(jnp.argsort(raw, axis=1), axis=1)
    chosen = jax.random.randint(pick_key, (N_REP,), 0, N_PIX)
    favored = ticket_ids[None, :] // CAP == chosen[:, None]
    ordering = jnp.where(favored, ticket_ids[None, :] % CAP - CAP, position)
    picked = jnp.argsort(ordering, axis=1)[:, :PIX_DEV]
    offsets = picked // CAP
    slot_raw = jax.random.randint(slot_key, (N_REP, PIX_DEV), 0, 1 << 20) * PIX_DEV + jnp.arange(PIX_DEV)[None, :]
    shuffle = jnp.argsort(slot_raw, axis=1)
    pixel_ids = jnp.arange(PIXELS)
    device = pixel_ids // (N_REP * PIX_DEV)
    group = pixel_ids // PIX_DEV % N_REP
    slot_index = pixel_ids % PIX_DEV
    route_dev = (device + offsets[group, slot_index]) % N_PIX
    route_slot = shuffle[group, slot_index]
    return (route_dev.astype(jnp.int32), route_slot.astype(jnp.int32))


def draw_lengths(key, part):
    lengths, masked = series_layout(key)
    return lengths


def draw_masked(key, part):
    lengths, masked = series_layout(key)
    return masked


def draw_route_dev(key, part):
    route_dev, route_slot = route_layout(key)
    return route_dev


def draw_route_slot(key, part):
    route_dev, route_slot = route_layout(key)
    return route_slot


def steps_of(rng, shape, cuts, smallest, high):
    loudness, own = 1.0, jax.random.fold_in(rng, 6)
    for dim, parts in cuts:
        steps = jnp.exp(jax.random.uniform(jax.random.fold_in(own, dim), (parts,), jnp.float32, smallest / len(cuts), high / len(cuts)))
        loudness = loudness * jnp.repeat(steps, shape[dim] // parts).reshape([-1 if axis == dim else 1 for axis in range(len(shape))])
    return loudness


def scatter_about(own_key, extent, scale, reach, cuts=(), kind=jnp.bfloat16):
    values = scale * jax.random.normal(own_key, extent, jnp.float32)
    if cuts:
        values = values * steps_of(own_key, extent, cuts, -0.22, 0.18)
    return jnp.clip(values, -reach, reach).astype(kind)


def setup_inputs(seed: int = 0) -> dict:
    splits = jax.random.split(jax.random.key(seed), 17)
    return {
        "tokens": scatter_about(splits[0], (PIXELS, SEQ, D), 1.0, 6.0, ((0, 32),)),
        "lengths": draw_lengths(jax.random.fold_in(splits[16], 71), 0),
        "masked": draw_masked(jax.random.fold_in(splits[16], 71), 0),
        "route_dev": draw_route_dev(jax.random.fold_in(splits[16], 71), 0),
        "route_slot": draw_route_slot(jax.random.fold_in(splits[16], 71), 0),
        "norm_gain": jnp.clip(1.0 + 0.1 * jax.random.normal(splits[5], (2, 2, D), jnp.float32), 0.5, 1.5),
        "norm_bias": scatter_about(splits[6], (2, 2, D), 0.3, 1.75, (), jnp.float32),
        "w_qkv": scatter_about(splits[7], (2, D, 3 * D), D ** -0.5, 0.5),
        "w_out": scatter_about(splits[8], (2, D, D), (D // 4) ** -0.5, 1.0),
        "w_up": scatter_about(splits[9], (2, D, FF), D ** -0.5, 0.5),
        "b_up": scatter_about(splits[10], (2, FF), 0.3, 1.75, (), jnp.float32),
        "w_down": scatter_about(splits[11], (2, FF, D), FF ** -0.5, 0.25),
        "b_down": scatter_about(splits[12], (2, D), 0.3, 1.75, (), jnp.float32),
        "mask_token": scatter_about(splits[13], (D,), 1.0, 6.0, (), jnp.float32),
        "pos_table": scatter_about(splits[14], (SEQ, D), 0.5, 3.0, (), jnp.float32),
        "cotangent": scatter_about(splits[15], (PIXELS, SEQ, D), 1.0, 6.0, ((0, 32),)),
    }


@jax.custom_vjp
def low(v):
    return lax.optimization_barrier(v.astype(jnp.bfloat16)).astype(jnp.float32)

@jax.custom_vjp
def low_back(v):
    return v

def low_keep(v):
    return (low(v), None)

def low_pass(kept, grad):
    return (grad,)

def back_keep(v):
    return (v, None)

def back_low(kept, grad):
    return (low(grad),)
low.defvjp(low_keep, low_pass)
low_back.defvjp(back_keep, back_low)
precise = lax.Precision.HIGHEST

def product(left, right, form):
    return jnp.einsum(form, left, right, precision=precise)

def normalize(values):
    centre = lax.optimization_barrier(jnp.mean(values, axis=-1, keepdims=True))
    centered = values - centre
    return centered * lax.rsqrt(lax.optimization_barrier(jnp.mean(centered * centered, axis=-1, keepdims=True)) + 1e-05)

def layer(inputs, key_valid, gains, shifts, w_qkv, w_out, w_up, b_up, w_down, b_down):
    pixels, seq_slots, model_width = inputs.shape
    norm_one = low(normalize(inputs) * gains[0] + shifts[0])
    projected = low(low_back(product(norm_one, w_qkv, 'psd,de->pse')))
    projected = projected.reshape(pixels, seq_slots, 3, HEADS, HEAD_DIM)
    queries = projected[:, :, 0]
    key_rows = projected[:, :, 1]
    value_rows = projected[:, :, 2]
    scaling = 1.0 / math.sqrt(HEAD_DIM)
    scores = low_back(product(queries, key_rows, 'pshe,pthe->phst') * scaling)
    scores = jnp.where(key_valid[:, None, None, :], scores, -1e+30)
    attn_probs = jax.nn.softmax(scores, axis=-1)
    mixed_rows = product(low(attn_probs), value_rows, 'phst,pthe->pshe')
    attended = low(low_back(mixed_rows.reshape(pixels, seq_slots, model_width)))
    middle = inputs + low_back(product(attended, w_out, 'psd,de->pse'))
    norm_two = low(normalize(middle) * gains[1] + shifts[1])
    hidden = low_back(product(norm_two, w_up, 'psd,df->psf') + b_up)
    active = low(jax.nn.gelu(hidden, approximate=False))
    return middle + low_back(product(active, w_down, 'psf,fd->psd') + b_down)

def reference(tokens, lengths, masked, route_dev, route_slot, norm_gain, norm_bias, w_qkv, w_out, w_up, b_up, w_down, b_down, mask_token, pos_table, cotangent):
    positions = jnp.arange(SEQ, dtype=jnp.int32)
    inside = positions[None, :] < lengths[:, None]
    visible = inside & (masked == 0)
    vis_int = visible.astype(jnp.int32)
    ranks = jnp.cumsum(vis_int, axis=1) - vis_int
    select = (visible[:, None, :] & (ranks[:, None, :] == jnp.arange(VIS, dtype=jnp.int32)[None, :, None])).astype(jnp.float32)
    enc_valid = jnp.arange(VIS, dtype=jnp.int32)[None, :] < lax.optimization_barrier(jnp.sum(vis_int, axis=1))[:, None]
    pixel_ids = jnp.arange(PIXELS, dtype=jnp.int32)
    rep_index = pixel_ids // PIX_DEV % N_REP
    target = (route_dev * N_REP + rep_index) * PIX_DEV + route_slot
    source = jnp.zeros((PIXELS,), jnp.int32).at[target].set(pixel_ids)
    dec_select = select[source]
    dec_hidden = 1.0 - visible[source].astype(jnp.float32)
    dec_inside = inside[source]
    dec_keep = dec_inside.astype(jnp.float32)

    def forward(tokens_f, gains, shifts, qkv_w, out_w, up_w, up_b, down_w, down_b, mask_vec, pos_rows):
        enc_in = product(select, tokens_f, 'pvt,ptd->pvd')
        enc_out = layer(enc_in, enc_valid, gains[0], shifts[0], qkv_w[0], out_w[0], up_w[0], up_b[0], down_w[0], down_b[0])
        sent = low(low_back(enc_out))[source]
        dec_in = product(dec_select, sent, 'pvt,pvd->ptd') + dec_hidden[..., None] * mask_vec + pos_rows[None]
        dec_out = layer(dec_in, dec_inside, gains[1], shifts[1], qkv_w[1], out_w[1], up_w[1], up_b[1], down_w[1], down_b[1])
        return dec_out * dec_keep[..., None]
    result, pullback = jax.vjp(forward, tokens.astype(jnp.float32), norm_gain, norm_bias, w_qkv.astype(jnp.float32), w_out.astype(jnp.float32), w_up.astype(jnp.float32), b_up, w_down.astype(jnp.float32), b_down, mask_token, pos_table)
    grads = pullback(cotangent.astype(jnp.float32))
    return (result, grads[0], grads[1], grads[2], grads[3], grads[4], grads[5], grads[6], grads[7], grads[8], grads[9], grads[10])
```

```python
import functools

import jax
import jax.numpy as jnp
from jax import lax
from jax.experimental import pallas as pl
from jax.experimental.pallas import tpu as pltpu
from jax.sharding import PartitionSpec as P

HEADS = 8
HEAD_DIM = 16
VIS = 8
GROUP = 16
PAD = 32
CHUNK = 48
EPS = 1e-05
NEG = -1e30
BF = jnp.bfloat16
F32 = jnp.float32
VMEM_LIMIT = 56 * 1024 * 1024


def nn(left, right):
    return jnp.dot(left, right, preferred_element_type=F32)


def nt(left, right):
    return lax.dot_general(left, right, (((1,), (1,)), ((), ())), preferred_element_type=F32)


def tn(left, right):
    return lax.dot_general(left, right, (((0,), (0,)), ((), ())), preferred_element_type=F32)


def iota(shape, dim):
    return lax.broadcasted_iota(jnp.int32, shape, dim)


def fold_rows(values):
    rows = values.shape[0]
    return jnp.sum(values.reshape(rows // 8, 8, values.shape[1]), axis=0)


def erf_parts(hidden):
    size = jnp.abs(hidden)
    base = 1.0 + size * (0.3275911 * 0.7071067811865476)
    t = 1.0 / base
    bell = jnp.exp(hidden * hidden * -0.5)
    poly = t * (
        0.5 * 0.254829592
        + t * (0.5 * -0.284496736 + t * (0.5 * 1.421413741 + t * (0.5 * -1.453152027 + t * (0.5 * 1.061405429))))
    )
    tail = poly * bell
    return jnp.where(hidden >= 0, 1.0 - tail, tail), bell


def expand(rows, masks):
    count = rows.shape[0]
    return jnp.concatenate([rows * masks[h, :count, :] for h in range(HEADS)], axis=0)


def fold_heads(rows, step, count):
    lane = iota((count, 128), 1)
    picked = rows[0:count]
    for head in range(1, HEADS):
        picked = jnp.where(lane >= head * HEAD_DIM, rows[head * step : head * step + count], picked)
    return picked


def ln_fwd(values, gain, bias, hat, inv, low, where):
    centred = values - jnp.mean(values, axis=-1, keepdims=True)
    scale = lax.rsqrt(jnp.mean(centred * centred, axis=-1, keepdims=True) + EPS)
    unit = centred * scale
    hat[where] = unit
    inv[where] = jnp.broadcast_to(scale, unit.shape)
    low[where] = (unit * gain + bias).astype(BF)


def ln_bwd(grad, gain, hat, inv, where):
    unit = hat[where]
    inner = grad * gain
    lean = jnp.mean(inner, axis=-1, keepdims=True)
    tilt = jnp.mean(inner * unit, axis=-1, keepdims=True)
    return inv[where] * (inner - lean - unit * tilt), fold_rows(grad * unit), fold_rows(grad)


def prep_kernel(
    cap, extra, count, me_ref, dest_ref, tokens_ref, len_ref, masked_ref, dest_row_ref,
    payload_ref, pos_ref, place_ref, take_ref, back_ref, tally,
):
    pixels, slots = masked_ref.shape
    groups = pixels // GROUP
    block = cap + extra
    wide = GROUP * slots
    len_col = jnp.broadcast_to(len_ref[...].astype(F32), (pixels, pixels)).T
    dest_col = jnp.broadcast_to(dest_row_ref[...].astype(F32), (pixels, pixels)).T
    seen = (masked_ref[...] == 0) & (iota((pixels, slots), 1).astype(F32) < len_col[:, :slots])
    seen_low = jnp.where(seen, 1.0, 0.0).astype(BF)
    earlier = jnp.where(iota((slots, slots), 0) < iota((slots, slots), 1), 1.0, 0.0).astype(BF)
    member = iota((pixels, slots), 0) % GROUP
    code = jnp.where(seen, nn(seen_low, earlier) + (member * VIS).astype(F32), -1.0)
    spread = jnp.where(iota((slots, wide), 0) == iota((slots, wide), 1) % slots, 1.0, 0.0).astype(BF)
    code_wide = nn(code.astype(BF), spread)
    own = iota((pixels, wide), 0) % GROUP == iota((pixels, wide), 1) // slots
    code_row = jnp.sum(jnp.where(own, code_wide, 0.0).reshape(groups, GROUP, wide), axis=1)
    lanes = GROUP * VIS
    own_low = iota((pixels, lanes), 0) % GROUP == iota((pixels, lanes), 1) // VIS
    len_rows = jnp.sum(jnp.where(own_low, len_col, 0.0).reshape(groups, GROUP, lanes), axis=1)
    dest_rows = jnp.sum(jnp.where(own_low, dest_col, 0.0).reshape(groups, GROUP, lanes), axis=1)
    me = me_ref[0]
    for dev in range(count):
        tally[dev] = 0
    order = iota((lanes, wide), 0).astype(F32)
    steps = (iota((GROUP, wide), 1) % slots + 1).astype(F32).astype(BF)
    found = []
    for group in range(groups):
        select = jnp.where(order == code_row[group : group + 1, :], 1.0, 0.0).astype(BF)
        rows = nn(select, tokens_ref[group * wide : (group + 1) * wide, :]).reshape(GROUP, VIS, 128)
        found.append(nt(steps, select)[0:1, :])
        for member_id in range(GROUP):
            series = group * GROUP + member_id
            dest = dest_ref[series]
            rank = tally[dest]
            tally[dest] = rank + 1
            sender = lax.rem(2 * me - dest + 2 * count, count)
            place_ref[series] = dest * cap + rank
            take_ref[series] = sender * block + rank
            back_ref[series] = sender * cap + rank
            payload_ref[dest * block + rank] = rows[member_id].astype(BF)
    pos_rows = jnp.concatenate(found, axis=0)
    pos_ref[...] = pos_rows

    def label(dev, carry):
        mine = dest_rows == dev.astype(F32)
        payload_ref[dev * block + cap] = jnp.where(mine, pos_rows, 0.0).astype(BF)
        payload_ref[dev * block + cap + 1] = jnp.where(mine, len_rows, 0.0).astype(BF)
        return carry

    lax.fori_loop(0, count, label, 0)


def prep(tokens, lengths, masked, route_dev, count, cap, extra, me):
    pixels, slots, width = tokens.shape
    smem = pl.BlockSpec(memory_space=pltpu.SMEM)
    vmem = pl.BlockSpec(memory_space=pltpu.VMEM)
    index = jax.ShapeDtypeStruct((pixels,), jnp.int32)
    return pl.pallas_call(
        functools.partial(prep_kernel, cap, extra, count),
        out_shape=(
            jax.ShapeDtypeStruct((count * (cap + extra), VIS, width), BF),
            jax.ShapeDtypeStruct((pixels // GROUP, GROUP * VIS), F32),
            index,
            index,
            index,
        ),
        in_specs=[smem, smem, vmem, vmem, vmem, vmem],
        out_specs=(vmem, vmem, smem, smem, smem),
        scratch_shapes=[pltpu.SMEM((count,), jnp.int32)],
        compiler_params=pltpu.CompilerParams(vmem_limit_bytes=VMEM_LIMIT),
        name="prep",
    )(
        me, route_dev, tokens.reshape(pixels * slots, width), lengths.reshape(1, pixels), masked,
        route_dev.reshape(1, pixels),
    )


class Box:
    pass


def gelu_stage(hidden, b_up, act, slope, base, rows):
    for start in range(0, rows, 16):
        value = hidden[start : start + 16] + b_up
        cdf, bell = erf_parts(value)
        where = pl.ds(base + start, 16)
        act[where] = (value * cdf).astype(BF)
        slope[where] = cdf + value * bell * 0.3989422804014327


def slope_stage(grad_act, slope, out, base, rows):
    total = None
    for start in range(0, rows, 16):
        part = (grad_act[start : start + 16] * slope[pl.ds(base + start, 16)]).astype(BF)
        out[pl.ds(start, 16)] = part
        summed = fold_rows(part.astype(F32))
        total = summed if total is None else total + summed
    return total


def softmax_rows(scores, keep):
    scores = jnp.where(keep, scores, NEG)
    powers = jnp.exp(scores - jnp.max(scores, axis=0, keepdims=True))
    return powers / jnp.sum(powers, axis=0, keepdims=True)


def soft_bwd(probs, grad):
    return (probs * (grad - jnp.sum(grad * probs, axis=0, keepdims=True))).astype(BF)


def encoder_fwd(b, base, rows):
    w = b.w
    for start in range(0, rows, 32):
        where = pl.ds(base + start, 32)
        ln_fwd(b.e_x[where], w.gain[0:1], w.bias[0:1], b.e_hat1, b.e_inv1, b.e_n1, where)
    whole = pl.ds(base, rows)
    qkv = nn(b.e_n1[whole], w.qkv[0])
    for start in range(0, rows, 32):
        where = pl.ds(base + start, 32)
        part = qkv[start : start + 32]
        b.e_qkv[where, 0:128] = (part[:, 0:128] * 0.25).astype(BF)
        b.e_qkv[where, 128:384] = part[:, 128:384].astype(BF)
    same = iota((16, 128), 0) // VIS == (iota((16, 128), 1) % 16) // VIS
    for start in range(0, rows, 16):
        where = pl.ds(base + start, 16)
        query = expand(b.e_qkv[where, 0:128], b.masks)
        keep = same & (b.pos_col[where] > 0)
        probs = softmax_rows(nt(b.e_qkv[where, 128:256], query), keep)
        b.e_probs[where] = probs
        mixed = tn(probs.astype(BF), b.e_qkv[where, 256:384])
        b.e_att[where] = fold_heads(mixed, 16, 16).astype(BF)
    proj = nn(b.e_att[whole], w.out[0])
    for start in range(0, rows, 32):
        where = pl.ds(base + start, 32)
        middle = b.e_x[where] + proj[start : start + 32]
        b.e_x[where] = middle
        ln_fwd(middle, w.gain[1:2], w.bias[1:2], b.e_hat2, b.e_inv2, b.e_n2, where)
    hidden = nn(b.e_n2[whole], w.up[0])
    gelu_stage(hidden, w.b_up[0:1], b.e_act, b.e_slope, base, rows)
    down = nn(b.e_act[whole], w.down[0])
    for start in range(0, rows, 32):
        where = pl.ds(base + start, 32)
        b.sent[where] = (b.e_x[where] + down[start : start + 32] + w.b_down[0:1]).astype(BF)


def encoder_bwd(b, base, rows):
    w = b.w
    whole = pl.ds(base, rows)
    grad_low = b.g_sent[whole]
    b.d_down[0] += tn(grad_low, b.e_act[whole])
    b.d_b_down[0] += fold_rows(grad_low.astype(F32))
    grad_act = nn(grad_low, b.down_t[0])
    b.d_b_up[0] += slope_stage(grad_act, b.e_slope, b.e_gh, base, rows)
    b.d_up[0] += tn(b.e_n2[whole], b.e_gh[...])
    grad_n2 = nn(b.e_gh[...], b.up_t[0])
    for start in range(0, rows, 32):
        where = pl.ds(base + start, 32)
        grad, gain_part, bias_part = ln_bwd(
            grad_n2[start : start + 32], w.gain[1:2], b.e_hat2, b.e_inv2, where
        )
        b.d_gain[1] += gain_part
        b.d_bias[1] += bias_part
        grad = grad + b.g_sent[where].astype(F32)
        b.e_gm[pl.ds(start, 32)] = grad
        b.e_gml[pl.ds(start, 32)] = grad.astype(BF)
    b.d_out[0] += tn(b.e_att[whole], b.e_gml[...])
    b.e_ga[...] = nn(b.e_gml[...], b.out_t[0]).astype(BF)
    for start in range(0, rows, 16):
        where = pl.ds(base + start, 16)
        query = expand(b.e_qkv[where, 0:128], b.masks)
        grad_out = expand(b.e_ga[start : start + 16], b.masks)
        probs = b.e_probs[where]
        grad_s = soft_bwd(probs, nt(b.e_qkv[where, 256:384], grad_out))
        here = pl.ds(start, 16)
        b.e_gqkv[here, 256:384] = nn(probs.astype(BF), grad_out).astype(BF)
        b.e_gqkv[here, 128:256] = nn(grad_s, query).astype(BF)
        grad_q = fold_heads(tn(grad_s, b.e_qkv[where, 128:256]), 16, 16)
        b.e_gqkv[here, 0:128] = (grad_q * 0.25).astype(BF)
    b.d_qkv[0] += tn(b.e_n1[whole], b.e_gqkv[...])
    grad_n1 = nn(b.e_gqkv[...], b.qkv_t[0])
    for start in range(0, rows, 32):
        where = pl.ds(base + start, 32)
        grad, gain_part, bias_part = ln_bwd(
            grad_n1[start : start + 32], w.gain[0:1], b.e_hat1, b.e_inv1, where
        )
        b.d_gain[0] += gain_part
        b.d_bias[0] += bias_part
        b.g_enc[where] = grad + b.e_gm[pl.ds(start, 32)]


def decoder_group(b, group):
    w = b.w
    slots = b.slots
    rows = GROUP * slots
    first = group * GROUP
    lane = iota((1, 128), 1)
    pos_row = b.pos_row[group]
    target = jnp.where(pos_row > 0, (lane // VIS * slots).astype(F32) + pos_row - 1.0, -1.0)
    for start in range(0, rows, CHUNK):
        spot = (iota((CHUNK, 128), 0) + start).astype(F32)
        b.hot[pl.ds(start, CHUNK)] = jnp.where(spot == target, 1.0, 0.0).astype(BF)
    sent_rows = pl.ds(pl.multiple_of(group * 128, 128), 128)
    placed = nn(b.hot[...], b.sent[sent_rows])
    shown = nn(b.hot[...], jnp.ones((128, 128), BF))
    step = iota((slots, 128), 0).astype(F32)

    def span(member):
        return pl.ds(member * slots, slots)

    def inside(member):
        lens = b.len_col[pl.ds(pl.multiple_of(group * 128, 128) + member * VIS, VIS)]
        return step < jnp.concatenate([lens] * (slots // VIS), axis=0)

    for member in range(GROUP):
        at = slice(member * slots, (member + 1) * slots)
        hidden_part = 1.0 - shown[at]
        b.unseen[span(member)] = hidden_part
        b.d_x[span(member)] = placed[at] + hidden_part * w.mask[...] + w.pos[...]
        cot = b.cot[b.slot[first + member]].astype(F32)
        b.d_g[span(member)] = jnp.where(inside(member), cot, 0.0)
    for start in range(0, rows, CHUNK):
        where = pl.ds(start, CHUNK)
        ln_fwd(b.d_x[where], w.gain[2:3], w.bias[2:3], b.d_hat1, b.d_inv1, b.d_n1, where)
    qkv = nn(b.d_n1[...], w.qkv[1])
    zeros = jnp.zeros((PAD - slots, 128), F32)

    def padded(values):
        return jnp.concatenate([values, zeros], axis=0).astype(BF)

    wide_zero = jnp.zeros((PAD - slots, HEADS * PAD), F32)

    def padded_wide(values):
        return jnp.concatenate([values, wide_zero], axis=0).astype(BF)

    for member in range(GROUP):
        at = slice(member * slots, (member + 1) * slots)
        query_low = padded(qkv[at, 0:128] * 0.25)
        key_low = padded(qkv[at, 128:256])
        value_low = padded(qkv[at, 256:384])
        b.d_q[member] = query_low
        b.d_k[member] = key_low
        b.d_v[member] = value_low
        scores = nt(key_low, expand(query_low, b.masks))[:slots]
        ok = inside(member)
        probs = softmax_rows(scores, jnp.concatenate([ok, ok], axis=1))
        b.d_probs[member] = probs
        mixed = tn(padded_wide(probs), value_low)
        b.d_att32[span(member)] = fold_heads(mixed, PAD, slots)
    for start in range(0, rows, CHUNK):
        where = pl.ds(start, CHUNK)
        b.d_att[where] = b.d_att32[where].astype(BF)
    proj = nn(b.d_att[...], w.out[1])
    for start in range(0, rows, CHUNK):
        where = pl.ds(start, CHUNK)
        middle = b.d_x[where] + proj[start : start + CHUNK]
        b.d_x[where] = middle
        ln_fwd(middle, w.gain[3:4], w.bias[3:4], b.d_hat2, b.d_inv2, b.d_n2, where)
    hidden = nn(b.d_n2[...], w.up[1])
    gelu_stage(hidden, w.b_up[1:2], b.d_act, b.d_slope, 0, rows)
    down = nn(b.d_act[...], w.down[1])
    for member in range(GROUP):
        at = slice(member * slots, (member + 1) * slots)
        value = b.d_x[span(member)] + down[at] + w.b_down[1:2]
        b.dec[b.slot[first + member]] = jnp.where(inside(member), value, 0.0)
    for start in range(0, rows, CHUNK):
        where = pl.ds(start, CHUNK)
        b.d_gl[where] = b.d_g[where].astype(BF)
    b.d_down[1] += tn(b.d_gl[...], b.d_act[...])
    b.d_b_down[1] += fold_rows(b.d_g[...])
    grad_act = nn(b.d_gl[...], b.down_t[1])
    b.d_b_up[1] += slope_stage(grad_act, b.d_slope, b.d_gh, 0, rows)
    b.d_up[1] += tn(b.d_n2[...], b.d_gh[...])
    grad_n2 = nn(b.d_gh[...], b.up_t[1])
    for start in range(0, rows, CHUNK):
        where = pl.ds(start, CHUNK)
        grad, gain_part, bias_part = ln_bwd(
            grad_n2[start : start + CHUNK], w.gain[3:4], b.d_hat2, b.d_inv2, where
        )
        b.d_gain[3] += gain_part
        b.d_bias[3] += bias_part
        grad = grad + b.d_g[where]
        b.d_g[where] = grad
        b.d_gl[where] = grad.astype(BF)
    b.d_out[1] += tn(b.d_att[...], b.d_gl[...])
    grad_att = nn(b.d_gl[...], b.out_t[1])
    for member in range(GROUP):
        at = slice(member * slots, (member + 1) * slots)
        query = expand(b.d_q[member], b.masks)
        grad_out = expand(padded(grad_att[at]), b.masks)
        probs = b.d_probs[member]
        grad_s = soft_bwd(probs, nt(b.d_v[member], grad_out)[:slots])
        grad_s = jnp.concatenate([grad_s.astype(F32), wide_zero], axis=0).astype(BF)
        b.d_gqkv32[span(member), 256:384] = nn(padded_wide(probs), grad_out)[:slots]
        b.d_gqkv32[span(member), 128:256] = nn(grad_s, query)[:slots]
        b.d_gqkv32[span(member), 0:128] = fold_heads(tn(grad_s, b.d_k[member]), PAD, slots) * 0.25
    for start in range(0, rows, CHUNK):
        where = pl.ds(start, CHUNK)
        b.d_gqkv[where] = b.d_gqkv32[where].astype(BF)
    b.d_qkv[1] += tn(b.d_n1[...], b.d_gqkv[...])
    grad_n1 = nn(b.d_gqkv[...], b.qkv_t[1])
    pos_total = None
    for start in range(0, rows, CHUNK):
        where = pl.ds(start, CHUNK)
        grad, gain_part, bias_part = ln_bwd(
            grad_n1[start : start + CHUNK], w.gain[2:3], b.d_hat1, b.d_inv1, where
        )
        b.d_gain[2] += gain_part
        b.d_bias[2] += bias_part
        grad = grad + b.d_g[where]
        b.d_gl[where] = grad.astype(BF)
        part = jnp.sum(grad.reshape(CHUNK // slots, slots, 128), axis=0)
        pos_total = part if pos_total is None else pos_total + part
        b.d_mask[...] += fold_rows(grad * b.unseen[where])
    b.d_pos[...] += pos_total
    b.g_sent[sent_rows] = tn(b.hot[...], b.d_gl[...]).astype(BF)


IN_NAMES = (
    "take", "back_at", "slot", "recv", "cot", "w_qkv", "w_out", "w_up", "w_down", "b_up", "b_down", "gain",
    "bias", "mask", "pos",
)
OUT_NAMES = ("dec", "back", "grads")


def small_rows(slots):
    return 18 + 1 + slots


def main_kernel(names, cap, extra, count, *refs):
    b = Box()
    for name, ref in zip(names, refs, strict=True):
        setattr(b, name, ref)
    b.w = Box()
    for name in ("qkv", "out", "up", "down"):
        setattr(b.w, name, getattr(b, "w_" + name))
    for name in ("b_up", "b_down", "gain", "bias", "mask", "pos"):
        setattr(b.w, name, getattr(b, name))
    b.slots = b.cot.shape[1]
    pixels = b.cot.shape[0]
    groups = pixels // GROUP
    block = cap + extra
    for head in range(HEADS):
        lane = iota((PAD, 128), 1) // HEAD_DIM
        b.masks[head] = jnp.where(lane == head, 1.0, 0.0).astype(BF)
    for layer in range(2):
        b.qkv_t[layer] = b.w_qkv[layer].T
        b.out_t[layer] = b.w_out[layer].T
        b.up_t[layer] = b.w_up[layer].T
        b.down_t[layer] = b.w_down[layer].T
    for ref in (b.d_qkv, b.d_out, b.d_up, b.d_down, b.d_gain, b.d_bias, b.d_b_up, b.d_b_down, b.d_mask, b.d_pos):
        ref[...] = jnp.zeros(ref.shape, F32)

    def gather(dev, carry):
        pos, lens = carry
        return (
            pos + b.recv[dev * block + cap].astype(F32),
            lens + b.recv[dev * block + cap + 1].astype(F32),
        )

    empty = jnp.zeros((groups, 128), F32)
    pos, lens = lax.fori_loop(0, count, gather, (empty, empty))
    for group in range(groups):
        where = pl.ds(group * 128, 128)
        b.pos_row[group] = pos[group : group + 1]
        b.pos_col[where] = jnp.broadcast_to(pos[group : group + 1], (128, 128)).T
        b.len_col[where] = jnp.broadcast_to(lens[group : group + 1], (128, 128)).T

    enc_rows = 256
    per = enc_rows // VIS

    def enc_forward(step, carry):
        base = pl.multiple_of(step * enc_rows, enc_rows)
        for member in range(per):
            b.e_x[pl.ds(base + member * VIS, VIS)] = b.recv[b.take[step * per + member]].astype(F32)
        encoder_fwd(b, base, enc_rows)
        return carry

    lax.fori_loop(0, pixels // per, enc_forward, 0)

    def dec_both(group, carry):
        decoder_group(b, group)
        return carry

    lax.fori_loop(0, groups, dec_both, 0)

    def enc_backward(step, carry):
        base = pl.multiple_of(step * enc_rows, enc_rows)
        encoder_bwd(b, base, enc_rows)
        for member in range(per):
            rows = b.g_enc[pl.ds(base + member * VIS, VIS)]
            b.back[b.back_at[step * per + member]] = rows.astype(BF)
        return carry

    lax.fori_loop(0, pixels // per, enc_backward, 0)

    offset = 0
    for layer in range(2):
        for start in range(0, 384, 128):
            b.grads[offset : offset + 128] = b.d_qkv[layer, :, start : start + 128].astype(BF)
            offset += 128
        b.grads[offset : offset + 128] = b.d_out[layer].astype(BF)
        offset += 128
        for start in range(0, 512, 128):
            b.grads[offset : offset + 128] = b.d_up[layer, :, start : start + 128].astype(BF)
            offset += 128
        for start in range(0, 512, 128):
            b.grads[offset : offset + 128] = b.d_down[layer, :, start : start + 128].T.astype(BF)
            offset += 128

    def total(ref, index):
        return jnp.sum(ref[index], axis=0, keepdims=True)

    small = [total(b.d_gain, i) for i in range(4)] + [total(b.d_bias, i) for i in range(4)]
    for layer in range(2):
        row = total(b.d_b_up, layer)
        small += [row[:, start : start + 128] for start in range(0, 512, 128)]
    small += [total(b.d_b_down, layer) for layer in range(2)]
    small.append(jnp.sum(b.d_mask[...], axis=0, keepdims=True))
    small.append(b.d_pos[...])
    tail = jnp.concatenate(small, axis=0)
    fill = -tail.shape[0] % 16
    tail = jnp.concatenate([tail, jnp.zeros((fill, 128), F32)], axis=0)
    b.grads[offset : offset + tail.shape[0]] = tail.astype(BF)


def main_call(args, cap, extra, count, grad_rows):
    recv, cot = args[3], args[4]
    pixels, slots, width = cot.shape
    enc = pixels * VIS
    rows = GROUP * slots
    smem = pl.BlockSpec(memory_space=pltpu.SMEM)
    vmem = pl.BlockSpec(memory_space=pltpu.VMEM)
    enc_rows = 256
    scratch = {
        "masks": ((HEADS, PAD, 128), BF),
        "qkv_t": ((2, 384, 128), BF),
        "out_t": ((2, 128, 128), BF),
        "up_t": ((2, 512, 128), BF),
        "down_t": ((2, 128, 512), BF),
        "d_qkv": ((2, 128, 384), F32),
        "d_out": ((2, 128, 128), F32),
        "d_up": ((2, 128, 512), F32),
        "d_down": ((2, 128, 512), F32),
        "d_gain": ((4, 8, 128), F32),
        "d_bias": ((4, 8, 128), F32),
        "d_b_up": ((2, 8, 512), F32),
        "d_b_down": ((2, 8, 128), F32),
        "d_mask": ((8, 128), F32),
        "d_pos": ((slots, 128), F32),
        "pos_row": ((pixels // GROUP, 1, 128), F32),
        "pos_col": ((enc, 128), F32),
        "len_col": ((enc, 128), F32),
        "sent": ((enc, 128), BF),
        "g_sent": ((enc, 128), BF),
        "g_enc": ((enc, 128), F32),
        "e_x": ((enc, 128), F32),
        "e_hat1": ((enc, 128), F32),
        "e_inv1": ((enc, 128), F32),
        "e_n1": ((enc, 128), BF),
        "e_qkv": ((enc, 384), BF),
        "e_probs": ((enc, 128), F32),
        "e_att": ((enc, 128), BF),
        "e_hat2": ((enc, 128), F32),
        "e_inv2": ((enc, 128), F32),
        "e_n2": ((enc, 128), BF),
        "e_act": ((enc, 512), BF),
        "e_slope": ((enc, 512), F32),
        "e_gh": ((enc_rows, 512), BF),
        "e_gm": ((enc_rows, 128), F32),
        "e_gml": ((enc_rows, 128), BF),
        "e_ga": ((enc_rows, 128), BF),
        "e_gqkv": ((enc_rows, 384), BF),
        "hot": ((rows, 128), BF),
        "unseen": ((rows, 128), F32),
        "d_x": ((rows, 128), F32),
        "d_g": ((rows, 128), F32),
        "d_gl": ((rows, 128), BF),
        "d_hat1": ((rows, 128), F32),
        "d_inv1": ((rows, 128), F32),
        "d_n1": ((rows, 128), BF),
        "d_q": ((GROUP, PAD, 128), BF),
        "d_k": ((GROUP, PAD, 128), BF),
        "d_v": ((GROUP, PAD, 128), BF),
        "d_probs": ((GROUP, slots, HEADS * PAD), F32),
        "d_att32": ((rows, 128), F32),
        "d_att": ((rows, 128), BF),
        "d_hat2": ((rows, 128), F32),
        "d_inv2": ((rows, 128), F32),
        "d_n2": ((rows, 128), BF),
        "d_act": ((rows, 512), BF),
        "d_slope": ((rows, 512), F32),
        "d_gh": ((rows, 512), BF),
        "d_gqkv32": ((rows, 384), F32),
        "d_gqkv": ((rows, 384), BF),
    }
    names = IN_NAMES + OUT_NAMES + tuple(scratch)
    return pl.pallas_call(
        functools.partial(main_kernel, names, cap, extra, count),
        out_shape=(
            jax.ShapeDtypeStruct((pixels, slots, width), F32),
            jax.ShapeDtypeStruct((count * cap, VIS, width), BF),
            jax.ShapeDtypeStruct((grad_rows, 128), BF),
        ),
        in_specs=[smem] * 3 + [vmem] * (len(IN_NAMES) - 3),
        out_specs=(vmem, vmem, vmem),
        scratch_shapes=[pltpu.VMEM(shape, kind) for shape, kind in scratch.values()],
        compiler_params=pltpu.CompilerParams(vmem_limit_bytes=VMEM_LIMIT),
        name="layers",
    )(*args)


def pair_sum_kernel(core_ref, mine_ref, theirs_ref, out_ref):
    core = core_ref[0]
    out_ref[...] = (mine_ref[core].astype(F32) + theirs_ref[core].astype(F32)).astype(BF)


def chunk_sum_kernel(parts_ref, out_ref):
    total = parts_ref[0].astype(F32)
    for part in range(1, parts_ref.shape[0]):
        total = total + parts_ref[part].astype(F32)
    low = total.astype(BF)
    for part in range(parts_ref.shape[0]):
        out_ref[part] = low


def unpack_kernel(
    slots, core_ref, mine_ref, theirs_ref, gain_ref, bias_ref, qkv_ref, out_ref, up_ref, b_up_ref, down_ref,
    b_down_ref, mask_ref, pos_ref, full,
):
    core = core_ref[0]
    full[core] = mine_ref[...]
    full[1 - core] = theirs_ref[...]
    half = full.shape[1]

    def rows(start, size):
        side, at = start // half, start % half
        if at + size <= half:
            return full[side, at : at + size].astype(F32)
        cut = half - at
        return jnp.concatenate(
            [full[side, at:half].astype(F32), full[side + 1, 0 : size - cut].astype(F32)], axis=0
        )

    offset = 0
    for layer in range(2):
        for start in range(0, 384, 128):
            qkv_ref[layer, :, start : start + 128] = rows(offset, 128)
            offset += 128
        out_ref[layer] = rows(offset, 128)
        offset += 128
        for start in range(0, 512, 128):
            up_ref[layer, :, start : start + 128] = rows(offset, 128)
            offset += 128
        for start in range(0, 512, 128):
            down_ref[layer, start : start + 128, :] = rows(offset, 128)
            offset += 128
    count = small_rows(slots)
    small = rows(offset, count + (-count % 16))
    gain_ref[...] = small[0:4]
    bias_ref[...] = small[4:8]
    for layer in range(2):
        for part in range(4):
            at = 8 + 4 * layer + part
            b_up_ref[layer : layer + 1, part * 128 : (part + 1) * 128] = small[at : at + 1]
    b_down_ref[...] = small[16:18]
    mask_ref[...] = small[18:19]
    pos_ref[...] = small[19 : 19 + slots]


def restore_kernel(place_ref, pos_ref, rows_ref, out_ref, held):
    groups = pos_ref.shape[0]
    wide = out_ref.shape[0] // groups
    slots = wide // GROUP
    lane = iota((1, 128), 1)
    for group in range(groups):
        for member in range(GROUP):
            block = rows_ref[place_ref[group * GROUP + member]]
            held[pl.ds(member * VIS, VIS)] = block.astype(F32)
        pos_row = pos_ref[group : group + 1]
        target = jnp.where(pos_row > 0, (lane // VIS * slots).astype(F32) + pos_row - 1.0, -1.0)
        hot = jnp.where(iota((wide, 128), 0).astype(F32) == target, 1.0, 0.0).astype(BF)
        out_ref[group * wide : (group + 1) * wide, :] = nn(hot, held[...].astype(BF))


def shards(
    tokens, lengths, masked, route_dev, route_slot, norm_gain, norm_bias, w_qkv, w_out, w_up, b_up, w_down,
    b_down, mask_token, pos_table, cotangent,
):
    count = lax.axis_size("pix")
    reps = lax.axis_size("rep")
    devices = count * reps
    pixels, slots, width = tokens.shape
    cap = max(2, (2 * pixels + count - 1) // count)
    extra = 2
    smem = pl.BlockSpec(memory_space=pltpu.SMEM)
    vmem = pl.BlockSpec(memory_space=pltpu.VMEM)
    params = pltpu.CompilerParams(vmem_limit_bytes=VMEM_LIMIT)
    pix = lax.axis_index("pix")
    me = pix.reshape(1).astype(jnp.int32)
    flat = pix * reps + lax.axis_index("rep")
    core = (flat % 2).reshape(1).astype(jnp.int32)
    payload, pos_rows, place, take, back_at = prep(
        tokens, lengths, masked, route_dev, count, cap, extra, me
    )
    block = cap + extra
    recv = lax.all_to_all(
        payload.reshape(count, block, VIS, width), "pix", split_axis=0, concat_axis=0, tiled=True
    ).reshape(count * block, VIS, width)
    chunk = -(-(3072 + small_rows(slots)) // devices)
    chunk += -chunk % 8
    half = devices // 2
    dec, back, grads = main_call(
        (
            take, back_at, route_slot, recv, cotangent, w_qkv, w_out, w_up, w_down, b_up, b_down,
            norm_gain.reshape(4, width), norm_bias.reshape(4, width), mask_token.reshape(1, width), pos_table,
        ),
        cap,
        extra,
        count,
        devices * chunk,
    )
    returned = lax.all_to_all(
        back.reshape(count, cap, VIS, width), "pix", split_axis=0, concat_axis=0, tiled=True
    ).reshape(count * cap, VIS, width)
    axes = ("pix", "rep")
    swap = [(i, i ^ 1) for i in range(devices)]
    groups = [[2 * i + side for i in range(half)] for side in range(2)]

    def exchange(values):
        return lax.all_to_all(
            values, axes, split_axis=0, concat_axis=0, axis_index_groups=groups, tiled=True
        )

    grads = grads.reshape(2, half, chunk, 128)
    theirs = lax.ppermute(grads, axes, swap)
    paired = pl.pallas_call(
        pair_sum_kernel,
        out_shape=jax.ShapeDtypeStruct((half, chunk, 128), BF),
        in_specs=[smem, vmem, vmem],
        out_specs=vmem,
        compiler_params=params,
        name="pair_sum",
    )(core, grads, theirs)
    spread = pl.pallas_call(
        chunk_sum_kernel,
        out_shape=jax.ShapeDtypeStruct((half, chunk, 128), BF),
        in_specs=[vmem],
        out_specs=vmem,
        compiler_params=params,
        name="chunk_sum",
    )(exchange(paired))
    summed = exchange(spread).reshape(half * chunk, 128)
    other = lax.ppermute(summed, axes, swap)
    gain, bias, qkv, out, up, bup, down, bdown, mask, pos = pl.pallas_call(
        functools.partial(unpack_kernel, slots),
        out_shape=tuple(
            jax.ShapeDtypeStruct(shape, F32)
            for shape in (
                (4, width), (4, width), w_qkv.shape, w_out.shape, w_up.shape, b_up.shape, w_down.shape,
                b_down.shape, (1, width), pos_table.shape,
            )
        ),
        in_specs=[smem, vmem, vmem],
        out_specs=(vmem,) * 10,
        scratch_shapes=[pltpu.VMEM((2, half * chunk, 128), BF)],
        compiler_params=params,
        name="unpack",
    )(core, summed, other)
    grad_tokens = pl.pallas_call(
        restore_kernel,
        out_shape=jax.ShapeDtypeStruct((pixels * slots, width), F32),
        in_specs=[smem, vmem, vmem],
        out_specs=vmem,
        scratch_shapes=[pltpu.VMEM((GROUP * VIS, width), F32)],
        compiler_params=params,
        name="restore",
    )(place, pos_rows, returned)
    return (
        dec,
        grad_tokens.reshape(pixels, slots, width),
        gain.reshape(norm_gain.shape),
        bias.reshape(norm_bias.shape),
        qkv,
        out,
        up,
        bup,
        down,
        bdown,
        mask.reshape(width),
        pos,
    )


def solution(mesh):
    rows = P(("pix", "rep"))
    in_specs = (rows,) * 5 + (P(),) * 10 + (rows,)
    out_specs = (rows, rows) + (P(),) * 10
    return jax.shard_map(shards, mesh=mesh, in_specs=in_specs, out_specs=out_specs, check_vma=False)
```

```python
import functools

import jax
import jax.numpy as jnp
from jax import lax
from jax.experimental import pallas as pl
from jax.experimental.pallas import tpu as pltpu
from jax.sharding import PartitionSpec as P

HEADS = 8
HEAD_DIM = 16
FOLD = 4
BATCH = 16
PAIRS = 16
ENC_ROWS = 512
VIS = 8
GROUP = 16
PAD = 32
CHUNK = 48
EPS = 1e-05
NEG = -1e30
BF = jnp.bfloat16
F32 = jnp.float32
VMEM_LIMIT = 56 * 1024 * 1024


def nn(left, right):
    return jnp.dot(left, right, preferred_element_type=F32)


def nt(left, right):
    return lax.dot_general(left, right, (((1,), (1,)), ((), ())), preferred_element_type=F32)


def tn(left, right):
    return lax.dot_general(left, right, (((0,), (0,)), ((), ())), preferred_element_type=F32)


def iota(shape, dim):
    return lax.broadcasted_iota(jnp.int32, shape, dim)


def fold_rows(values):
    rows = values.shape[0]
    return jnp.sum(values.reshape(rows // 8, 8, values.shape[1]), axis=0)


def erf_parts(hidden):
    size = jnp.abs(hidden)
    base = 1.0 + size * (0.3275911 * 0.7071067811865476)
    t = 1.0 / base
    bell = jnp.exp(hidden * hidden * -0.5)
    poly = t * (
        0.5 * 0.254829592
        + t * (0.5 * -0.284496736 + t * (0.5 * 1.421413741 + t * (0.5 * -1.453152027 + t * (0.5 * 1.061405429))))
    )
    tail = poly * bell
    return jnp.where(hidden >= 0, 1.0 - tail, tail), bell


def expand(rows, masks):
    count = rows.shape[0]
    return jnp.concatenate([rows * masks[h, :count, :] for h in range(HEADS)], axis=0)


def fold_heads(rows, step, count):
    lane = iota((count, 128), 1)
    picked = rows[0:count]
    for head in range(1, HEADS):
        picked = jnp.where(lane >= head * HEAD_DIM, rows[head * step : head * step + count], picked)
    return picked


def fold_halves(rows, step, count):
    lane = iota((count, 128), 1) // HEAD_DIM % FOLD
    picked = rows[0:count]
    for head in range(1, FOLD):
        picked = jnp.where(lane == head, rows[head * step : head * step + count], picked)
    return picked


def expand_halves(rows, masks):
    return jnp.concatenate([rows * masks[h] for h in range(FOLD)], axis=0)


def stack_halves(values):
    low = iota(values.shape, 1) < 64
    return jnp.concatenate([jnp.where(low, values, 0.0), jnp.where(low, 0.0, values)], axis=0).astype(BF)


def join_halves(values):
    count = values.shape[0] // 2
    return jnp.where(iota((count, 128), 1) < 64, values[:count], values[count:])


def both_diagonals(values, rows):
    return values[:rows, :128], values[rows:, 128:]


def block_diagonal(first, second):
    low = jnp.concatenate([first, jnp.zeros_like(first)], axis=1)
    return jnp.concatenate([low, jnp.concatenate([jnp.zeros_like(second), second], axis=1)], axis=0)


def pair_nt(rows, columns):
    full = nt(jnp.concatenate(rows, axis=0), jnp.concatenate(columns, axis=0))
    return both_diagonals(full, rows[0].shape[0])


def pair_nn(rows, columns):
    full = nn(jnp.concatenate(rows, axis=0), jnp.concatenate(columns, axis=1))
    return both_diagonals(full, rows[0].shape[0])


def pair_tn(rows, columns):
    full = tn(jnp.concatenate(rows, axis=0), block_diagonal(*columns))
    return full[:, :128], full[:, 128:]


def softmax_halves(scores, keep):
    count = scores.shape[0] // 2
    scores = jnp.where(keep[None], scores.reshape(2, count, 128), NEG)
    powers = jnp.exp(scores - jnp.max(scores, axis=1, keepdims=True))
    probs = powers * (1.0 / jnp.sum(powers, axis=1, keepdims=True))
    return probs.reshape(2 * count, 128)


def soft_bwd_halves(probs, grad):
    count = probs.shape[0] // 2
    both = (grad * probs).reshape(2, count, 128)
    lean = jnp.sum(both, axis=1, keepdims=True)
    return (probs.reshape(2, count, 128) * (grad.reshape(2, count, 128) - lean)).reshape(2 * count, 128).astype(BF)


def ln_fwd(values, gain, bias, hat, inv, low, where):
    centred = values - jnp.mean(values, axis=-1, keepdims=True)
    scale = lax.rsqrt(jnp.mean(centred * centred, axis=-1, keepdims=True) + EPS)
    unit = centred * scale
    hat[where] = unit
    inv[where] = jnp.broadcast_to(scale, unit.shape)
    low[where] = (unit * gain + bias).astype(BF)


def ln_bwd(grad, gain, hat, inv, where):
    unit = hat[where]
    inner = grad * gain
    lean = jnp.mean(inner, axis=-1, keepdims=True)
    tilt = jnp.mean(inner * unit, axis=-1, keepdims=True)
    return inv[where] * (inner - lean - unit * tilt), fold_rows(grad * unit), fold_rows(grad)


def prep_kernel(
    cap, extra, count, me_ref, dest_ref, tokens_ref, len_ref, masked_ref, dest_row_ref,
    payload_ref, pos_ref, place_ref, take_ref, back_ref, tally,
):
    pixels, slots = masked_ref.shape
    groups = pixels // GROUP
    block = cap + extra
    wide = GROUP * slots
    len_col = jnp.broadcast_to(len_ref[...].astype(F32), (pixels, pixels)).T
    dest_col = jnp.broadcast_to(dest_row_ref[...].astype(F32), (pixels, pixels)).T
    seen = (masked_ref[...] == 0) & (iota((pixels, slots), 1).astype(F32) < len_col[:, :slots])
    seen_low = jnp.where(seen, 1.0, 0.0).astype(BF)
    earlier = jnp.where(iota((slots, slots), 0) < iota((slots, slots), 1), 1.0, 0.0).astype(BF)
    member = iota((pixels, slots), 0) % GROUP
    code = jnp.where(seen, nn(seen_low, earlier) + (member * VIS).astype(F32), -1.0)
    spread = jnp.where(iota((slots, wide), 0) == iota((slots, wide), 1) % slots, 1.0, 0.0).astype(BF)
    code_wide = nn(code.astype(BF), spread)
    own = iota((pixels, wide), 0) % GROUP == iota((pixels, wide), 1) // slots
    code_row = jnp.sum(jnp.where(own, code_wide, 0.0).reshape(groups, GROUP, wide), axis=1)
    lanes = GROUP * VIS
    own_low = iota((pixels, lanes), 0) % GROUP == iota((pixels, lanes), 1) // VIS
    len_rows = jnp.sum(jnp.where(own_low, len_col, 0.0).reshape(groups, GROUP, lanes), axis=1)
    dest_rows = jnp.sum(jnp.where(own_low, dest_col, 0.0).reshape(groups, GROUP, lanes), axis=1)
    me = me_ref[0]
    for dev in range(count):
        tally[dev] = 0
    order = iota((lanes, wide), 0).astype(F32)
    steps = (iota((GROUP, wide), 1) % slots + 1).astype(F32).astype(BF)
    found = []
    for group in range(groups):
        select = jnp.where(order == code_row[group : group + 1, :], 1.0, 0.0).astype(BF)
        rows = nn(select, tokens_ref[group * wide : (group + 1) * wide, :]).reshape(GROUP, VIS, 128)
        found.append(nt(steps, select)[0:1, :])
        for member_id in range(GROUP):
            series = group * GROUP + member_id
            dest = dest_ref[series]
            rank = tally[dest]
            tally[dest] = rank + 1
            sender = lax.rem(2 * me - dest + 2 * count, count)
            place_ref[series] = dest * cap + rank
            take_ref[series] = sender * block + rank
            back_ref[series] = sender * cap + rank
            payload_ref[dest * block + rank] = rows[member_id].astype(BF)
    pos_rows = jnp.concatenate(found, axis=0)
    pos_ref[...] = pos_rows

    def label(dev, carry):
        mine = dest_rows == dev.astype(F32)
        payload_ref[dev * block + cap] = jnp.where(mine, pos_rows, 0.0).astype(BF)
        payload_ref[dev * block + cap + 1] = jnp.where(mine, len_rows, 0.0).astype(BF)
        return carry

    lax.fori_loop(0, count, label, 0)


def prep(tokens, lengths, masked, route_dev, count, cap, extra, me):
    pixels, slots, width = tokens.shape
    smem = pl.BlockSpec(memory_space=pltpu.SMEM)
    vmem = pl.BlockSpec(memory_space=pltpu.VMEM)
    index = jax.ShapeDtypeStruct((pixels,), jnp.int32)
    return pl.pallas_call(
        functools.partial(prep_kernel, cap, extra, count),
        out_shape=(
            jax.ShapeDtypeStruct((count * (cap + extra), VIS, width), BF),
            jax.ShapeDtypeStruct((pixels // GROUP, GROUP * VIS), F32),
            index,
            index,
            index,
        ),
        in_specs=[smem, smem, vmem, vmem, vmem, vmem],
        out_specs=(vmem, vmem, smem, smem, smem),
        scratch_shapes=[pltpu.SMEM((count,), jnp.int32)],
        compiler_params=pltpu.CompilerParams(vmem_limit_bytes=VMEM_LIMIT),
        name="prep",
    )(
        me, route_dev, tokens.reshape(pixels * slots, width), lengths.reshape(1, pixels), masked,
        route_dev.reshape(1, pixels),
    )


class Box:
    pass


def gelu_stage(hidden, b_up, act, slope, base, rows):
    for start in range(0, rows, 16):
        value = hidden[start : start + 16] + b_up
        cdf, bell = erf_parts(value)
        where = pl.ds(base + start, 16)
        act[where] = (value * cdf).astype(BF)
        slope[where] = cdf + value * bell * 0.3989422804014327


def slope_stage(grad_act, slope, out, base, rows):
    total = None
    for start in range(0, rows, 16):
        part = (grad_act[start : start + 16] * slope[pl.ds(base + start, 16)]).astype(BF)
        out[pl.ds(start, 16)] = part
        summed = fold_rows(part.astype(F32))
        total = summed if total is None else total + summed
    return total


def softmax_rows(scores, keep):
    scores = jnp.where(keep, scores, NEG)
    powers = jnp.exp(scores - jnp.max(scores, axis=0, keepdims=True))
    return powers / jnp.sum(powers, axis=0, keepdims=True)


def soft_bwd(probs, grad):
    return (probs * (grad - jnp.sum(grad * probs, axis=0, keepdims=True))).astype(BF)


class Encoder:
    def __init__(self, b, base, rows):
        self.b, self.base, self.rows = b, base, rows
        self.whole = slice(base, base + rows)

    def chunks(self):
        return [slice(start, start + 32) for start in range(self.base, self.base + self.rows, 32)]

    def part(self, values, where):
        return values[where.start - self.base : where.stop - self.base]

    def attend(self):
        b, w, whole = self.b, self.b.w, self.whole
        v = Box()
        same = iota((16, 128), 0) // VIS == (iota((16, 128), 1) % 16) // VIS

        def load(series):
            b.e_x[series * VIS : (series + 1) * VIS] = b.recv[b.take[series]].astype(F32)

        steps = [functools.partial(load, series) for series in range(self.base // VIS, (self.base + self.rows) // VIS)]

        def norm(where):
            ln_fwd(b.e_x[where], w.gain[0:1], w.bias[0:1], b.e_hat1, b.e_inv1, b.e_n1, where)

        steps += [functools.partial(norm, where) for where in self.chunks()]

        def project():
            v.qkv = nn(b.e_n1[whole], w.qkv[0])
            v.score, v.prob, v.mixed = {}, {}, {}

        steps.append(project)

        def split(where):
            part = self.part(v.qkv, where)
            b.e_qkv[where, 0:128] = (part[:, 0:128] * 0.25).astype(BF)
            b.e_qkv[where, 128:384] = part[:, 128:384].astype(BF)

        steps += [functools.partial(split, where) for where in self.chunks()]

        def score(at):
            pair = (at, at + 16)
            queries = [expand(b.e_qkv[one : one + 16, 0:128], b.masks) for one in pair]
            keys = [b.e_qkv[one : one + 16, 128:256] for one in pair]
            v.score[at], v.score[at + 16] = pair_nt(keys, queries)

        def soft(at):
            v.prob[at] = softmax_rows(v.score[at], same & (b.pos_col[at : at + 16] > 0))
            b.e_probs[at : at + 16] = v.prob[at]

        def mix(at):
            pair = (at, at + 16)
            values = [b.e_qkv[one : one + 16, 256:384] for one in pair]
            v.mixed[at], v.mixed[at + 16] = pair_tn([v.prob[one].astype(BF) for one in pair], values)

        def gather(at):
            b.e_att[at : at + 16] = fold_heads(v.mixed[at], 16, 16).astype(BF)

        for first in range(self.base, self.base + self.rows, 16 * PAIRS):
            for stage, stride in ((score, 32), (soft, 16), (mix, 32), (gather, 16)):
                steps += [functools.partial(stage, at) for at in range(first, first + 16 * PAIRS, stride)]

        def out():
            v.proj = nn(b.e_att[whole], w.out[0])

        steps.append(out)

        def second(where):
            middle = b.e_x[where] + self.part(v.proj, where)
            b.e_x[where] = middle
            ln_fwd(middle, w.gain[1:2], w.bias[1:2], b.e_hat2, b.e_inv2, b.e_n2, where)

        steps += [functools.partial(second, where) for where in self.chunks()]
        return steps

    def bend(self):
        b, w, whole = self.b, self.b.w, self.whole
        v = Box()

        def up():
            v.hidden = nn(b.e_n2[whole], w.up[0])

        def curve(start):
            value = v.hidden[start : start + 16] + w.b_up[0:1]
            cdf, bell = erf_parts(value)
            where = slice(self.base + start, self.base + start + 16)
            b.e_act[where] = (value * cdf).astype(BF)
            b.e_slope[where] = cdf + value * bell * 0.3989422804014327

        def down():
            v.down = nn(b.e_act[whole], w.down[0])

        def finish(where):
            b.sent[where] = (b.e_x[where] + self.part(v.down, where) + w.b_down[0:1]).astype(BF)

        return (
            [up]
            + [functools.partial(curve, start) for start in range(0, self.rows, 16)]
            + [down]
            + [functools.partial(finish, where) for where in self.chunks()]
        )

    def feed(self):
        b, whole = self.b, self.whole
        v = Box()

        def back():
            grad_low = b.g_sent[whole]
            b.d_down[0] += tn(grad_low, b.e_act[whole])
            b.d_b_down[0] += fold_rows(grad_low.astype(F32))
            v.grad_act = nn(grad_low, b.down_t[0])
            v.total = None

        def unbend(start):
            where = slice(self.base + start, self.base + start + 16)
            part = (v.grad_act[start : start + 16] * b.e_slope[where]).astype(BF)
            b.e_gh[where] = part
            summed = fold_rows(part.astype(F32))
            v.total = summed if v.total is None else v.total + summed

        def end():
            b.d_b_up[0] += v.total
            b.d_up[0] += tn(b.e_n2[whole], b.e_gh[whole])
            b.e_gn2[whole] = nn(b.e_gh[whole], b.up_t[0])

        return [back] + [functools.partial(unbend, start) for start in range(0, self.rows, 16)] + [end]

    def retreat(self):
        b, w, whole = self.b, self.b.w, self.whole
        v = Box()

        def norm(where):
            grad, gain_part, bias_part = ln_bwd(b.e_gn2[where], w.gain[1:2], b.e_hat2, b.e_inv2, where)
            b.d_gain[1] += gain_part
            b.d_bias[1] += bias_part
            grad = grad + b.g_sent[where].astype(F32)
            b.e_gm[where] = grad
            b.e_gml[where] = grad.astype(BF)

        steps = [functools.partial(norm, where) for where in self.chunks()]

        def out():
            b.d_out[0] += tn(b.e_att[whole], b.e_gml[whole])
            v.grad_att = nn(b.e_gml[whole], b.out_t[0])
            v.grad, v.grad_p, v.grad_s, v.grad_v, v.grad_k, v.grad_q = ({} for _ in range(6))

        steps.append(out)

        def spread(at):
            pair = (at, at + 16)
            for one in pair:
                low = v.grad_att[one - self.base : one - self.base + 16].astype(BF)
                v.grad[one] = expand(low, b.masks)
            values = [b.e_qkv[one : one + 16, 256:384] for one in pair]
            v.grad_p[at], v.grad_p[at + 16] = pair_nt(values, [v.grad[one] for one in pair])

        def values(at):
            pair = (at, at + 16)
            probs = [b.e_probs[one : one + 16].astype(BF) for one in pair]
            v.grad_v[at], v.grad_v[at + 16] = pair_nn(probs, [v.grad[one] for one in pair])

        def soft(at):
            v.grad_s[at] = soft_bwd(b.e_probs[at : at + 16], v.grad_p[at])

        def keys(at):
            pair = (at, at + 16)
            columns = [expand(b.e_qkv[one : one + 16, 0:128], b.masks) for one in pair]
            v.grad_k[at], v.grad_k[at + 16] = pair_nn([v.grad_s[one] for one in pair], columns)

        def queries(at):
            pair = (at, at + 16)
            keys = [b.e_qkv[one : one + 16, 128:256] for one in pair]
            v.grad_q[at], v.grad_q[at + 16] = pair_tn([v.grad_s[one] for one in pair], keys)

        def gather(at):
            b.e_gqkv[at : at + 16, 256:384] = v.grad_v[at].astype(BF)
            b.e_gqkv[at : at + 16, 128:256] = v.grad_k[at].astype(BF)
            b.e_gqkv[at : at + 16, 0:128] = (fold_heads(v.grad_q[at], 16, 16) * 0.25).astype(BF)

        for first in range(self.base, self.base + self.rows, 16 * PAIRS):
            for stage, stride in ((spread, 32), (values, 32), (soft, 16), (keys, 32), (queries, 32), (gather, 16)):
                steps += [functools.partial(stage, at) for at in range(first, first + 16 * PAIRS, stride)]

        def project():
            b.d_qkv[0] += tn(b.e_n1[whole], b.e_gqkv[whole])
            v.grad_n1 = nn(b.e_gqkv[whole], b.qkv_t[0])

        steps.append(project)

        def first_norm(where):
            grad, gain_part, bias_part = ln_bwd(
                self.part(v.grad_n1, where), w.gain[0:1], b.e_hat1, b.e_inv1, where
            )
            b.d_gain[0] += gain_part
            b.d_bias[0] += bias_part
            grad = grad + b.e_gm[where]
            for series in range(where.start // VIS, where.stop // VIS):
                at = series * VIS - where.start
                b.back[b.back_at[series]] = grad[at : at + VIS].astype(BF)

        steps += [functools.partial(first_norm, where) for where in self.chunks()]
        return steps


def weave(*streams):
    lists = [list(stream) for stream in streams]
    order = []
    for which, steps in enumerate(lists):
        order += [((index + 0.5) / len(steps), which, step) for index, step in enumerate(steps)]
    for _, _, step in sorted(order, key=lambda entry: entry[:2]):
        step()


class Decoder:
    def __init__(self, b, d, group):
        self.b, self.d, self.group = b, d, group
        self.slots = b.slots
        self.rows = GROUP * b.slots
        self.sent_rows = pl.ds(pl.multiple_of(group * 128, 128), 128)
        self.zeros = jnp.zeros((PAD - b.slots, 128), F32)
        self.step = iota((b.slots, 128), 0).astype(F32)

    def span(self, member):
        return pl.ds(member * self.slots, self.slots)

    def cut(self, member):
        return slice(member * self.slots, (member + 1) * self.slots)

    def inside(self, member):
        lens = self.b.len_col[pl.ds(pl.multiple_of(self.group * 128, 128) + member * VIS, VIS)]
        return self.step < jnp.concatenate([lens] * (self.slots // VIS), axis=0)

    def padded(self, values):
        return jnp.concatenate([values, self.zeros], axis=0).astype(BF)

    def chunks(self):
        return range(0, self.rows, CHUNK)

    def attend(self):
        b, d, w, slots = self.b, self.d, self.b.w, self.slots
        v = Box()
        steps = []

        def begin():
            pos_row = b.pos_row[self.group]
            lane = iota((1, 128), 1)
            target = jnp.where(pos_row > 0, (lane // VIS * slots).astype(F32) + pos_row - 1.0, -1.0)
            for start in self.chunks():
                spot = (iota((CHUNK, 128), 0) + start).astype(F32)
                d.hot[pl.ds(start, CHUNK)] = jnp.where(spot == target, 1.0, 0.0).astype(BF)
            v.placed = nn(d.hot[...], b.sent[self.sent_rows])
            v.shown = nn(d.hot[...], jnp.ones((128, 128), BF))

        steps.append(begin)

        def assemble(member):
            at = self.cut(member)
            hidden_part = 1.0 - v.shown[at]
            d.unseen[self.span(member)] = hidden_part
            d.x[self.span(member)] = v.placed[at] + hidden_part * w.mask[...] + w.pos[...]
            cot = b.cot[b.slot[self.group * GROUP + member]].astype(F32)
            d.g[self.span(member)] = jnp.where(self.inside(member), cot, 0.0)

        steps += [functools.partial(assemble, member) for member in range(GROUP)]

        def norm(start):
            where = pl.ds(start, CHUNK)
            ln_fwd(d.x[where], w.gain[2:3], w.bias[2:3], d.hat1, d.inv1, d.n1, where)

        steps += [functools.partial(norm, start) for start in self.chunks()]

        def project():
            v.qkv = nn(d.n1[...], w.qkv[1])
            v.score, v.prob, v.mixed = {}, {}, {}

        steps.append(project)

        def split(member):
            at = self.cut(member)
            d.q[member] = self.padded(v.qkv[at, 0:128] * 0.25)
            d.k[member] = stack_halves(v.qkv[at, 128:256])
            d.v[member] = stack_halves(v.qkv[at, 256:384])

        def score(member):
            pair = (member, member + 1)
            queries = [expand_halves(d.q[one], b.masks_half) for one in pair]
            v.score[member], v.score[member + 1] = pair_nt([d.k[one] for one in pair], queries)

        def soft(member):
            v.prob[member] = softmax_halves(v.score[member], self.inside(member))
            d.probs[member] = v.prob[member]

        def mix(member):
            pair = (member, member + 1)
            mixed = pair_tn([v.prob[one].astype(BF) for one in pair], [d.v[one] for one in pair])
            v.mixed[member], v.mixed[member + 1] = mixed

        def gather(member):
            d.att32[self.span(member)] = fold_halves(v.mixed[member], PAD, slots)

        for first in range(0, GROUP, BATCH):
            for stage, stride in ((split, 1), (score, 2), (soft, 1), (mix, 2), (gather, 1)):
                steps += [functools.partial(stage, member) for member in range(first, first + BATCH, stride)]

        def low(start):
            where = pl.ds(start, CHUNK)
            d.att[where] = d.att32[where].astype(BF)

        steps += [functools.partial(low, start) for start in self.chunks()]

        def out():
            v.proj = nn(d.att[...], w.out[1])

        steps.append(out)

        def second(start):
            where = pl.ds(start, CHUNK)
            middle = d.x[where] + v.proj[start : start + CHUNK]
            d.x[where] = middle
            ln_fwd(middle, w.gain[3:4], w.bias[3:4], d.hat2, d.inv2, d.n2, where)

        steps += [functools.partial(second, start) for start in self.chunks()]
        return steps

    def bend(self):
        b, d, w = self.b, self.d, self.b.w
        v = Box()
        steps = []

        def up():
            v.hidden = nn(d.n2[...], w.up[1])

        steps.append(up)

        def curve(start):
            value = v.hidden[start : start + 16] + w.b_up[1:2]
            cdf, bell = erf_parts(value)
            where = pl.ds(start, 16)
            d.act[where] = (value * cdf).astype(BF)
            d.slope[where] = cdf + value * bell * 0.3989422804014327

        steps += [functools.partial(curve, start) for start in range(0, self.rows, 16)]
        return steps

    def feed(self):
        b, d, w = self.b, self.d, self.b.w
        v = Box()
        steps = []

        def down():
            v.down = nn(d.act[...], w.down[1])

        steps.append(down)

        def finish(member):
            value = d.x[self.span(member)] + v.down[self.cut(member)] + w.b_down[1:2]
            b.dec[b.slot[self.group * GROUP + member]] = jnp.where(self.inside(member), value, 0.0)

        steps += [functools.partial(finish, member) for member in range(GROUP)]

        def low(start):
            where = pl.ds(start, CHUNK)
            d.gl[where] = d.g[where].astype(BF)

        steps += [functools.partial(low, start) for start in self.chunks()]

        def back():
            b.d_down[1] += tn(d.gl[...], d.act[...])
            b.d_b_down[1] += fold_rows(d.g[...])
            v.grad_act = nn(d.gl[...], b.down_t[1])
            v.total = None

        steps.append(back)

        def unbend(start):
            part = (v.grad_act[start : start + 16] * d.slope[pl.ds(start, 16)]).astype(BF)
            d.gh[pl.ds(start, 16)] = part
            summed = fold_rows(part.astype(F32))
            v.total = summed if v.total is None else v.total + summed

        steps += [functools.partial(unbend, start) for start in range(0, self.rows, 16)]

        def end():
            b.d_b_up[1] += v.total
            b.d_up[1] += tn(d.n2[...], d.gh[...])
            d.gn2[...] = nn(d.gh[...], b.up_t[1])

        steps.append(end)
        return steps

    def retreat(self):
        b, d, w, slots = self.b, self.d, self.b.w, self.slots
        v = Box()
        steps = []

        def norm(start):
            where = pl.ds(start, CHUNK)
            grad, gain_part, bias_part = ln_bwd(d.gn2[where], w.gain[3:4], d.hat2, d.inv2, where)
            b.d_gain[3] += gain_part
            b.d_bias[3] += bias_part
            grad = grad + d.g[where]
            d.g[where] = grad
            d.gl[where] = grad.astype(BF)

        steps += [functools.partial(norm, start) for start in self.chunks()]

        def out():
            b.d_out[1] += tn(d.att[...], d.gl[...])
            v.grad_att = nn(d.gl[...], b.out_t[1])
            v.grad, v.prob, v.grad_p, v.grad_s, v.grad_v, v.grad_k, v.grad_q = ({} for _ in range(7))

        steps.append(out)

        def spread(member):
            pair = (member, member + 1)
            for one in pair:
                v.grad[one] = expand_halves(self.padded(v.grad_att[self.cut(one)]), b.masks_half)
            grads = [v.grad[one] for one in pair]
            v.grad_p[member], v.grad_p[member + 1] = pair_nt([d.v[one] for one in pair], grads)

        def values(member):
            pair = (member, member + 1)
            probs = [d.probs[one].astype(BF) for one in pair]
            v.grad_v[member], v.grad_v[member + 1] = pair_nn(probs, [v.grad[one] for one in pair])

        def soft(member):
            v.grad_s[member] = soft_bwd_halves(d.probs[member], v.grad_p[member])

        def keys(member):
            pair = (member, member + 1)
            columns = [expand_halves(d.q[one], b.masks_half) for one in pair]
            v.grad_k[member], v.grad_k[member + 1] = pair_nn([v.grad_s[one] for one in pair], columns)

        def queries(member):
            pair = (member, member + 1)
            grads = pair_tn([v.grad_s[one] for one in pair], [d.k[one] for one in pair])
            v.grad_q[member], v.grad_q[member + 1] = grads

        def gather(member):
            d.gqkv32[self.span(member), 256:384] = join_halves(v.grad_v[member])
            d.gqkv32[self.span(member), 128:256] = join_halves(v.grad_k[member])
            d.gqkv32[self.span(member), 0:128] = fold_halves(v.grad_q[member], PAD, slots) * 0.25

        for first in range(0, GROUP, BATCH):
            for stage, stride in ((spread, 2), (values, 2), (soft, 1), (keys, 2), (queries, 2), (gather, 1)):
                steps += [functools.partial(stage, member) for member in range(first, first + BATCH, stride)]

        def low(start):
            where = pl.ds(start, CHUNK)
            d.gqkv[where] = d.gqkv32[where].astype(BF)

        steps += [functools.partial(low, start) for start in self.chunks()]

        def project():
            b.d_qkv[1] += tn(d.n1[...], d.gqkv[...])
            v.grad_n1 = nn(d.gqkv[...], b.qkv_t[1])
            v.pos = None

        steps.append(project)

        def first_norm(start):
            where = pl.ds(start, CHUNK)
            grad, gain_part, bias_part = ln_bwd(
                v.grad_n1[start : start + CHUNK], w.gain[2:3], d.hat1, d.inv1, where
            )
            b.d_gain[2] += gain_part
            b.d_bias[2] += bias_part
            grad = grad + d.g[where]
            d.gl[where] = grad.astype(BF)
            part = jnp.sum(grad.reshape(CHUNK // slots, slots, 128), axis=0)
            v.pos = part if v.pos is None else v.pos + part
            b.d_mask[...] += fold_rows(grad * d.unseen[where])

        steps += [functools.partial(first_norm, start) for start in self.chunks()]

        def end():
            b.d_pos[...] += v.pos
            b.g_sent[self.sent_rows] = tn(d.hot[...], d.gl[...]).astype(BF)

        steps.append(end)
        return steps


def decoder_all(b, groups, before, after):
    first, second = b.sets
    pairs = groups // 2
    here = Decoder(b, first, 0)
    there = Decoder(b, second, 1)
    weave(before, here.attend())
    weave(here.bend())
    weave(here.feed(), there.attend())

    def pair(index, carry):
        here = Decoder(b, first, 2 * index)
        there = Decoder(b, second, 2 * index + 1)
        later = Decoder(b, first, 2 * index + 2)
        latest = Decoder(b, second, 2 * index + 3)
        weave(there.bend(), here.retreat())
        weave(there.feed(), later.attend())
        weave(later.bend(), there.retreat())
        weave(later.feed(), latest.attend())
        return carry

    lax.fori_loop(0, pairs - 1, pair, 0)
    here = Decoder(b, first, groups - 2)
    there = Decoder(b, second, groups - 1)
    weave(there.bend(), here.retreat())
    weave(there.feed())
    weave(there.retreat(), after)


IN_NAMES = (
    "take", "back_at", "slot", "recv", "cot", "w_qkv", "w_out", "w_up", "w_down", "b_up", "b_down", "gain",
    "bias", "mask", "pos",
)
OUT_NAMES = ("dec", "back", "grads")


def small_rows(slots):
    return 18 + 1 + slots


def main_kernel(names, cap, extra, count, *refs):
    b = Box()
    b.sets = (Box(), Box())
    for name, ref in zip(names, refs, strict=True):
        name, _, side = name.partition("@")
        setattr(b.sets[int(side)] if side else b, name, ref)
    b.w = Box()
    for name in ("qkv", "out", "up", "down"):
        setattr(b.w, name, getattr(b, "w_" + name))
    for name in ("b_up", "b_down", "gain", "bias", "mask", "pos"):
        setattr(b.w, name, getattr(b, name))
    b.slots = b.cot.shape[1]
    pixels = b.cot.shape[0]
    groups = pixels // GROUP
    block = cap + extra
    for head in range(HEADS):
        lane = iota((PAD, 128), 1) // HEAD_DIM
        b.masks[head] = jnp.where(lane == head, 1.0, 0.0).astype(BF)
    for head in range(FOLD):
        lane = iota((PAD, 128), 1) // HEAD_DIM % FOLD
        b.masks_half[head] = jnp.where(lane == head, 1.0, 0.0).astype(BF)
    for layer in range(2):
        b.qkv_t[layer] = b.w_qkv[layer].T
        b.out_t[layer] = b.w_out[layer].T
        b.up_t[layer] = b.w_up[layer].T
        b.down_t[layer] = b.w_down[layer].T
    for ref in (b.d_qkv, b.d_out, b.d_up, b.d_down, b.d_gain, b.d_bias, b.d_b_up, b.d_b_down, b.d_mask, b.d_pos):
        ref[...] = jnp.zeros(ref.shape, F32)

    def gather(dev, carry):
        pos, lens = carry
        return (
            pos + b.recv[dev * block + cap].astype(F32),
            lens + b.recv[dev * block + cap + 1].astype(F32),
        )

    empty = jnp.zeros((groups, 128), F32)
    pos, lens = lax.fori_loop(0, count, gather, (empty, empty))
    for group in range(groups):
        where = pl.ds(group * 128, 128)
        b.pos_row[group] = pos[group : group + 1]
        b.pos_col[where] = jnp.broadcast_to(pos[group : group + 1], (128, 128)).T
        b.len_col[where] = jnp.broadcast_to(lens[group : group + 1], (128, 128)).T

    encoders = [Encoder(b, base, ENC_ROWS) for base in range(0, pixels * VIS, ENC_ROWS)]
    weave(encoders[0].attend())
    for now, later in zip(encoders, encoders[1:]):
        weave(now.bend(), later.attend())
    decoder_all(b, groups, encoders[-1].bend(), encoders[0].feed())
    for now, later in zip(encoders, encoders[1:]):
        weave(now.retreat(), later.feed())
    weave(encoders[-1].retreat())

    offset = 0
    for layer in range(2):
        for start in range(0, 384, 128):
            b.grads[offset : offset + 128] = b.d_qkv[layer, :, start : start + 128].astype(BF)
            offset += 128
        b.grads[offset : offset + 128] = b.d_out[layer].astype(BF)
        offset += 128
        for start in range(0, 512, 128):
            b.grads[offset : offset + 128] = b.d_up[layer, :, start : start + 128].astype(BF)
            offset += 128
        for start in range(0, 512, 128):
            b.grads[offset : offset + 128] = b.d_down[layer, :, start : start + 128].T.astype(BF)
            offset += 128

    def total(ref, index):
        return jnp.sum(ref[index], axis=0, keepdims=True)

    small = [total(b.d_gain, i) for i in range(4)] + [total(b.d_bias, i) for i in range(4)]
    for layer in range(2):
        row = total(b.d_b_up, layer)
        small += [row[:, start : start + 128] for start in range(0, 512, 128)]
    small += [total(b.d_b_down, layer) for layer in range(2)]
    small.append(jnp.sum(b.d_mask[...], axis=0, keepdims=True))
    small.append(b.d_pos[...])
    tail = jnp.concatenate(small, axis=0)
    fill = -tail.shape[0] % 16
    tail = jnp.concatenate([tail, jnp.zeros((fill, 128), F32)], axis=0)
    b.grads[offset : offset + tail.shape[0]] = tail.astype(BF)


def decoder_scratch(rows, slots):
    return {
        "hot": ((rows, 128), BF),
        "unseen": ((rows, 128), F32),
        "x": ((rows, 128), F32),
        "g": ((rows, 128), F32),
        "gl": ((rows, 128), BF),
        "hat1": ((rows, 128), F32),
        "inv1": ((rows, 128), F32),
        "n1": ((rows, 128), BF),
        "q": ((GROUP, PAD, 128), BF),
        "k": ((GROUP, 2 * slots, 128), BF),
        "v": ((GROUP, 2 * slots, 128), BF),
        "probs": ((GROUP, 2 * slots, 128), F32),
        "att32": ((rows, 128), F32),
        "att": ((rows, 128), BF),
        "hat2": ((rows, 128), F32),
        "inv2": ((rows, 128), F32),
        "n2": ((rows, 128), BF),
        "act": ((rows, 512), BF),
        "slope": ((rows, 512), F32),
        "gh": ((rows, 512), BF),
        "gn2": ((rows, 128), F32),
        "gqkv32": ((rows, 384), F32),
        "gqkv": ((rows, 384), BF),
    }


def main_call(args, cap, extra, count, grad_rows):
    recv, cot = args[3], args[4]
    pixels, slots, width = cot.shape
    enc = pixels * VIS
    rows = GROUP * slots
    smem = pl.BlockSpec(memory_space=pltpu.SMEM)
    vmem = pl.BlockSpec(memory_space=pltpu.VMEM)
    scratch = {
        "masks": ((HEADS, PAD, 128), BF),
        "masks_half": ((FOLD, PAD, 128), BF),
        "qkv_t": ((2, 384, 128), BF),
        "out_t": ((2, 128, 128), BF),
        "up_t": ((2, 512, 128), BF),
        "down_t": ((2, 128, 512), BF),
        "d_qkv": ((2, 128, 384), F32),
        "d_out": ((2, 128, 128), F32),
        "d_up": ((2, 128, 512), F32),
        "d_down": ((2, 128, 512), F32),
        "d_gain": ((4, 8, 128), F32),
        "d_bias": ((4, 8, 128), F32),
        "d_b_up": ((2, 8, 512), F32),
        "d_b_down": ((2, 8, 128), F32),
        "d_mask": ((8, 128), F32),
        "d_pos": ((slots, 128), F32),
        "pos_row": ((pixels // GROUP, 1, 128), F32),
        "pos_col": ((enc, 128), F32),
        "len_col": ((enc, 128), F32),
        "sent": ((enc, 128), BF),
        "g_sent": ((enc, 128), BF),
        "e_x": ((enc, 128), F32),
        "e_hat1": ((enc, 128), F32),
        "e_inv1": ((enc, 128), F32),
        "e_n1": ((enc, 128), BF),
        "e_qkv": ((enc, 384), BF),
        "e_probs": ((enc, 128), F32),
        "e_att": ((enc, 128), BF),
        "e_hat2": ((enc, 128), F32),
        "e_inv2": ((enc, 128), F32),
        "e_n2": ((enc, 128), BF),
        "e_act": ((enc, 512), BF),
        "e_slope": ((enc, 512), F32),
        "e_gh": ((enc, 512), BF),
        "e_gn2": ((enc, 128), F32),
        "e_gm": ((enc, 128), F32),
        "e_gml": ((enc, 128), BF),
        "e_gqkv": ((enc, 384), BF),
    }
    for side in range(2):
        for name, entry in decoder_scratch(rows, slots).items():
            scratch[f"{name}@{side}"] = entry
    names = IN_NAMES + OUT_NAMES + tuple(scratch)
    return pl.pallas_call(
        functools.partial(main_kernel, names, cap, extra, count),
        out_shape=(
            jax.ShapeDtypeStruct((pixels, slots, width), F32),
            jax.ShapeDtypeStruct((count * cap, VIS, width), BF),
            jax.ShapeDtypeStruct((grad_rows, 128), BF),
        ),
        in_specs=[smem] * 3 + [vmem] * (len(IN_NAMES) - 3),
        out_specs=(vmem, vmem, vmem),
        scratch_shapes=[pltpu.VMEM(shape, kind) for shape, kind in scratch.values()],
        compiler_params=pltpu.CompilerParams(vmem_limit_bytes=VMEM_LIMIT),
        name="layers",
    )(*args)


def pair_sum_kernel(core_ref, mine_ref, theirs_ref, out_ref):
    core = core_ref[0]
    out_ref[...] = (mine_ref[core].astype(F32) + theirs_ref[core].astype(F32)).astype(BF)


def chunk_sum_kernel(parts_ref, out_ref):
    total = parts_ref[0].astype(F32)
    for part in range(1, parts_ref.shape[0]):
        total = total + parts_ref[part].astype(F32)
    low = total.astype(BF)
    for part in range(parts_ref.shape[0]):
        out_ref[part] = low


def unpack_kernel(
    slots, core_ref, mine_ref, theirs_ref, gain_ref, bias_ref, qkv_ref, out_ref, up_ref, b_up_ref, down_ref,
    b_down_ref, mask_ref, pos_ref, full,
):
    core = core_ref[0]
    full[core] = mine_ref[...]
    full[1 - core] = theirs_ref[...]
    half = full.shape[1]

    def rows(start, size):
        side, at = start // half, start % half
        if at + size <= half:
            return full[side, at : at + size].astype(F32)
        cut = half - at
        return jnp.concatenate(
            [full[side, at:half].astype(F32), full[side + 1, 0 : size - cut].astype(F32)], axis=0
        )

    offset = 0
    for layer in range(2):
        for start in range(0, 384, 128):
            qkv_ref[layer, :, start : start + 128] = rows(offset, 128)
            offset += 128
        out_ref[layer] = rows(offset, 128)
        offset += 128
        for start in range(0, 512, 128):
            up_ref[layer, :, start : start + 128] = rows(offset, 128)
            offset += 128
        for start in range(0, 512, 128):
            down_ref[layer, start : start + 128, :] = rows(offset, 128)
            offset += 128
    count = small_rows(slots)
    small = rows(offset, count + (-count % 16))
    gain_ref[...] = small[0:4]
    bias_ref[...] = small[4:8]
    for layer in range(2):
        for part in range(4):
            at = 8 + 4 * layer + part
            b_up_ref[layer : layer + 1, part * 128 : (part + 1) * 128] = small[at : at + 1]
    b_down_ref[...] = small[16:18]
    mask_ref[...] = small[18:19]
    pos_ref[...] = small[19 : 19 + slots]


def restore_kernel(place_ref, pos_ref, rows_ref, out_ref, held):
    groups = pos_ref.shape[0]
    wide = out_ref.shape[0] // groups
    slots = wide // GROUP
    lane = iota((1, 128), 1)
    for group in range(groups):
        for member in range(GROUP):
            block = rows_ref[place_ref[group * GROUP + member]]
            held[pl.ds(member * VIS, VIS)] = block.astype(F32)
        pos_row = pos_ref[group : group + 1]
        target = jnp.where(pos_row > 0, (lane // VIS * slots).astype(F32) + pos_row - 1.0, -1.0)
        hot = jnp.where(iota((wide, 128), 0).astype(F32) == target, 1.0, 0.0).astype(BF)
        out_ref[group * wide : (group + 1) * wide, :] = nn(hot, held[...].astype(BF))


def shards(
    tokens, lengths, masked, route_dev, route_slot, norm_gain, norm_bias, w_qkv, w_out, w_up, b_up, w_down,
    b_down, mask_token, pos_table, cotangent,
):
    count = lax.axis_size("pix")
    reps = lax.axis_size("rep")
    devices = count * reps
    pixels, slots, width = tokens.shape
    cap = max(2, (2 * pixels + count - 1) // count)
    extra = 2
    smem = pl.BlockSpec(memory_space=pltpu.SMEM)
    vmem = pl.BlockSpec(memory_space=pltpu.VMEM)
    params = pltpu.CompilerParams(vmem_limit_bytes=VMEM_LIMIT)
    pix = lax.axis_index("pix")
    me = pix.reshape(1).astype(jnp.int32)
    flat = pix * reps + lax.axis_index("rep")
    core = (flat % 2).reshape(1).astype(jnp.int32)
    payload, pos_rows, place, take, back_at = prep(
        tokens, lengths, masked, route_dev, count, cap, extra, me
    )
    block = cap + extra
    recv = lax.all_to_all(
        payload.reshape(count, block, VIS, width), "pix", split_axis=0, concat_axis=0, tiled=True
    ).reshape(count * block, VIS, width)
    chunk = -(-(3072 + small_rows(slots)) // devices)
    chunk += -chunk % 8
    half = devices // 2
    dec, back, grads = main_call(
        (
            take, back_at, route_slot, recv, cotangent, w_qkv, w_out, w_up, w_down, b_up, b_down,
            norm_gain.reshape(4, width), norm_bias.reshape(4, width), mask_token.reshape(1, width), pos_table,
        ),
        cap,
        extra,
        count,
        devices * chunk,
    )
    returned = lax.all_to_all(
        back.reshape(count, cap, VIS, width), "pix", split_axis=0, concat_axis=0, tiled=True
    ).reshape(count * cap, VIS, width)
    axes = ("pix", "rep")
    swap = [(i, i ^ 1) for i in range(devices)]
    groups = [[2 * i + side for i in range(half)] for side in range(2)]

    def exchange(values):
        return lax.all_to_all(
            values, axes, split_axis=0, concat_axis=0, axis_index_groups=groups, tiled=True
        )

    grads = grads.reshape(2, half, chunk, 128)
    theirs = lax.ppermute(grads, axes, swap)
    paired = pl.pallas_call(
        pair_sum_kernel,
        out_shape=jax.ShapeDtypeStruct((half, chunk, 128), BF),
        in_specs=[smem, vmem, vmem],
        out_specs=vmem,
        compiler_params=params,
        name="pair_sum",
    )(core, grads, theirs)
    spread = pl.pallas_call(
        chunk_sum_kernel,
        out_shape=jax.ShapeDtypeStruct((half, chunk, 128), BF),
        in_specs=[vmem],
        out_specs=vmem,
        compiler_params=params,
        name="chunk_sum",
    )(exchange(paired))
    summed = exchange(spread).reshape(half * chunk, 128)
    other = lax.ppermute(summed, axes, swap)
    gain, bias, qkv, out, up, bup, down, bdown, mask, pos = pl.pallas_call(
        functools.partial(unpack_kernel, slots),
        out_shape=tuple(
            jax.ShapeDtypeStruct(shape, F32)
            for shape in (
                (4, width), (4, width), w_qkv.shape, w_out.shape, w_up.shape, b_up.shape, w_down.shape,
                b_down.shape, (1, width), pos_table.shape,
            )
        ),
        in_specs=[smem, vmem, vmem],
        out_specs=(vmem,) * 10,
        scratch_shapes=[pltpu.VMEM((2, half * chunk, 128), BF)],
        compiler_params=params,
        name="unpack",
    )(core, summed, other)
    grad_tokens = pl.pallas_call(
        restore_kernel,
        out_shape=jax.ShapeDtypeStruct((pixels * slots, width), F32),
        in_specs=[smem, vmem, vmem],
        out_specs=vmem,
        scratch_shapes=[pltpu.VMEM((GROUP * VIS, width), F32)],
        compiler_params=params,
        name="restore",
    )(place, pos_rows, returned)
    return (
        dec,
        grad_tokens.reshape(pixels, slots, width),
        gain.reshape(norm_gain.shape),
        bias.reshape(norm_bias.shape),
        qkv,
        out,
        up,
        bup,
        down,
        bdown,
        mask.reshape(width),
        pos,
    )


def solution(mesh):
    rows = P(("pix", "rep"))
    in_specs = (rows,) * 5 + (P(),) * 10 + (rows,)
    out_specs = (rows, rows) + (P(),) * 10
    return jax.shard_map(shards, mesh=mesh, in_specs=in_specs, out_specs=out_specs, check_vma=False)
```

```python
import functools

import jax
import jax.numpy as jnp
from jax import lax
from jax.experimental import pallas as pl
from jax.experimental.pallas import tpu as pltpu
from jax.sharding import PartitionSpec as P

HEADS = 8
HEAD_DIM = 16
FOLD = 4
BATCH = 16
PAIRS = 32
ENC_ROWS = 512
VIS = 8
GROUP = 16
PAD = 32
CHUNK = 48
EPS = 1e-05
NEG = -1e30
BF = jnp.bfloat16
F32 = jnp.float32
MIB = 1024 * 1024


def nn(left, right):
    return jnp.dot(left, right, preferred_element_type=F32)


def nt(left, right):
    return lax.dot_general(left, right, (((1,), (1,)), ((), ())), preferred_element_type=F32)


def tn(left, right):
    return lax.dot_general(left, right, (((0,), (0,)), ((), ())), preferred_element_type=F32)


def iota(shape, dim):
    return lax.broadcasted_iota(jnp.int32, shape, dim)


def fold_rows(values):
    rows = values.shape[0]
    return jnp.sum(values.reshape(rows // 8, 8, values.shape[1]), axis=0)


def erf_parts(hidden):
    size = jnp.abs(hidden)
    base = 1.0 + size * (0.3275911 * 0.7071067811865476)
    t = 1.0 / base
    bell = jnp.exp(hidden * hidden * -0.5)
    poly = t * (
        0.5 * 0.254829592
        + t * (0.5 * -0.284496736 + t * (0.5 * 1.421413741 + t * (0.5 * -1.453152027 + t * (0.5 * 1.061405429))))
    )
    tail = poly * bell
    return jnp.where(hidden >= 0, 1.0 - tail, tail), bell


def expand(rows, masks):
    count = rows.shape[0]
    return jnp.concatenate([rows * masks[h, :count, :] for h in range(HEADS)], axis=0)


def fold_heads(rows, step, count):
    lane = iota((count, 128), 1)
    picked = rows[0:count]
    for head in range(1, HEADS):
        picked = jnp.where(lane >= head * HEAD_DIM, rows[head * step : head * step + count], picked)
    return picked


def fold_halves(rows, step, count):
    lane = iota((count, 128), 1) // HEAD_DIM % FOLD
    picked = rows[0:count]
    for head in range(1, FOLD):
        picked = jnp.where(lane == head, rows[head * step : head * step + count], picked)
    return picked


def expand_halves(rows, masks):
    return jnp.concatenate([rows * masks[h] for h in range(FOLD)], axis=0)


def stack_halves(values):
    low = iota(values.shape, 1) < 64
    return jnp.concatenate([jnp.where(low, values, 0.0), jnp.where(low, 0.0, values)], axis=0).astype(BF)


def join_halves(values):
    count = values.shape[0] // 2
    return jnp.where(iota((count, 128), 1) < 64, values[:count], values[count:])


def both_diagonals(values, rows):
    return values[:rows, :128], values[rows:, 128:]


def block_diagonal(first, second):
    low = jnp.concatenate([first, jnp.zeros_like(first)], axis=1)
    return jnp.concatenate([low, jnp.concatenate([jnp.zeros_like(second), second], axis=1)], axis=0)


def pair_nt(rows, columns):
    full = nt(jnp.concatenate(rows, axis=0), jnp.concatenate(columns, axis=0))
    return both_diagonals(full, rows[0].shape[0])


def pair_nn(rows, columns):
    full = nn(jnp.concatenate(rows, axis=0), jnp.concatenate(columns, axis=1))
    return both_diagonals(full, rows[0].shape[0])


def pair_tn(rows, columns):
    full = tn(jnp.concatenate(rows, axis=0), block_diagonal(*columns))
    return full[:, :128], full[:, 128:]


def softmax_halves(scores, keep):
    count = scores.shape[0] // 2
    scores = jnp.where(keep[None], scores.reshape(2, count, 128), NEG)
    powers = jnp.exp(scores - jnp.max(scores, axis=1, keepdims=True))
    probs = powers * (1.0 / jnp.sum(powers, axis=1, keepdims=True))
    return probs.reshape(2 * count, 128)


def soft_bwd_halves(probs, grad):
    count = probs.shape[0] // 2
    both = (grad * probs).reshape(2, count, 128)
    lean = jnp.sum(both, axis=1, keepdims=True)
    return (probs.reshape(2, count, 128) * (grad.reshape(2, count, 128) - lean)).reshape(2 * count, 128).astype(BF)


def ln_fwd(values, gain, bias, hat, inv, low, where):
    centred = values - jnp.mean(values, axis=-1, keepdims=True)
    scale = lax.rsqrt(jnp.mean(centred * centred, axis=-1, keepdims=True) + EPS)
    unit = centred * scale
    hat[where] = unit
    inv[where] = jnp.broadcast_to(scale, unit.shape)
    low[where] = (unit * gain + bias).astype(BF)


def ln_bwd(grad, gain, hat, inv, where):
    unit = hat[where]
    inner = grad * gain
    lean = jnp.mean(inner, axis=-1, keepdims=True)
    tilt = jnp.mean(inner * unit, axis=-1, keepdims=True)
    return inv[where] * (inner - lean - unit * tilt), fold_rows(grad * unit), fold_rows(grad)


def prep_kernel(
    cap, extra, count, me_ref, dest_ref, tokens_ref, len_ref, masked_ref, dest_row_ref,
    payload_ref, pos_ref, take_ref, back_ref, tally,
):
    slots, pixels = masked_ref.shape
    groups = pixels // GROUP
    block = cap + extra
    wide = GROUP * slots
    lanes = GROUP * VIS
    lens = len_ref[...].astype(F32)
    seen = (masked_ref[...] == 0) & (iota((slots, pixels), 0).astype(F32) < lens)
    seen_low = jnp.where(seen, 1.0, 0.0).astype(BF)
    earlier = jnp.where(iota((slots, slots), 1) < iota((slots, slots), 0), 1.0, 0.0).astype(BF)
    member = iota((slots, pixels), 1) % GROUP
    code = jnp.where(seen, nn(earlier, seen_low) + (member * VIS).astype(F32), -1.0)
    spread = jnp.where(iota((slots, wide), 0) == iota((slots, wide), 1) % slots, 1.0, 0.0).astype(BF)
    code_wide = tn(code.astype(BF), spread)
    own = iota((pixels, wide), 0) % GROUP == iota((pixels, wide), 1) // slots
    code_row = jnp.sum(jnp.where(own, code_wide, 0.0).reshape(groups, GROUP, wide), axis=1)
    in_group = iota((groups, pixels), 1) // GROUP == iota((groups, pixels), 0)
    fan = iota((pixels, lanes), 0) % GROUP == iota((pixels, lanes), 1) // VIS
    fan = jnp.where(fan, 1.0, 0.0).astype(BF)
    len_rows = nn(jnp.where(in_group, lens, 0.0).astype(BF), fan)
    dest_rows = nn(jnp.where(in_group, dest_row_ref[...].astype(F32), 0.0).astype(BF), fan)
    me = me_ref[0]
    for dev in range(count):
        tally[dev] = 0
    order = iota((lanes, wide), 0).astype(F32)
    steps = (iota((GROUP, wide), 1) % slots + 1).astype(F32).astype(BF)
    found = []
    for group in range(groups):
        select = jnp.where(order == code_row[group : group + 1, :], 1.0, 0.0).astype(BF)
        rows = nn(select, tokens_ref[group * wide : (group + 1) * wide, :]).reshape(GROUP, VIS, 128)
        found.append(nt(steps, select)[0:1, :])
        for member_id in range(GROUP):
            series = group * GROUP + member_id
            dest = dest_ref[series]
            rank = tally[dest]
            tally[dest] = rank + 1
            sender = lax.rem(2 * me - dest + 2 * count, count)
            take_ref[series] = sender * block + rank
            back_ref[series] = lax.rem(dest - me + count, count) * cap + rank
            payload_ref[dest * block + rank] = rows[member_id].astype(BF)
    pos_rows = jnp.concatenate(found, axis=0)
    pos_ref[...] = pos_rows

    def label(dev, carry):
        mine = dest_rows == dev.astype(F32)
        payload_ref[dev * block + cap] = jnp.where(mine, pos_rows, 0.0).astype(BF)
        payload_ref[dev * block + cap + 1] = jnp.where(mine, len_rows, 0.0).astype(BF)
        return carry

    lax.fori_loop(0, count, label, 0)


def prep(tokens, lengths, masked, route_dev, count, cap, extra, me):
    pixels, slots, width = tokens.shape
    smem = pl.BlockSpec(memory_space=pltpu.SMEM)
    vmem = pl.BlockSpec(memory_space=pltpu.VMEM)
    index = jax.ShapeDtypeStruct((pixels,), jnp.int32)
    return pl.pallas_call(
        functools.partial(prep_kernel, cap, extra, count),
        out_shape=(
            jax.ShapeDtypeStruct((count * (cap + extra), VIS, width), BF),
            jax.ShapeDtypeStruct((pixels // GROUP, GROUP * VIS), F32),
            index,
            index,
        ),
        in_specs=[smem, smem, vmem, vmem, vmem, vmem],
        out_specs=(vmem, vmem, smem, smem),
        scratch_shapes=[pltpu.SMEM((count,), jnp.int32)],
        compiler_params=pltpu.CompilerParams(vmem_limit_bytes=6 * MIB),
        name="prep",
    )(
        me, route_dev, tokens.reshape(pixels * slots, width), lengths.reshape(1, pixels), masked.T,
        route_dev.reshape(1, pixels),
    )


class Box:
    pass


def gelu_stage(hidden, b_up, act, slope, base, rows):
    for start in range(0, rows, 16):
        value = hidden[start : start + 16] + b_up
        cdf, bell = erf_parts(value)
        where = pl.ds(base + start, 16)
        act[where] = (value * cdf).astype(BF)
        slope[where] = cdf + value * bell * 0.3989422804014327


def slope_stage(grad_act, slope, out, base, rows):
    total = None
    for start in range(0, rows, 16):
        part = (grad_act[start : start + 16] * slope[pl.ds(base + start, 16)]).astype(BF)
        out[pl.ds(start, 16)] = part
        summed = fold_rows(part.astype(F32))
        total = summed if total is None else total + summed
    return total


def softmax_rows(scores, keep):
    scores = jnp.where(keep, scores, NEG)
    powers = jnp.exp(scores - jnp.max(scores, axis=0, keepdims=True))
    return powers / jnp.sum(powers, axis=0, keepdims=True)


def soft_bwd(probs, grad):
    return (probs * (grad - jnp.sum(grad * probs, axis=0, keepdims=True))).astype(BF)


class Encoder:
    def __init__(self, b, base, rows):
        self.b, self.base, self.rows = b, base, rows
        self.whole = slice(base, base + rows)

    def chunks(self):
        return [slice(start, start + 32) for start in range(self.base, self.base + self.rows, 32)]

    def part(self, values, where):
        return values[where.start - self.base : where.stop - self.base]

    def attend(self):
        b, w, whole = self.b, self.b.w, self.whole
        v = Box()
        same = iota((16, 128), 0) // VIS == (iota((16, 128), 1) % 16) // VIS

        def load(series):
            b.e_x[series * VIS : (series + 1) * VIS] = b.recv[b.take[series]].astype(F32)

        steps = [functools.partial(load, series) for series in range(self.base // VIS, (self.base + self.rows) // VIS)]

        def norm(where):
            ln_fwd(b.e_x[where], w.gain[0:1], w.bias[0:1], b.e_hat1, b.e_inv1, b.e_n1, where)

        steps += [functools.partial(norm, where) for where in self.chunks()]

        def project():
            v.qkv = nn(b.e_n1[whole], w.qkv[0])
            v.score, v.prob, v.mixed = {}, {}, {}

        steps.append(project)

        def split(where):
            part = self.part(v.qkv, where)
            b.e_qkv[where, 0:128] = (part[:, 0:128] * 0.25).astype(BF)
            b.e_qkv[where, 128:384] = part[:, 128:384].astype(BF)

        steps += [functools.partial(split, where) for where in self.chunks()]

        def score(at):
            pair = (at, at + 16)
            queries = [expand(b.e_qkv[one : one + 16, 0:128], b.masks) for one in pair]
            keys = [b.e_qkv[one : one + 16, 128:256] for one in pair]
            v.score[at], v.score[at + 16] = pair_nt(keys, queries)

        def soft(at):
            v.prob[at] = softmax_rows(v.score[at], same & (b.pos_col[at : at + 16] > 0))
            b.e_probs[at : at + 16] = v.prob[at]

        def mix(at):
            pair = (at, at + 16)
            values = [b.e_qkv[one : one + 16, 256:384] for one in pair]
            v.mixed[at], v.mixed[at + 16] = pair_tn([v.prob[one].astype(BF) for one in pair], values)

        def gather(at):
            b.e_att[at : at + 16] = fold_heads(v.mixed[at], 16, 16).astype(BF)

        for first in range(self.base, self.base + self.rows, 16 * PAIRS):
            for stage, stride in ((score, 32), (soft, 16), (mix, 32), (gather, 16)):
                steps += [functools.partial(stage, at) for at in range(first, first + 16 * PAIRS, stride)]

        def out():
            v.proj = nn(b.e_att[whole], w.out[0])

        steps.append(out)

        def second(where):
            middle = b.e_x[where] + self.part(v.proj, where)
            b.e_x[where] = middle
            ln_fwd(middle, w.gain[1:2], w.bias[1:2], b.e_hat2, b.e_inv2, b.e_n2, where)

        steps += [functools.partial(second, where) for where in self.chunks()]
        return steps

    def bend(self):
        b, w, whole = self.b, self.b.w, self.whole
        v = Box()

        def up():
            v.hidden = nn(b.e_n2[whole], w.up[0])

        def curve(start):
            value = v.hidden[start : start + 16] + w.b_up[0:1]
            cdf, bell = erf_parts(value)
            where = slice(self.base + start, self.base + start + 16)
            b.e_act[where] = (value * cdf).astype(BF)
            b.e_slope[where] = cdf + value * bell * 0.3989422804014327

        def down():
            v.down = nn(b.e_act[whole], w.down[0])

        def finish(where):
            b.sent[where] = (b.e_x[where] + self.part(v.down, where) + w.b_down[0:1]).astype(BF)

        return (
            [up]
            + [functools.partial(curve, start) for start in range(0, self.rows, 16)]
            + [down]
            + [functools.partial(finish, where) for where in self.chunks()]
        )

    def feed(self):
        b, whole = self.b, self.whole
        v = Box()

        def back():
            grad_low = b.g_sent[whole]
            b.d_down[0] += tn(grad_low, b.e_act[whole])
            b.d_b_down[0] += fold_rows(grad_low.astype(F32))
            v.grad_act = nn(grad_low, b.down_t[0])
            v.total = None

        def unbend(start):
            where = slice(self.base + start, self.base + start + 16)
            part = (v.grad_act[start : start + 16] * b.e_slope[where]).astype(BF)
            b.e_gh[where] = part
            summed = fold_rows(part.astype(F32))
            v.total = summed if v.total is None else v.total + summed

        def end():
            b.d_b_up[0] += v.total
            b.d_up[0] += tn(b.e_n2[whole], b.e_gh[whole])
            b.e_gn2[whole] = nn(b.e_gh[whole], b.up_t[0])

        return [back] + [functools.partial(unbend, start) for start in range(0, self.rows, 16)] + [end]

    def retreat(self):
        b, w, whole = self.b, self.b.w, self.whole
        v = Box()

        def norm(where):
            grad, gain_part, bias_part = ln_bwd(b.e_gn2[where], w.gain[1:2], b.e_hat2, b.e_inv2, where)
            b.d_gain[1] += gain_part
            b.d_bias[1] += bias_part
            grad = grad + b.g_sent[where].astype(F32)
            b.e_gm[where] = grad
            b.e_gml[where] = grad.astype(BF)

        steps = [functools.partial(norm, where) for where in self.chunks()]

        def out():
            b.d_out[0] += tn(b.e_att[whole], b.e_gml[whole])
            v.grad_att = nn(b.e_gml[whole], b.out_t[0])
            v.grad, v.grad_p, v.grad_s, v.grad_v, v.grad_k, v.grad_q = ({} for _ in range(6))

        steps.append(out)

        def spread(at):
            pair = (at, at + 16)
            for one in pair:
                low = v.grad_att[one - self.base : one - self.base + 16].astype(BF)
                v.grad[one] = expand(low, b.masks)
            values = [b.e_qkv[one : one + 16, 256:384] for one in pair]
            v.grad_p[at], v.grad_p[at + 16] = pair_nt(values, [v.grad[one] for one in pair])

        def values(at):
            pair = (at, at + 16)
            probs = [b.e_probs[one : one + 16].astype(BF) for one in pair]
            v.grad_v[at], v.grad_v[at + 16] = pair_nn(probs, [v.grad[one] for one in pair])

        def soft(at):
            v.grad_s[at] = soft_bwd(b.e_probs[at : at + 16], v.grad_p[at])

        def keys(at):
            pair = (at, at + 16)
            columns = [expand(b.e_qkv[one : one + 16, 0:128], b.masks) for one in pair]
            v.grad_k[at], v.grad_k[at + 16] = pair_nn([v.grad_s[one] for one in pair], columns)

        def queries(at):
            pair = (at, at + 16)
            keys = [b.e_qkv[one : one + 16, 128:256] for one in pair]
            v.grad_q[at], v.grad_q[at + 16] = pair_tn([v.grad_s[one] for one in pair], keys)

        def gather(at):
            b.e_gqkv[at : at + 16, 256:384] = v.grad_v[at].astype(BF)
            b.e_gqkv[at : at + 16, 128:256] = v.grad_k[at].astype(BF)
            b.e_gqkv[at : at + 16, 0:128] = (fold_heads(v.grad_q[at], 16, 16) * 0.25).astype(BF)

        for first in range(self.base, self.base + self.rows, 16 * PAIRS):
            for stage, stride in ((spread, 32), (values, 32), (soft, 16), (keys, 32), (queries, 32), (gather, 16)):
                steps += [functools.partial(stage, at) for at in range(first, first + 16 * PAIRS, stride)]

        def project():
            b.d_qkv[0] += tn(b.e_n1[whole], b.e_gqkv[whole])
            v.grad_n1 = nn(b.e_gqkv[whole], b.qkv_t[0])

        steps.append(project)

        def first_norm(where):
            grad, gain_part, bias_part = ln_bwd(
                self.part(v.grad_n1, where), w.gain[0:1], b.e_hat1, b.e_inv1, where
            )
            b.d_gain[0] += gain_part
            b.d_bias[0] += bias_part
            grad = grad + b.e_gm[where]
            for series in range(where.start // VIS, where.stop // VIS):
                at = series * VIS - where.start
                b.back[b.back_at[series]] = grad[at : at + VIS].astype(BF)

        steps += [functools.partial(first_norm, where) for where in self.chunks()]
        return steps


def weave(*streams):
    lists = [list(stream) for stream in streams]
    order = []
    for which, steps in enumerate(lists):
        order += [((index + 0.5) / len(steps), which, step) for index, step in enumerate(steps)]
    for _, _, step in sorted(order, key=lambda entry: entry[:2]):
        step()


class Decoder:
    def __init__(self, b, d, group):
        self.b, self.d, self.group = b, d, group
        self.slots = b.slots
        self.rows = GROUP * b.slots
        self.sent_rows = pl.ds(pl.multiple_of(group * 128, 128), 128)
        self.zeros = jnp.zeros((PAD - b.slots, 128), F32)
        self.step = iota((b.slots, 128), 0).astype(F32)

    def span(self, member):
        return pl.ds(member * self.slots, self.slots)

    def cut(self, member):
        return slice(member * self.slots, (member + 1) * self.slots)

    def inside(self, member):
        lens = self.b.len_col[pl.ds(pl.multiple_of(self.group * 128, 128) + member * VIS, VIS)]
        return self.step < jnp.concatenate([lens] * (self.slots // VIS), axis=0)

    def padded(self, values):
        return jnp.concatenate([values, self.zeros], axis=0).astype(BF)

    def chunks(self):
        return range(0, self.rows, CHUNK)

    def attend(self):
        b, d, w, slots = self.b, self.d, self.b.w, self.slots
        v = Box()
        steps = []

        def begin():
            pos_row = b.pos_row[self.group]
            lane = iota((1, 128), 1)
            target = jnp.where(pos_row > 0, (lane // VIS * slots).astype(F32) + pos_row - 1.0, -1.0)
            for start in self.chunks():
                spot = (iota((CHUNK, 128), 0) + start).astype(F32)
                d.hot[pl.ds(start, CHUNK)] = jnp.where(spot == target, 1.0, 0.0).astype(BF)
            v.placed = nn(d.hot[...], b.sent[self.sent_rows])
            v.shown = nn(d.hot[...], jnp.ones((128, 128), BF))

        steps.append(begin)

        def assemble(member):
            at = self.cut(member)
            hidden_part = 1.0 - v.shown[at]
            d.unseen[self.span(member)] = hidden_part
            d.x[self.span(member)] = v.placed[at] + hidden_part * w.mask[...] + w.pos[...]
            cot = b.cot[b.slot[self.group * GROUP + member]].astype(F32)
            d.g[self.span(member)] = jnp.where(self.inside(member), cot, 0.0)

        steps += [functools.partial(assemble, member) for member in range(GROUP)]

        def norm(start):
            where = pl.ds(start, CHUNK)
            ln_fwd(d.x[where], w.gain[2:3], w.bias[2:3], d.hat1, d.inv1, d.n1, where)

        steps += [functools.partial(norm, start) for start in self.chunks()]

        def project():
            v.qkv = nn(d.n1[...], w.qkv[1])
            v.score, v.prob, v.mixed = {}, {}, {}

        steps.append(project)

        def split(member):
            at = self.cut(member)
            d.q[member] = self.padded(v.qkv[at, 0:128] * 0.25)
            d.k[member] = stack_halves(v.qkv[at, 128:256])
            d.v[member] = stack_halves(v.qkv[at, 256:384])

        def score(member):
            pair = (member, member + 1)
            queries = [expand_halves(d.q[one], b.masks_half) for one in pair]
            v.score[member], v.score[member + 1] = pair_nt([d.k[one] for one in pair], queries)

        def soft(member):
            v.prob[member] = softmax_halves(v.score[member], self.inside(member))
            d.probs[member] = v.prob[member]

        def mix(member):
            pair = (member, member + 1)
            mixed = pair_tn([v.prob[one].astype(BF) for one in pair], [d.v[one] for one in pair])
            v.mixed[member], v.mixed[member + 1] = mixed

        def gather(member):
            d.att32[self.span(member)] = fold_halves(v.mixed[member], PAD, slots)

        for first in range(0, GROUP, BATCH):
            for stage, stride in ((split, 1), (score, 2), (soft, 1), (mix, 2), (gather, 1)):
                steps += [functools.partial(stage, member) for member in range(first, first + BATCH, stride)]

        def low(start):
            where = pl.ds(start, CHUNK)
            d.att[where] = d.att32[where].astype(BF)

        steps += [functools.partial(low, start) for start in self.chunks()]

        def out():
            v.proj = nn(d.att[...], w.out[1])

        steps.append(out)

        def second(start):
            where = pl.ds(start, CHUNK)
            middle = d.x[where] + v.proj[start : start + CHUNK]
            d.x[where] = middle
            ln_fwd(middle, w.gain[3:4], w.bias[3:4], d.hat2, d.inv2, d.n2, where)

        steps += [functools.partial(second, start) for start in self.chunks()]
        return steps

    def bend(self):
        b, d, w = self.b, self.d, self.b.w
        v = Box()
        steps = []

        def up():
            v.hidden = nn(d.n2[...], w.up[1])

        steps.append(up)

        def curve(start):
            value = v.hidden[start : start + 16] + w.b_up[1:2]
            cdf, bell = erf_parts(value)
            where = pl.ds(start, 16)
            d.act[where] = (value * cdf).astype(BF)
            d.slope[where] = cdf + value * bell * 0.3989422804014327

        steps += [functools.partial(curve, start) for start in range(0, self.rows, 16)]
        return steps

    def feed(self):
        b, d, w = self.b, self.d, self.b.w
        v = Box()
        steps = []

        def down():
            v.down = nn(d.act[...], w.down[1])

        steps.append(down)

        def finish(member):
            value = d.x[self.span(member)] + v.down[self.cut(member)] + w.b_down[1:2]
            slot = b.slot[self.group * GROUP + member]
            b.dec[slot] = jnp.where(self.inside(member), value, 0.0)
            pltpu.make_async_copy(b.dec.at[slot], b.dec_out.at[slot], b.sems.at[1]).start()

        steps += [functools.partial(finish, member) for member in range(GROUP)]

        def low(start):
            where = pl.ds(start, CHUNK)
            d.gl[where] = d.g[where].astype(BF)

        steps += [functools.partial(low, start) for start in self.chunks()]

        def back():
            b.d_down[1] += tn(d.gl[...], d.act[...])
            b.d_b_down[1] += fold_rows(d.g[...])
            v.grad_act = nn(d.gl[...], b.down_t[1])
            v.total = None

        steps.append(back)

        def unbend(start):
            part = (v.grad_act[start : start + 16] * d.slope[pl.ds(start, 16)]).astype(BF)
            d.gh[pl.ds(start, 16)] = part
            summed = fold_rows(part.astype(F32))
            v.total = summed if v.total is None else v.total + summed

        steps += [functools.partial(unbend, start) for start in range(0, self.rows, 16)]

        def end():
            b.d_b_up[1] += v.total
            b.d_up[1] += tn(d.n2[...], d.gh[...])
            d.gn2[...] = nn(d.gh[...], b.up_t[1])

        steps.append(end)
        return steps

    def retreat(self):
        b, d, w, slots = self.b, self.d, self.b.w, self.slots
        v = Box()
        steps = []

        def norm(start):
            where = pl.ds(start, CHUNK)
            grad, gain_part, bias_part = ln_bwd(d.gn2[where], w.gain[3:4], d.hat2, d.inv2, where)
            b.d_gain[3] += gain_part
            b.d_bias[3] += bias_part
            grad = grad + d.g[where]
            d.g[where] = grad
            d.gl[where] = grad.astype(BF)

        steps += [functools.partial(norm, start) for start in self.chunks()]

        def out():
            b.d_out[1] += tn(d.att[...], d.gl[...])
            v.grad_att = nn(d.gl[...], b.out_t[1])
            v.grad, v.prob, v.grad_p, v.grad_s, v.grad_v, v.grad_k, v.grad_q = ({} for _ in range(7))

        steps.append(out)

        def spread(member):
            pair = (member, member + 1)
            for one in pair:
                v.grad[one] = expand_halves(self.padded(v.grad_att[self.cut(one)]), b.masks_half)
            grads = [v.grad[one] for one in pair]
            v.grad_p[member], v.grad_p[member + 1] = pair_nt([d.v[one] for one in pair], grads)

        def values(member):
            pair = (member, member + 1)
            probs = [d.probs[one].astype(BF) for one in pair]
            v.grad_v[member], v.grad_v[member + 1] = pair_nn(probs, [v.grad[one] for one in pair])

        def soft(member):
            v.grad_s[member] = soft_bwd_halves(d.probs[member], v.grad_p[member])

        def keys(member):
            pair = (member, member + 1)
            columns = [expand_halves(d.q[one], b.masks_half) for one in pair]
            v.grad_k[member], v.grad_k[member + 1] = pair_nn([v.grad_s[one] for one in pair], columns)

        def queries(member):
            pair = (member, member + 1)
            grads = pair_tn([v.grad_s[one] for one in pair], [d.k[one] for one in pair])
            v.grad_q[member], v.grad_q[member + 1] = grads

        def gather(member):
            d.gqkv32[self.span(member), 256:384] = join_halves(v.grad_v[member])
            d.gqkv32[self.span(member), 128:256] = join_halves(v.grad_k[member])
            d.gqkv32[self.span(member), 0:128] = fold_halves(v.grad_q[member], PAD, slots) * 0.25

        for first in range(0, GROUP, BATCH):
            for stage, stride in ((spread, 2), (values, 2), (soft, 1), (keys, 2), (queries, 2), (gather, 1)):
                steps += [functools.partial(stage, member) for member in range(first, first + BATCH, stride)]

        def low(start):
            where = pl.ds(start, CHUNK)
            d.gqkv[where] = d.gqkv32[where].astype(BF)

        steps += [functools.partial(low, start) for start in self.chunks()]

        def project():
            b.d_qkv[1] += tn(d.n1[...], d.gqkv[...])
            v.grad_n1 = nn(d.gqkv[...], b.qkv_t[1])
            v.pos = None

        steps.append(project)

        def first_norm(start):
            where = pl.ds(start, CHUNK)
            grad, gain_part, bias_part = ln_bwd(
                v.grad_n1[start : start + CHUNK], w.gain[2:3], d.hat1, d.inv1, where
            )
            b.d_gain[2] += gain_part
            b.d_bias[2] += bias_part
            grad = grad + d.g[where]
            d.gl[where] = grad.astype(BF)
            part = jnp.sum(grad.reshape(CHUNK // slots, slots, 128), axis=0)
            v.pos = part if v.pos is None else v.pos + part
            b.d_mask[...] += fold_rows(grad * d.unseen[where])

        steps += [functools.partial(first_norm, start) for start in self.chunks()]

        def end():
            b.d_pos[...] += v.pos
            b.g_sent[self.sent_rows] = tn(d.hot[...], d.gl[...]).astype(BF)

        steps.append(end)
        return steps


def decoder_all(b, groups, before, after):
    first, second = b.sets
    pairs = groups // 2
    here = Decoder(b, first, 0)
    there = Decoder(b, second, 1)
    weave(before, here.attend())
    weave(here.bend())
    weave(here.feed(), there.attend())

    def pair(index, carry):
        here = Decoder(b, first, 2 * index)
        there = Decoder(b, second, 2 * index + 1)
        later = Decoder(b, first, 2 * index + 2)
        latest = Decoder(b, second, 2 * index + 3)
        weave(there.bend(), here.retreat())
        weave(there.feed(), later.attend())
        weave(later.bend(), there.retreat())
        weave(later.feed(), latest.attend())
        return carry

    lax.fori_loop(0, pairs - 1, pair, 0)
    here = Decoder(b, first, groups - 2)
    there = Decoder(b, second, groups - 1)
    weave(there.bend(), here.retreat())
    weave(there.feed())
    weave(there.retreat(), after)


IN_NAMES = (
    "core", "take", "back_at", "slot", "recv_in", "cot_in", "w_qkv", "w_out", "w_up", "w_down", "b_up", "b_down",
    "gain", "bias", "mask", "pos",
)
OUT_NAMES = ("dec_out", "keep", "send")


def small_rows(slots):
    return 18 + 1 + slots


def main_kernel(names, cap, extra, count, outs, *refs):
    b = Box()
    b.sets = (Box(), Box())
    b.back_out = refs[len(IN_NAMES) + len(OUT_NAMES) : len(IN_NAMES) + len(OUT_NAMES) + outs]
    refs = refs[: len(IN_NAMES) + len(OUT_NAMES)] + refs[len(IN_NAMES) + len(OUT_NAMES) + outs :]
    for name, ref in zip(names, refs, strict=True):
        name, _, side = name.partition("@")
        setattr(b.sets[int(side)] if side else b, name, ref)
    b.w = Box()
    for name in ("qkv", "out", "up", "down"):
        setattr(b.w, name, getattr(b, "w_" + name))
    for name in ("b_up", "b_down", "gain", "bias", "mask", "pos"):
        setattr(b.w, name, getattr(b, name))
    b.slots = b.cot.shape[1]
    pixels = b.cot.shape[0]
    groups = pixels // GROUP
    block = cap + extra
    recv_copy = pltpu.make_async_copy(b.recv_in, b.recv, b.sems.at[0])
    recv_copy.start()
    cot_copy = pltpu.make_async_copy(b.cot_in, b.cot, b.sems.at[2])
    cot_copy.start()
    for head in range(HEADS):
        lane = iota((PAD, 128), 1) // HEAD_DIM
        b.masks[head] = jnp.where(lane == head, 1.0, 0.0).astype(BF)
    for head in range(FOLD):
        lane = iota((PAD, 128), 1) // HEAD_DIM % FOLD
        b.masks_half[head] = jnp.where(lane == head, 1.0, 0.0).astype(BF)
    for layer in range(2):
        b.qkv_t[layer] = b.w_qkv[layer].T
        b.out_t[layer] = b.w_out[layer].T
        b.up_t[layer] = b.w_up[layer].T
        b.down_t[layer] = b.w_down[layer].T
    for ref in (b.d_qkv, b.d_out, b.d_up, b.d_down, b.d_gain, b.d_bias, b.d_b_up, b.d_b_down, b.d_mask, b.d_pos):
        ref[...] = jnp.zeros(ref.shape, F32)

    def gather(dev, carry):
        pos, lens = carry
        return (
            pos + b.recv[dev * block + cap].astype(F32),
            lens + b.recv[dev * block + cap + 1].astype(F32),
        )

    empty = jnp.zeros((groups, 128), F32)
    recv_copy.wait()
    pos, lens = lax.fori_loop(0, count, gather, (empty, empty))
    for group in range(groups):
        where = pl.ds(group * 128, 128)
        b.pos_row[group] = pos[group : group + 1]
        b.pos_col[where] = jnp.broadcast_to(pos[group : group + 1], (128, 128)).T
        b.len_col[where] = jnp.broadcast_to(lens[group : group + 1], (128, 128)).T

    encoders = [Encoder(b, base, ENC_ROWS) for base in range(0, pixels * VIS, ENC_ROWS)]
    weave(encoders[0].attend())
    for now, later in zip(encoders, encoders[1:]):
        weave(now.bend(), later.attend())
    cot_copy.wait()
    decoder_all(b, groups, encoders[-1].bend(), encoders[0].feed())
    for now, later in zip(encoders, encoders[1:]):
        weave(now.retreat(), later.feed())
    weave(encoders[-1].retreat())
    copies = []
    size = b.back.shape[0] // outs
    for index, ref in enumerate(b.back_out):
        copies.append(pltpu.make_async_copy(b.back.at[pl.ds(index * size, size)], ref, b.sems.at[5 + index]))
        copies[-1].start()

    offset = 0
    for layer in range(2):
        for start in range(0, 384, 128):
            b.grads[offset : offset + 128] = b.d_qkv[layer, :, start : start + 128].astype(BF)
            offset += 128
        b.grads[offset : offset + 128] = b.d_out[layer].astype(BF)
        offset += 128
        for start in range(0, 512, 128):
            b.grads[offset : offset + 128] = b.d_up[layer, :, start : start + 128].astype(BF)
            offset += 128
        for start in range(0, 512, 128):
            b.grads[offset : offset + 128] = b.d_down[layer, :, start : start + 128].T.astype(BF)
            offset += 128

    def total(ref, index):
        return jnp.sum(ref[index], axis=0, keepdims=True)

    small = [total(b.d_gain, i) for i in range(4)] + [total(b.d_bias, i) for i in range(4)]
    for layer in range(2):
        row = total(b.d_b_up, layer)
        small += [row[:, start : start + 128] for start in range(0, 512, 128)]
    small += [total(b.d_b_down, layer) for layer in range(2)]
    small.append(jnp.sum(b.d_mask[...], axis=0, keepdims=True))
    small.append(b.d_pos[...])
    tail = jnp.concatenate(small, axis=0)
    fill = -tail.shape[0] % 16
    tail = jnp.concatenate([tail, jnp.zeros((fill, 128), F32)], axis=0)
    b.grads[offset : offset + tail.shape[0]] = tail.astype(BF)
    half = b.grads.shape[0] // 2
    mine = b.core[0]
    for side, ref, sem in ((mine, b.keep, 3), (1 - mine, b.send, 4)):
        rows = pl.ds(pl.multiple_of(side * half, half), half)
        copies.append(pltpu.make_async_copy(b.grads.at[rows], ref, b.sems.at[sem]))
        copies[-1].start()
    for copy in copies:
        copy.wait()
    pltpu.make_async_copy(b.dec, b.dec_out, b.sems.at[1]).wait()


def decoder_scratch(rows, slots):
    return {
        "hot": ((rows, 128), BF),
        "unseen": ((rows, 128), F32),
        "x": ((rows, 128), F32),
        "g": ((rows, 128), F32),
        "gl": ((rows, 128), BF),
        "hat1": ((rows, 128), F32),
        "inv1": ((rows, 128), F32),
        "n1": ((rows, 128), BF),
        "q": ((GROUP, PAD, 128), BF),
        "k": ((GROUP, 2 * slots, 128), BF),
        "v": ((GROUP, 2 * slots, 128), BF),
        "probs": ((GROUP, 2 * slots, 128), F32),
        "att32": ((rows, 128), F32),
        "att": ((rows, 128), BF),
        "hat2": ((rows, 128), F32),
        "inv2": ((rows, 128), F32),
        "n2": ((rows, 128), BF),
        "act": ((rows, 512), BF),
        "slope": ((rows, 512), F32),
        "gh": ((rows, 512), BF),
        "gn2": ((rows, 128), F32),
        "gqkv32": ((rows, 384), F32),
        "gqkv": ((rows, 384), BF),
    }


def main_call(args, cap, extra, count, grad_rows, outs):
    recv, cot = args[4], args[5]
    pixels, slots, width = cot.shape
    enc = pixels * VIS
    rows = GROUP * slots
    smem = pl.BlockSpec(memory_space=pltpu.SMEM)
    vmem = pl.BlockSpec(memory_space=pltpu.VMEM)
    anywhere = pl.BlockSpec(memory_space=pl.ANY)
    scratch = {
        "recv": (recv.shape, BF),
        "cot": (cot.shape, BF),
        "dec": (cot.shape, F32),
        "back": ((count * cap, VIS, width), BF),
        "grads": ((grad_rows, 128), BF),
        "masks": ((HEADS, PAD, 128), BF),
        "masks_half": ((FOLD, PAD, 128), BF),
        "qkv_t": ((2, 384, 128), BF),
        "out_t": ((2, 128, 128), BF),
        "up_t": ((2, 512, 128), BF),
        "down_t": ((2, 128, 512), BF),
        "d_qkv": ((2, 128, 384), F32),
        "d_out": ((2, 128, 128), F32),
        "d_up": ((2, 128, 512), F32),
        "d_down": ((2, 128, 512), F32),
        "d_gain": ((4, 8, 128), F32),
        "d_bias": ((4, 8, 128), F32),
        "d_b_up": ((2, 8, 512), F32),
        "d_b_down": ((2, 8, 128), F32),
        "d_mask": ((8, 128), F32),
        "d_pos": ((slots, 128), F32),
        "pos_row": ((pixels // GROUP, 1, 128), F32),
        "pos_col": ((enc, 128), F32),
        "len_col": ((enc, 128), F32),
        "sent": ((enc, 128), BF),
        "g_sent": ((enc, 128), BF),
        "e_x": ((enc, 128), F32),
        "e_hat1": ((enc, 128), F32),
        "e_inv1": ((enc, 128), F32),
        "e_n1": ((enc, 128), BF),
        "e_qkv": ((enc, 384), BF),
        "e_probs": ((enc, 128), F32),
        "e_att": ((enc, 128), BF),
        "e_hat2": ((enc, 128), F32),
        "e_inv2": ((enc, 128), F32),
        "e_n2": ((enc, 128), BF),
        "e_act": ((enc, 512), BF),
        "e_slope": ((enc, 512), F32),
        "e_gh": ((enc, 512), BF),
        "e_gn2": ((enc, 128), F32),
        "e_gm": ((enc, 128), F32),
        "e_gml": ((enc, 128), BF),
        "e_gqkv": ((enc, 384), BF),
    }
    for side in range(2):
        for name, entry in decoder_scratch(rows, slots).items():
            scratch[f"{name}@{side}"] = entry
    names = IN_NAMES + OUT_NAMES + tuple(scratch) + ("sems",)
    half = jax.ShapeDtypeStruct((grad_rows // 2, 128), BF)
    return pl.pallas_call(
        functools.partial(main_kernel, names, cap, extra, count, outs),
        out_shape=(jax.ShapeDtypeStruct((pixels, slots, width), F32), half, half)
        + (jax.ShapeDtypeStruct((count * cap // outs, VIS, width), BF),) * outs,
        in_specs=[smem] * 4 + [anywhere] * 2 + [vmem] * (len(IN_NAMES) - 6),
        out_specs=(anywhere,) * (3 + outs),
        scratch_shapes=[pltpu.VMEM(shape, kind) for shape, kind in scratch.values()]
        + [pltpu.SemaphoreType.DMA((5 + outs,))],
        compiler_params=pltpu.CompilerParams(vmem_limit_bytes=32 * MIB),
        name="layers",
    )(*args)


def fetch(pairs, sems):
    copies = [pltpu.make_async_copy(src, dst, sems.at[index]) for index, (src, dst) in enumerate(pairs)]
    for copy in copies:
        copy.start()
    return copies


def pair_sum_kernel(mine_ref, theirs_ref, out_ref, mine, theirs, sems):
    for copy in fetch([(mine_ref, mine), (theirs_ref, theirs)], sems):
        copy.wait()
    out_ref[...] = (mine[...].astype(F32) + theirs[...].astype(F32)).astype(BF)


def chunk_sum_kernel(parts_ref, out_ref, parts, low, sems):
    count = parts_ref.shape[0]
    (copy,) = fetch([(parts_ref, parts)], sems)
    copy.wait()
    total = parts[0].astype(F32)
    for part in range(1, count):
        total = total + parts[part].astype(F32)
    low[...] = total.astype(BF)
    for copy in fetch([(low, out_ref.at[part]) for part in range(count)], sems):
        copy.wait()


BIG = ("qkv", "out", "up", "down")


def unpack_kernel(slots, *refs):
    (core_ref, mine_ref, theirs_ref, gain_ref, bias_ref, b_up_ref, b_down_ref, mask_ref, pos_ref) = refs[:9]
    outs = dict(zip(BIG, refs[9:13]))
    held = dict(zip(BIG, refs[13:17]))
    full, sems = refs[17:]
    core = core_ref[0]
    for copy in fetch([(mine_ref, full.at[core]), (theirs_ref, full.at[1 - core])], sems):
        copy.wait()
    half = full.shape[1]

    def rows(start, size):
        side, at = start // half, start % half
        if at + size <= half:
            return full[side, at : at + size].astype(F32)
        cut = half - at
        return jnp.concatenate(
            [full[side, at:half].astype(F32), full[side + 1, 0 : size - cut].astype(F32)], axis=0
        )

    offset = 0
    copies = []

    def leave(name, layer):
        copy = pltpu.make_async_copy(held[name].at[layer], outs[name].at[layer], sems.at[2 + len(copies)])
        copy.start()
        copies.append(copy)

    for layer in range(2):
        for start in range(0, 384, 128):
            held["qkv"][layer, :, start : start + 128] = rows(offset, 128)
            offset += 128
        leave("qkv", layer)
        held["out"][layer] = rows(offset, 128)
        offset += 128
        leave("out", layer)
        for start in range(0, 512, 128):
            held["up"][layer, :, start : start + 128] = rows(offset, 128)
            offset += 128
        leave("up", layer)
        for start in range(0, 512, 128):
            held["down"][layer, start : start + 128, :] = rows(offset, 128)
            offset += 128
        leave("down", layer)
    count = small_rows(slots)
    small = rows(offset, count + (-count % 16))
    gain_ref[...] = small[0:4]
    bias_ref[...] = small[4:8]
    for layer in range(2):
        for part in range(4):
            at = 8 + 4 * layer + part
            b_up_ref[layer : layer + 1, part * 128 : (part + 1) * 128] = small[at : at + 1]
    b_down_ref[...] = small[16:18]
    mask_ref[...] = small[18:19]
    pos_ref[...] = small[19 : 19 + slots]
    for copy in copies:
        copy.wait()


def restore_kernel(cap, count, place_ref, pos_ref, *refs):
    blocks, (out_ref, rows, held, out, sems) = refs[:count], refs[count:]
    size = rows.shape[0] // count
    copies = fetch([(ref, rows.at[pl.ds(index * size, size)]) for index, ref in enumerate(blocks)], sems)
    groups = pos_ref.shape[0]
    wide = out.shape[0] // groups
    slots = wide // GROUP
    lane = iota((1, 128), 1)
    for copy in copies:
        copy.wait()
    for group in range(groups):
        for member in range(GROUP):
            block = rows[place_ref[group * GROUP + member]]
            held[pl.ds((group % 2) * 128 + member * VIS, VIS)] = block.astype(F32)
        pos_row = pos_ref[group : group + 1]
        target = jnp.where(pos_row > 0, (lane // VIS * slots).astype(F32) + pos_row - 1.0, -1.0)
        hot = jnp.where(iota((wide, 128), 0).astype(F32) == target, 1.0, 0.0).astype(BF)
        where = pl.ds(group * wide, wide)
        out[where] = nn(hot, held[pl.ds((group % 2) * 128, 128)].astype(BF))
        pltpu.make_async_copy(out.at[where], out_ref.at[where], sems.at[count]).start()
    pltpu.make_async_copy(out, out_ref, sems.at[count]).wait()


def shards(
    tokens, lengths, masked, route_dev, route_slot, norm_gain, norm_bias, w_qkv, w_out, w_up, b_up, w_down,
    b_down, mask_token, pos_table, cotangent,
):
    count = lax.axis_size("pix")
    reps = lax.axis_size("rep")
    devices = count * reps
    pixels, slots, width = tokens.shape
    cap = max(2, (2 * pixels + count - 1) // count)
    extra = 2
    smem = pl.BlockSpec(memory_space=pltpu.SMEM)
    vmem = pl.BlockSpec(memory_space=pltpu.VMEM)
    anywhere = pl.BlockSpec(memory_space=pl.ANY)
    pix = lax.axis_index("pix")
    me = pix.reshape(1).astype(jnp.int32)
    flat = pix * reps + lax.axis_index("rep")
    core = (flat % 2).reshape(1).astype(jnp.int32)
    payload, pos_rows, take, back_at = prep(tokens, lengths, masked, route_dev, count, cap, extra, me)
    block = cap + extra
    recv = lax.all_to_all(
        payload.reshape(count, block, VIS, width), "pix", split_axis=0, concat_axis=0, tiled=True
    ).reshape(count * block, VIS, width)
    chunk = -(-(3072 + small_rows(slots)) // devices)
    chunk += -chunk % 8
    half = devices // 2
    direct = count <= 8
    dec, keep, send, *back = main_call(
        (
            core, take, back_at, route_slot, recv, cotangent, w_qkv, w_out, w_up, w_down, b_up, b_down,
            norm_gain.reshape(4, width), norm_bias.reshape(4, width), mask_token.reshape(1, width), pos_table,
        ),
        cap,
        extra,
        count,
        devices * chunk,
        count if direct else 1,
    )
    axes = ("pix", "rep")
    swap = [(i, i ^ 1) for i in range(devices)]
    groups = [[2 * i + side for i in range(half)] for side in range(2)]

    def exchange(values):
        return lax.all_to_all(
            values, axes, split_axis=0, concat_axis=0, axis_index_groups=groups, tiled=True
        )

    theirs = lax.ppermute(send, axes, swap)
    piece = jax.ShapeDtypeStruct((half, chunk, 128), BF)
    line = pltpu.VMEM((half, chunk, 128), BF)
    paired = pl.pallas_call(
        pair_sum_kernel,
        out_shape=piece,
        in_specs=[anywhere, anywhere],
        out_specs=vmem,
        scratch_shapes=[line, line, pltpu.SemaphoreType.DMA((2,))],
        compiler_params=pltpu.CompilerParams(vmem_limit_bytes=4 * MIB),
        name="pair_sum",
    )(keep.reshape(half, chunk, 128), theirs.reshape(half, chunk, 128))
    if direct:
        returned = back[:1]
        for step in range(1, count):
            returned.append(lax.ppermute(back[step], "pix", [(i, (i - step) % count) for i in range(count)]))
    else:
        turn = (pix - jnp.arange(count)) % count
        blocks = lax.all_to_all(
            back[0].reshape(count, cap, VIS, width)[turn], "pix", split_axis=0, concat_axis=0, tiled=True
        )
        returned = [blocks[(pix + jnp.arange(count)) % count].reshape(count * cap, VIS, width)]
    spread = pl.pallas_call(
        chunk_sum_kernel,
        out_shape=piece,
        in_specs=[anywhere],
        out_specs=anywhere,
        scratch_shapes=[line, pltpu.VMEM((chunk, 128), BF), pltpu.SemaphoreType.DMA((half,))],
        compiler_params=pltpu.CompilerParams(vmem_limit_bytes=4 * MIB),
        name="chunk_sum",
    )(exchange(paired))
    spread, *returned = lax.optimization_barrier((spread, *returned))
    summed = exchange(spread).reshape(half * chunk, 128)
    other = lax.ppermute(summed, axes, swap)
    small = ((4, width), (4, width), b_up.shape, b_down.shape, (1, width), pos_table.shape)
    large = tuple(w.shape for w in (w_qkv, w_out, w_up, w_down))
    gain, bias, bup, bdown, mask, pos, qkv, out, up, down = pl.pallas_call(
        functools.partial(unpack_kernel, slots),
        out_shape=tuple(jax.ShapeDtypeStruct(shape, F32) for shape in small + large),
        in_specs=[smem, anywhere, anywhere],
        out_specs=(vmem,) * 6 + (anywhere,) * 4,
        scratch_shapes=[pltpu.VMEM(shape, F32) for shape in large]
        + [pltpu.VMEM((2, half * chunk, 128), BF), pltpu.SemaphoreType.DMA((10,))],
        compiler_params=pltpu.CompilerParams(vmem_limit_bytes=8 * MIB),
        name="unpack",
    )(core, summed, other)
    grad_tokens = pl.pallas_call(
        functools.partial(restore_kernel, cap, len(returned)),
        out_shape=jax.ShapeDtypeStruct((pixels * slots, width), F32),
        in_specs=[smem, vmem] + [anywhere] * len(returned),
        out_specs=anywhere,
        scratch_shapes=[
            pltpu.VMEM((count * cap, VIS, width), BF),
            pltpu.VMEM((2 * GROUP * VIS, width), F32),
            pltpu.VMEM((pixels * slots, width), F32),
            pltpu.SemaphoreType.DMA((len(returned) + 1,)),
        ],
        compiler_params=pltpu.CompilerParams(vmem_limit_bytes=8 * MIB),
        name="restore",
    )(back_at, pos_rows, *returned)
    return (
        dec,
        grad_tokens.reshape(pixels, slots, width),
        gain.reshape(norm_gain.shape),
        bias.reshape(norm_bias.shape),
        qkv,
        out,
        up,
        bup,
        down,
        bdown,
        mask.reshape(width),
        pos,
    )


def solution(mesh):
    rows = P(("pix", "rep"))
    in_specs = (rows,) * 5 + (P(),) * 10 + (rows,)
    out_specs = (rows, rows) + (P(),) * 10
    return jax.shard_map(shards, mesh=mesh, in_specs=in_specs, out_specs=out_specs, check_vma=False)
```

```python
import functools

import jax
import jax.numpy as jnp
from jax import lax
from jax.experimental import pallas as pl
from jax.experimental.pallas import tpu as pltpu
from jax.sharding import PartitionSpec as P

HEADS = 8
HEAD_DIM = 16
FOLD = 4
BATCH = 16
PAIRS = 16
ENC_ROWS = 256
SETS = 2
PLACES = (0.0, 1.0, 2.0, 3.0, 4.0)
VIS = 8
GROUP = 16
PAD = 32
CHUNK = 48
EPS = 1e-05
NEG = -1e30
BF = jnp.bfloat16
F32 = jnp.float32
MIB = 1024 * 1024


def nn(left, right):
    return jnp.dot(left, right, preferred_element_type=F32)


def nt(left, right):
    return lax.dot_general(left, right, (((1,), (1,)), ((), ())), preferred_element_type=F32)


def tn(left, right):
    return lax.dot_general(left, right, (((0,), (0,)), ((), ())), preferred_element_type=F32)


def iota(shape, dim):
    return lax.broadcasted_iota(jnp.int32, shape, dim)


def fold_rows(values):
    rows = values.shape[0]
    return jnp.sum(values.reshape(rows // 8, 8, values.shape[1]), axis=0)


def erf_parts(hidden):
    size = jnp.abs(hidden)
    base = 1.0 + size * (0.3275911 * 0.7071067811865476)
    t = 1.0 / base
    bell = jnp.exp2(hidden * hidden * (-0.5 * 1.4426950408889634))
    poly = t * (
        0.5 * 0.254829592
        + t * (0.5 * -0.284496736 + t * (0.5 * 1.421413741 + t * (0.5 * -1.453152027 + t * (0.5 * 1.061405429))))
    )
    tail = poly * bell
    return jnp.where(hidden >= 0, 1.0 - tail, tail), bell


def expand(rows, masks):
    count = rows.shape[0]
    return jnp.concatenate([rows * masks[h, :count, :] for h in range(HEADS)], axis=0)


def fold_heads(rows, step, count):
    lane = iota((count, 128), 1)
    picked = rows[0:count]
    for head in range(1, HEADS):
        picked = jnp.where(lane >= head * HEAD_DIM, rows[head * step : head * step + count], picked)
    return picked


def fold_halves(rows, step, count):
    lane = iota((count, 128), 1) // HEAD_DIM % FOLD
    picked = rows[0:count]
    for head in range(1, FOLD):
        picked = jnp.where(lane == head, rows[head * step : head * step + count], picked)
    return picked


def expand_halves(rows, masks):
    return jnp.concatenate([rows * masks[h] for h in range(FOLD)], axis=0)


def stack_halves(values):
    low = iota(values.shape, 1) < 64
    return jnp.concatenate([jnp.where(low, values, 0.0), jnp.where(low, 0.0, values)], axis=0).astype(BF)


def join_halves(values):
    count = values.shape[0] // 2
    return jnp.where(iota((count, 128), 1) < 64, values[:count], values[count:])


def both_diagonals(values, rows):
    return values[:rows, :128], values[rows:, 128:]


def block_diagonal(first, second):
    low = jnp.concatenate([first, jnp.zeros_like(first)], axis=1)
    return jnp.concatenate([low, jnp.concatenate([jnp.zeros_like(second), second], axis=1)], axis=0)


def pair_nt(rows, columns):
    full = nt(jnp.concatenate(rows, axis=0), jnp.concatenate(columns, axis=0))
    return both_diagonals(full, rows[0].shape[0])


def pair_nn(rows, columns):
    full = nn(jnp.concatenate(rows, axis=0), jnp.concatenate(columns, axis=1))
    return both_diagonals(full, rows[0].shape[0])


def pair_tn(rows, columns):
    full = tn(jnp.concatenate(rows, axis=0), block_diagonal(*columns))
    return full[:, :128], full[:, 128:]


def with_bias(rows, grad):
    full = nn(jnp.concatenate([rows.T, jnp.ones((16, rows.shape[0]), BF)], axis=0), grad)
    return full[:-16], full[-8:]


def softmax_halves(scores, keep):
    count = scores.shape[0] // 2
    scores = jnp.where(keep[None], scores.reshape(2, count, 128), NEG)
    powers = jnp.exp(scores - jnp.max(scores, axis=1, keepdims=True))
    probs = powers * (1.0 / jnp.sum(powers, axis=1, keepdims=True))
    return probs.reshape(2 * count, 128)


def soft_bwd_halves(probs, grad):
    count = probs.shape[0] // 2
    both = (grad * probs).reshape(2, count, 128)
    lean = jnp.sum(both, axis=1, keepdims=True)
    return (probs.reshape(2, count, 128) * (grad.reshape(2, count, 128) - lean)).reshape(2 * count, 128).astype(BF)


def ln_fwd(values, gain, bias, hat, inv, low, where):
    centred = values - jnp.mean(values, axis=-1, keepdims=True)
    scale = lax.rsqrt(jnp.mean(centred * centred, axis=-1, keepdims=True) + EPS)
    unit = centred * scale
    hat[where] = unit
    inv[where] = jnp.broadcast_to(scale, unit.shape)
    low[where] = (unit * gain + bias).astype(BF)


def ln_bwd(grad, gain, hat, inv, where):
    unit = hat[where]
    inner = grad * gain
    lean = jnp.sum(inner, axis=-1, keepdims=True)
    tilt = jnp.sum(inner * unit, axis=-1, keepdims=True)
    return inv[where] * (inner - (lean + unit * tilt) * (1.0 / unit.shape[-1])), fold_rows(grad * unit), fold_rows(grad)


def prep_kernel(
    cap, extra, count, me_ref, dest_ref, tokens_ref, len_ref, masked_ref, dest_row_ref,
    payload_ref, pos_ref, take_ref, back_ref, tally,
):
    slots, pixels = masked_ref.shape
    groups = pixels // GROUP
    block = cap + extra
    wide = GROUP * slots
    lanes = GROUP * VIS
    lens = len_ref[...].astype(F32)
    seen = (masked_ref[...] == 0) & (iota((slots, pixels), 0).astype(F32) < lens)
    seen_low = jnp.where(seen, 1.0, 0.0).astype(BF)
    earlier = jnp.where(iota((slots, slots), 1) < iota((slots, slots), 0), 1.0, 0.0).astype(BF)
    member = iota((slots, pixels), 1) % GROUP
    code = jnp.where(seen, nn(earlier, seen_low) + (member * VIS).astype(F32), -1.0)
    spread = jnp.where(iota((slots, wide), 0) == iota((slots, wide), 1) % slots, 1.0, 0.0).astype(BF)
    code_wide = tn(code.astype(BF), spread)
    own = iota((pixels, wide), 0) % GROUP == iota((pixels, wide), 1) // slots
    code_row = jnp.sum(jnp.where(own, code_wide, 0.0).reshape(groups, GROUP, wide), axis=1)
    in_group = iota((groups, pixels), 1) // GROUP == iota((groups, pixels), 0)
    fan = iota((pixels, lanes), 0) % GROUP == iota((pixels, lanes), 1) // VIS
    fan = jnp.where(fan, 1.0, 0.0).astype(BF)
    len_rows = nn(jnp.where(in_group, lens, 0.0).astype(BF), fan)
    dest_rows = nn(jnp.where(in_group, dest_row_ref[...].astype(F32), 0.0).astype(BF), fan)
    me = me_ref[0]
    for dev in range(count):
        tally[dev] = 0
    order = iota((lanes, wide), 0).astype(F32)
    steps = (iota((GROUP, wide), 1) % slots + 1).astype(F32).astype(BF)
    found = []
    for group in range(groups):
        select = jnp.where(order == code_row[group : group + 1, :], 1.0, 0.0).astype(BF)
        rows = nn(select, tokens_ref[group * wide : (group + 1) * wide, :]).reshape(GROUP, VIS, 128)
        found.append(nt(steps, select)[0:1, :])
        for member_id in range(GROUP):
            series = group * GROUP + member_id
            dest = dest_ref[series]
            rank = tally[dest]
            tally[dest] = rank + 1
            sender = lax.rem(2 * me - dest + 2 * count, count)
            take_ref[series] = sender * block + rank
            back_ref[series] = lax.rem(dest - me + count, count) * cap + rank
            payload_ref[dest * block + rank] = rows[member_id].astype(BF)
    pos_rows = jnp.concatenate(found, axis=0)
    pos_ref[...] = pos_rows

    def label(dev, carry):
        mine = dest_rows == dev.astype(F32)
        payload_ref[dev * block + cap] = jnp.where(mine, pos_rows, 0.0).astype(BF)
        payload_ref[dev * block + cap + 1] = jnp.where(mine, len_rows, 0.0).astype(BF)
        return carry

    lax.fori_loop(0, count, label, 0)


def prep(tokens, lengths, masked, route_dev, count, cap, extra, me):
    pixels, slots, width = tokens.shape
    smem = pl.BlockSpec(memory_space=pltpu.SMEM)
    vmem = pl.BlockSpec(memory_space=pltpu.VMEM)
    index = jax.ShapeDtypeStruct((pixels,), jnp.int32)
    return pl.pallas_call(
        functools.partial(prep_kernel, cap, extra, count),
        out_shape=(
            jax.ShapeDtypeStruct((count * (cap + extra), VIS, width), BF),
            jax.ShapeDtypeStruct((pixels // GROUP, GROUP * VIS), F32),
            index,
            index,
        ),
        in_specs=[smem, smem, vmem, vmem, vmem, vmem],
        out_specs=(vmem, vmem, smem, smem),
        scratch_shapes=[pltpu.SMEM((count,), jnp.int32)],
        compiler_params=pltpu.CompilerParams(vmem_limit_bytes=6 * MIB),
        name="prep",
    )(
        me, route_dev, tokens.reshape(pixels * slots, width), lengths.reshape(1, pixels), masked.T,
        route_dev.reshape(1, pixels),
    )


class Box:
    pass


def gelu_stage(hidden, b_up, act, slope, base, rows):
    for start in range(0, rows, 16):
        value = hidden[start : start + 16] + b_up
        cdf, bell = erf_parts(value)
        where = pl.ds(base + start, 16)
        act[where] = (value * cdf).astype(BF)
        slope[where] = cdf + value * bell * 0.3989422804014327


def slope_stage(grad_act, slope, out, base, rows):
    total = None
    for start in range(0, rows, 16):
        part = (grad_act[start : start + 16] * slope[pl.ds(base + start, 16)]).astype(BF)
        out[pl.ds(start, 16)] = part
        summed = fold_rows(part.astype(F32))
        total = summed if total is None else total + summed
    return total


def softmax_rows(scores, keep):
    scores = jnp.where(keep, scores, NEG)
    powers = jnp.exp(scores - jnp.max(scores, axis=0, keepdims=True))
    return powers / jnp.sum(powers, axis=0, keepdims=True)


def soft_bwd(probs, grad):
    return (probs * (grad - jnp.sum(grad * probs, axis=0, keepdims=True))).astype(BF)


class Encoder:
    def __init__(self, b, base, rows):
        self.b, self.base, self.rows = b, base, rows
        self.whole = slice(base, base + rows)

    def chunks(self):
        return [slice(start, start + 32) for start in range(self.base, self.base + self.rows, 32)]

    def part(self, values, where):
        return values[where.start - self.base : where.stop - self.base]

    def attend(self):
        b, w, whole = self.b, self.b.w, self.whole
        v = Box()
        same = iota((16, 128), 0) // VIS == (iota((16, 128), 1) % 16) // VIS

        def load(series):
            b.e_x[series * VIS : (series + 1) * VIS] = b.recv[b.take[series]].astype(F32)

        steps = [functools.partial(load, series) for series in range(self.base // VIS, (self.base + self.rows) // VIS)]

        def norm(where):
            ln_fwd(b.e_x[where], w.gain[0:1], w.bias[0:1], b.e_hat1, b.e_inv1, b.e_n1, where)

        steps += [functools.partial(norm, where) for where in self.chunks()]

        def project():
            v.qkv = nn(b.e_n1[whole], w.qkv[0])
            v.score, v.prob, v.mixed = {}, {}, {}

        steps.append(project)

        def split(where):
            part = self.part(v.qkv, where)
            b.e_qkv[where, 0:128] = (part[:, 0:128] * 0.25).astype(BF)
            b.e_qkv[where, 128:384] = part[:, 128:384].astype(BF)

        steps += [functools.partial(split, where) for where in self.chunks()]

        def score(at):
            pair = (at, at + 16)
            queries = [expand(b.e_qkv[one : one + 16, 0:128], b.masks) for one in pair]
            keys = [b.e_qkv[one : one + 16, 128:256] for one in pair]
            v.score[at], v.score[at + 16] = pair_nt(keys, queries)

        def soft(at):
            v.prob[at] = softmax_rows(v.score[at], same & (b.pos_col[at : at + 16] > 0))
            b.e_probs[at : at + 16] = v.prob[at]

        def mix(at):
            pair = (at, at + 16)
            values = [b.e_qkv[one : one + 16, 256:384] for one in pair]
            v.mixed[at], v.mixed[at + 16] = pair_tn([v.prob[one].astype(BF) for one in pair], values)

        def gather(at):
            b.e_att[at : at + 16] = fold_heads(v.mixed[at], 16, 16).astype(BF)

        for first in range(self.base, self.base + self.rows, 16 * PAIRS):
            for stage, stride in ((score, 32), (soft, 16), (mix, 32), (gather, 16)):
                steps += [functools.partial(stage, at) for at in range(first, first + 16 * PAIRS, stride)]

        def out():
            v.proj = nn(b.e_att[whole], w.out[0])

        steps.append(out)

        def second(where):
            middle = b.e_x[where] + self.part(v.proj, where)
            b.e_x[where] = middle
            ln_fwd(middle, w.gain[1:2], w.bias[1:2], b.e_hat2, b.e_inv2, b.e_n2, where)

        steps += [functools.partial(second, where) for where in self.chunks()]
        return steps

    def bend(self):
        b, w, whole = self.b, self.b.w, self.whole
        v = Box()

        def up():
            v.hidden = nn(b.e_n2[whole], w.up[0])

        def curve(start):
            value = v.hidden[start : start + 16] + w.b_up[0:1]
            cdf, bell = erf_parts(value)
            where = slice(self.base + start, self.base + start + 16)
            b.e_act[where] = (value * cdf).astype(BF)
            b.e_slope[where] = cdf + value * bell * 0.3989422804014327

        def down():
            v.down = nn(b.e_act[whole], w.down[0])

        def finish(where):
            b.sent[where] = (b.e_x[where] + self.part(v.down, where) + w.b_down[0:1]).astype(BF)

        return (
            [up]
            + [functools.partial(curve, start) for start in range(0, self.rows, 16)]
            + [down]
            + [functools.partial(finish, where) for where in self.chunks()]
        )

    def feed(self):
        b, whole = self.b, self.whole
        v = Box()

        def back():
            grad_low = b.g_sent[whole]
            b.d_down[0] += tn(grad_low, b.e_act[whole])
            b.d_b_down[0] += fold_rows(grad_low.astype(F32))
            v.grad_act = nn(grad_low, b.down_t[0])

        def unbend(start):
            where = slice(self.base + start, self.base + start + 16)
            b.e_gh[where] = (v.grad_act[start : start + 16] * b.e_slope[where]).astype(BF)

        def end():
            weights, bias = with_bias(b.e_n2[whole], b.e_gh[whole])
            b.d_up[0] += weights
            b.d_b_up[0] += bias
            b.e_gn2[whole] = nn(b.e_gh[whole], b.up_t[0])

        return [back] + [functools.partial(unbend, start) for start in range(0, self.rows, 16)] + [end]

    def retreat(self):
        b, w, whole = self.b, self.b.w, self.whole
        v = Box()

        def norm(where):
            grad, gain_part, bias_part = ln_bwd(b.e_gn2[where], w.gain[1:2], b.e_hat2, b.e_inv2, where)
            b.d_gain[1] += gain_part
            b.d_bias[1] += bias_part
            grad = grad + b.g_sent[where].astype(F32)
            b.e_gm[where] = grad
            b.e_gml[where] = grad.astype(BF)

        steps = [functools.partial(norm, where) for where in self.chunks()]

        def out():
            b.d_out[0] += tn(b.e_att[whole], b.e_gml[whole])
            v.grad_att = nn(b.e_gml[whole], b.out_t[0])
            v.grad, v.grad_p, v.grad_s, v.grad_v, v.grad_k, v.grad_q = ({} for _ in range(6))

        steps.append(out)

        def spread(at):
            pair = (at, at + 16)
            for one in pair:
                low = v.grad_att[one - self.base : one - self.base + 16].astype(BF)
                v.grad[one] = expand(low, b.masks)
            values = [b.e_qkv[one : one + 16, 256:384] for one in pair]
            v.grad_p[at], v.grad_p[at + 16] = pair_nt(values, [v.grad[one] for one in pair])

        def values(at):
            pair = (at, at + 16)
            probs = [b.e_probs[one : one + 16].astype(BF) for one in pair]
            v.grad_v[at], v.grad_v[at + 16] = pair_nn(probs, [v.grad[one] for one in pair])

        def soft(at):
            v.grad_s[at] = soft_bwd(b.e_probs[at : at + 16], v.grad_p[at])

        def keys(at):
            pair = (at, at + 16)
            columns = [expand(b.e_qkv[one : one + 16, 0:128], b.masks) for one in pair]
            v.grad_k[at], v.grad_k[at + 16] = pair_nn([v.grad_s[one] for one in pair], columns)

        def queries(at):
            pair = (at, at + 16)
            keys = [b.e_qkv[one : one + 16, 128:256] for one in pair]
            v.grad_q[at], v.grad_q[at + 16] = pair_tn([v.grad_s[one] for one in pair], keys)

        def gather(at):
            b.e_gqkv[at : at + 16, 256:384] = v.grad_v[at].astype(BF)
            b.e_gqkv[at : at + 16, 128:256] = v.grad_k[at].astype(BF)
            b.e_gqkv[at : at + 16, 0:128] = (fold_heads(v.grad_q[at], 16, 16) * 0.25).astype(BF)

        for first in range(self.base, self.base + self.rows, 16 * PAIRS):
            for stage, stride in ((spread, 32), (values, 32), (soft, 16), (keys, 32), (queries, 32), (gather, 16)):
                steps += [functools.partial(stage, at) for at in range(first, first + 16 * PAIRS, stride)]

        def project():
            b.d_qkv[0] += tn(b.e_n1[whole], b.e_gqkv[whole])
            v.grad_n1 = nn(b.e_gqkv[whole], b.qkv_t[0])

        steps.append(project)

        def first_norm(where):
            grad, gain_part, bias_part = ln_bwd(
                self.part(v.grad_n1, where), w.gain[0:1], b.e_hat1, b.e_inv1, where
            )
            b.d_gain[0] += gain_part
            b.d_bias[0] += bias_part
            grad = grad + b.e_gm[where]
            for series in range(where.start // VIS, where.stop // VIS):
                at = series * VIS - where.start
                b.back[b.back_at[series]] = grad[at : at + VIS].astype(BF)

        steps += [functools.partial(first_norm, where) for where in self.chunks()]
        return steps


def weave(timeline):
    order = []
    for which, (start, length, steps) in enumerate(timeline):
        order += [(start + length * (index + 0.5) / len(steps), which, step) for index, step in enumerate(steps)]
    for _, _, step in sorted(order, key=lambda entry: entry[:2]):
        step()


class Decoder:
    def __init__(self, b, d, group):
        self.b, self.d, self.group = b, d, group
        self.slots = b.slots
        self.rows = GROUP * b.slots
        self.sent_rows = pl.ds(pl.multiple_of(group * 128, 128), 128)
        self.zeros = jnp.zeros((PAD - b.slots, 128), F32)
        self.step = iota((b.slots, 128), 0).astype(F32)

    def span(self, member):
        return pl.ds(member * self.slots, self.slots)

    def cut(self, member):
        return slice(member * self.slots, (member + 1) * self.slots)

    def inside(self, member):
        lens = self.b.len_col[pl.ds(pl.multiple_of(self.group * 128, 128) + member * VIS, VIS)]
        return self.step < jnp.concatenate([lens] * (self.slots // VIS), axis=0)

    def padded(self, values):
        return jnp.concatenate([values, self.zeros], axis=0).astype(BF)

    def chunks(self):
        return range(0, self.rows, CHUNK)

    def attend(self):
        b, d, w, slots = self.b, self.d, self.b.w, self.slots
        v = Box()
        steps = []

        def begin():
            pos_row = b.pos_row[self.group]
            lane = iota((1, 128), 1)
            target = jnp.where(pos_row > 0, (lane // VIS * slots).astype(F32) + pos_row - 1.0, -1.0)
            for start in self.chunks():
                spot = (iota((CHUNK, 128), 0) + start).astype(F32)
                d.hot[pl.ds(start, CHUNK)] = jnp.where(spot == target, 1.0, 0.0).astype(BF)
            both = jnp.concatenate([b.sent[self.sent_rows], jnp.ones((128, 128), BF)], axis=1)
            full = nn(d.hot[...], both)
            v.placed, v.shown = full[:, 0:128], full[:, 128:256]

        steps.append(begin)

        def assemble(member):
            at = self.cut(member)
            hidden_part = 1.0 - v.shown[at]
            d.unseen[self.span(member)] = hidden_part
            d.x[self.span(member)] = v.placed[at] + hidden_part * w.mask[...] + w.pos[...]
            cot = b.cot[b.slot[self.group * GROUP + member]].astype(F32)
            d.g[self.span(member)] = jnp.where(self.inside(member), cot, 0.0)

        steps += [functools.partial(assemble, member) for member in range(GROUP)]

        def norm(start):
            where = pl.ds(start, CHUNK)
            ln_fwd(d.x[where], w.gain[2:3], w.bias[2:3], d.hat1, d.inv1, d.n1, where)

        steps += [functools.partial(norm, start) for start in self.chunks()]

        def project():
            v.qkv = nn(d.n1[...], w.qkv[1])
            v.score, v.prob, v.mixed = {}, {}, {}

        steps.append(project)

        def split(member):
            at = self.cut(member)
            d.q[member] = self.padded(v.qkv[at, 0:128] * 0.25)
            d.k[member] = stack_halves(v.qkv[at, 128:256])
            d.v[member] = stack_halves(v.qkv[at, 256:384])

        def score(member):
            pair = (member, member + 1)
            queries = [expand_halves(d.q[one], b.masks_half) for one in pair]
            v.score[member], v.score[member + 1] = pair_nt([d.k[one] for one in pair], queries)

        def soft(member):
            v.prob[member] = softmax_halves(v.score[member], self.inside(member))
            d.probs[member] = v.prob[member]

        def mix(member):
            pair = (member, member + 1)
            mixed = pair_tn([v.prob[one].astype(BF) for one in pair], [d.v[one] for one in pair])
            v.mixed[member], v.mixed[member + 1] = mixed

        def gather(member):
            d.att32[self.span(member)] = fold_halves(v.mixed[member], PAD, slots)

        for first in range(0, GROUP, BATCH):
            for stage, stride in ((split, 1), (score, 2), (soft, 1), (mix, 2), (gather, 1)):
                steps += [functools.partial(stage, member) for member in range(first, first + BATCH, stride)]

        def low(start):
            where = pl.ds(start, CHUNK)
            d.att[where] = d.att32[where].astype(BF)

        steps += [functools.partial(low, start) for start in self.chunks()]

        def out():
            v.proj = nn(d.att[...], w.out[1])

        steps.append(out)

        def second(start):
            where = pl.ds(start, CHUNK)
            middle = d.x[where] + v.proj[start : start + CHUNK]
            d.x[where] = middle
            ln_fwd(middle, w.gain[3:4], w.bias[3:4], d.hat2, d.inv2, d.n2, where)

        steps += [functools.partial(second, start) for start in self.chunks()]
        return steps

    def bend(self):
        b, d, w = self.b, self.d, self.b.w
        v = Box()
        steps = []

        def up():
            v.hidden = nn(d.n2[...], w.up[1])

        steps.append(up)

        def curve(start):
            value = v.hidden[start : start + 16] + w.b_up[1:2]
            cdf, bell = erf_parts(value)
            where = pl.ds(start, 16)
            d.act[where] = (value * cdf).astype(BF)
            d.slope[where] = cdf + value * bell * 0.3989422804014327

        steps += [functools.partial(curve, start) for start in range(0, self.rows, 16)]
        return steps

    def feed(self):
        b, d, w = self.b, self.d, self.b.w
        v = Box()
        steps = []

        def down():
            v.down = nn(d.act[...], w.down[1])

        steps.append(down)

        def finish(member):
            value = d.x[self.span(member)] + v.down[self.cut(member)] + w.b_down[1:2]
            slot = b.slot[self.group * GROUP + member]
            b.dec[slot] = jnp.where(self.inside(member), value, 0.0)
            pltpu.make_async_copy(b.dec.at[slot], b.dec_out.at[slot], b.sems.at[1]).start()

        steps += [functools.partial(finish, member) for member in range(GROUP)]

        def low(start):
            where = pl.ds(start, CHUNK)
            d.gl[where] = d.g[where].astype(BF)

        steps += [functools.partial(low, start) for start in self.chunks()]

        def back():
            b.d_down[1] += tn(d.gl[...], d.act[...])
            b.d_b_down[1] += fold_rows(d.g[...])
            v.grad_act = nn(d.gl[...], b.down_t[1])

        steps.append(back)

        def unbend(start):
            d.gh[pl.ds(start, 16)] = (v.grad_act[start : start + 16] * d.slope[pl.ds(start, 16)]).astype(BF)

        steps += [functools.partial(unbend, start) for start in range(0, self.rows, 16)]

        def end():
            weights, bias = with_bias(d.n2[...], d.gh[...])
            b.d_up[1] += weights
            b.d_b_up[1] += bias
            d.gn2[...] = nn(d.gh[...], b.up_t[1])

        steps.append(end)
        return steps

    def retreat(self):
        b, d, w, slots = self.b, self.d, self.b.w, self.slots
        v = Box()
        steps = []

        def norm(start):
            where = pl.ds(start, CHUNK)
            grad, gain_part, bias_part = ln_bwd(d.gn2[where], w.gain[3:4], d.hat2, d.inv2, where)
            b.d_gain[3] += gain_part
            b.d_bias[3] += bias_part
            grad = grad + d.g[where]
            d.g[where] = grad
            d.gl[where] = grad.astype(BF)

        steps += [functools.partial(norm, start) for start in self.chunks()]

        def out():
            b.d_out[1] += tn(d.att[...], d.gl[...])
            v.grad_att = nn(d.gl[...], b.out_t[1])
            v.grad, v.prob, v.grad_p, v.grad_s, v.grad_v, v.grad_k, v.grad_q = ({} for _ in range(7))

        steps.append(out)

        def spread(member):
            pair = (member, member + 1)
            for one in pair:
                v.grad[one] = expand_halves(self.padded(v.grad_att[self.cut(one)]), b.masks_half)
            grads = [v.grad[one] for one in pair]
            v.grad_p[member], v.grad_p[member + 1] = pair_nt([d.v[one] for one in pair], grads)

        def values(member):
            pair = (member, member + 1)
            probs = [d.probs[one].astype(BF) for one in pair]
            v.grad_v[member], v.grad_v[member + 1] = pair_nn(probs, [v.grad[one] for one in pair])

        def soft(member):
            v.grad_s[member] = soft_bwd_halves(d.probs[member], v.grad_p[member])

        def keys(member):
            pair = (member, member + 1)
            columns = [expand_halves(d.q[one], b.masks_half) for one in pair]
            v.grad_k[member], v.grad_k[member + 1] = pair_nn([v.grad_s[one] for one in pair], columns)

        def queries(member):
            pair = (member, member + 1)
            grads = pair_tn([v.grad_s[one] for one in pair], [d.k[one] for one in pair])
            v.grad_q[member], v.grad_q[member + 1] = grads

        def gather(member):
            d.gqkv32[self.span(member), 256:384] = join_halves(v.grad_v[member])
            d.gqkv32[self.span(member), 128:256] = join_halves(v.grad_k[member])
            d.gqkv32[self.span(member), 0:128] = fold_halves(v.grad_q[member], PAD, slots) * 0.25

        for first in range(0, GROUP, BATCH):
            for stage, stride in ((spread, 2), (values, 2), (soft, 1), (keys, 2), (queries, 2), (gather, 1)):
                steps += [functools.partial(stage, member) for member in range(first, first + BATCH, stride)]

        def low(start):
            where = pl.ds(start, CHUNK)
            d.gqkv[where] = d.gqkv32[where].astype(BF)

        steps += [functools.partial(low, start) for start in self.chunks()]

        def project():
            b.d_qkv[1] += tn(d.n1[...], d.gqkv[...])
            v.grad_n1 = nn(d.gqkv[...], b.qkv_t[1])
            v.pos = None

        steps.append(project)

        def first_norm(start):
            where = pl.ds(start, CHUNK)
            grad, gain_part, bias_part = ln_bwd(
                v.grad_n1[start : start + CHUNK], w.gain[2:3], d.hat1, d.inv1, where
            )
            b.d_gain[2] += gain_part
            b.d_bias[2] += bias_part
            grad = grad + d.g[where]
            d.gl[where] = grad.astype(BF)
            part = jnp.sum(grad.reshape(CHUNK // slots, slots, 128), axis=0)
            v.pos = part if v.pos is None else v.pos + part
            b.d_mask[...] += fold_rows(grad * d.unseen[where])

        steps += [functools.partial(first_norm, start) for start in self.chunks()]

        def end():
            b.d_pos[...] += v.pos
            b.g_sent[self.sent_rows] = tn(d.hot[...], d.gl[...]).astype(BF)

        steps.append(end)
        return steps


def plan(b, groups, encoders, before_first):
    timeline = []
    for index in range(groups):
        decoder = Decoder(b, b.sets[index % SETS], index)
        phases = (decoder.attend, decoder.bend, decoder.feed, decoder.retreat)
        for start, stop, phase in zip(PLACES, PLACES[1:], phases):
            timeline.append((2 * index + start, stop - start, phase()))
    timeline.append((-0.01, 0.01, [before_first]))
    for chunk in encoders:
        first, last = chunk.base // (GROUP * VIS), (chunk.base + chunk.rows) // (GROUP * VIS) - 1
        early = 2 * first - (4 if first else 2)
        room = (2 * first - early) / 2
        timeline.append((early, room, chunk.attend()))
        timeline.append((early + room, room, chunk.bend()))
        late = 2 * last + PLACES[-1]
        room = 2 if last < groups - 1 else 1
        timeline.append((late, room, chunk.feed()))
        timeline.append((late + room, room, chunk.retreat()))
    return timeline


IN_NAMES = (
    "core", "take", "back_at", "slot", "recv_in", "cot_in", "w_qkv", "w_out", "w_up", "w_down", "b_up", "b_down",
    "gain", "bias", "mask", "pos",
)
OUT_NAMES = ("dec_out", "keep", "send")


def small_rows(slots):
    return 18 + 1 + slots


def main_kernel(names, cap, extra, count, outs, *refs):
    b = Box()
    b.sets = tuple(Box() for _ in range(SETS))
    b.back_out = refs[len(IN_NAMES) + len(OUT_NAMES) : len(IN_NAMES) + len(OUT_NAMES) + outs]
    refs = refs[: len(IN_NAMES) + len(OUT_NAMES)] + refs[len(IN_NAMES) + len(OUT_NAMES) + outs :]
    for name, ref in zip(names, refs, strict=True):
        name, _, side = name.partition("@")
        setattr(b.sets[int(side)] if side else b, name, ref)
    b.w = Box()
    for name in ("qkv", "out", "up", "down"):
        setattr(b.w, name, getattr(b, "w_" + name))
    for name in ("b_up", "b_down", "gain", "bias", "mask", "pos"):
        setattr(b.w, name, getattr(b, name))
    b.slots = b.cot.shape[1]
    pixels = b.cot.shape[0]
    groups = pixels // GROUP
    block = cap + extra
    recv_copy = pltpu.make_async_copy(b.recv_in, b.recv, b.sems.at[0])
    recv_copy.start()
    cot_copy = pltpu.make_async_copy(b.cot_in, b.cot, b.sems.at[2])
    cot_copy.start()
    for head in range(HEADS):
        lane = iota((PAD, 128), 1) // HEAD_DIM
        b.masks[head] = jnp.where(lane == head, 1.0, 0.0).astype(BF)
    for head in range(FOLD):
        lane = iota((PAD, 128), 1) // HEAD_DIM % FOLD
        b.masks_half[head] = jnp.where(lane == head, 1.0, 0.0).astype(BF)
    for layer in range(2):
        b.qkv_t[layer] = b.w_qkv[layer].T
        b.out_t[layer] = b.w_out[layer].T
        b.up_t[layer] = b.w_up[layer].T
        b.down_t[layer] = b.w_down[layer].T
    for ref in (b.d_qkv, b.d_out, b.d_up, b.d_down, b.d_gain, b.d_bias, b.d_b_up, b.d_b_down, b.d_mask, b.d_pos):
        ref[...] = jnp.zeros(ref.shape, F32)

    def gather(dev, carry):
        pos, lens = carry
        return (
            pos + b.recv[dev * block + cap].astype(F32),
            lens + b.recv[dev * block + cap + 1].astype(F32),
        )

    empty = jnp.zeros((groups, 128), F32)
    recv_copy.wait()
    pos, lens = lax.fori_loop(0, count, gather, (empty, empty))
    for group in range(groups):
        where = pl.ds(group * 128, 128)
        b.pos_row[group] = pos[group : group + 1]
        b.pos_col[where] = jnp.broadcast_to(pos[group : group + 1], (128, 128)).T
        b.len_col[where] = jnp.broadcast_to(lens[group : group + 1], (128, 128)).T

    encoders = [Encoder(b, base, ENC_ROWS) for base in range(0, pixels * VIS, ENC_ROWS)]
    weave(plan(b, groups, encoders, cot_copy.wait))
    copies = []
    size = b.back.shape[0] // outs
    for index, ref in enumerate(b.back_out):
        copies.append(pltpu.make_async_copy(b.back.at[pl.ds(index * size, size)], ref, b.sems.at[5 + index]))
        copies[-1].start()

    offset = 0
    for layer in range(2):
        for start in range(0, 384, 128):
            b.grads[offset : offset + 128] = b.d_qkv[layer, :, start : start + 128].astype(BF)
            offset += 128
        b.grads[offset : offset + 128] = b.d_out[layer].astype(BF)
        offset += 128
        for start in range(0, 512, 128):
            b.grads[offset : offset + 128] = b.d_up[layer, :, start : start + 128].astype(BF)
            offset += 128
        for start in range(0, 512, 128):
            b.grads[offset : offset + 128] = b.d_down[layer, :, start : start + 128].T.astype(BF)
            offset += 128

    def total(ref, index):
        return jnp.sum(ref[index], axis=0, keepdims=True)

    small = [total(b.d_gain, i) for i in range(4)] + [total(b.d_bias, i) for i in range(4)]
    for layer in range(2):
        row = b.d_b_up[layer, 0:1]
        small += [row[:, start : start + 128] for start in range(0, 512, 128)]
    small += [total(b.d_b_down, layer) for layer in range(2)]
    small.append(jnp.sum(b.d_mask[...], axis=0, keepdims=True))
    small.append(b.d_pos[...])
    tail = jnp.concatenate(small, axis=0)
    fill = -tail.shape[0] % 16
    tail = jnp.concatenate([tail, jnp.zeros((fill, 128), F32)], axis=0)
    b.grads[offset : offset + tail.shape[0]] = tail.astype(BF)
    half = b.grads.shape[0] // 2
    mine = b.core[0]
    for side, ref, sem in ((mine, b.keep, 3), (1 - mine, b.send, 4)):
        rows = pl.ds(pl.multiple_of(side * half, half), half)
        copies.append(pltpu.make_async_copy(b.grads.at[rows], ref, b.sems.at[sem]))
        copies[-1].start()
    for copy in copies:
        copy.wait()
    pltpu.make_async_copy(b.dec, b.dec_out, b.sems.at[1]).wait()


def decoder_scratch(rows, slots):
    return {
        "hot": ((rows, 128), BF),
        "unseen": ((rows, 128), F32),
        "x": ((rows, 128), F32),
        "g": ((rows, 128), F32),
        "gl": ((rows, 128), BF),
        "hat1": ((rows, 128), F32),
        "inv1": ((rows, 128), F32),
        "n1": ((rows, 128), BF),
        "q": ((GROUP, PAD, 128), BF),
        "k": ((GROUP, 2 * slots, 128), BF),
        "v": ((GROUP, 2 * slots, 128), BF),
        "probs": ((GROUP, 2 * slots, 128), F32),
        "att32": ((rows, 128), F32),
        "att": ((rows, 128), BF),
        "hat2": ((rows, 128), F32),
        "inv2": ((rows, 128), F32),
        "n2": ((rows, 128), BF),
        "act": ((rows, 512), BF),
        "slope": ((rows, 512), F32),
        "gh": ((rows, 512), BF),
        "gn2": ((rows, 128), F32),
        "gqkv32": ((rows, 384), F32),
        "gqkv": ((rows, 384), BF),
    }


def main_call(args, cap, extra, count, grad_rows, outs):
    recv, cot = args[4], args[5]
    pixels, slots, width = cot.shape
    enc = pixels * VIS
    rows = GROUP * slots
    smem = pl.BlockSpec(memory_space=pltpu.SMEM)
    vmem = pl.BlockSpec(memory_space=pltpu.VMEM)
    anywhere = pl.BlockSpec(memory_space=pl.ANY)
    scratch = {
        "recv": (recv.shape, BF),
        "cot": (cot.shape, BF),
        "dec": (cot.shape, F32),
        "back": ((count * cap, VIS, width), BF),
        "grads": ((grad_rows, 128), BF),
        "masks": ((HEADS, PAD, 128), BF),
        "masks_half": ((FOLD, PAD, 128), BF),
        "qkv_t": ((2, 384, 128), BF),
        "out_t": ((2, 128, 128), BF),
        "up_t": ((2, 512, 128), BF),
        "down_t": ((2, 128, 512), BF),
        "d_qkv": ((2, 128, 384), F32),
        "d_out": ((2, 128, 128), F32),
        "d_up": ((2, 128, 512), F32),
        "d_down": ((2, 128, 512), F32),
        "d_gain": ((4, 8, 128), F32),
        "d_bias": ((4, 8, 128), F32),
        "d_b_up": ((2, 8, 512), F32),
        "d_b_down": ((2, 8, 128), F32),
        "d_mask": ((8, 128), F32),
        "d_pos": ((slots, 128), F32),
        "pos_row": ((pixels // GROUP, 1, 128), F32),
        "pos_col": ((enc, 128), F32),
        "len_col": ((enc, 128), F32),
        "sent": ((enc, 128), BF),
        "g_sent": ((enc, 128), BF),
        "e_x": ((enc, 128), F32),
        "e_hat1": ((enc, 128), F32),
        "e_inv1": ((enc, 128), F32),
        "e_n1": ((enc, 128), BF),
        "e_qkv": ((enc, 384), BF),
        "e_probs": ((enc, 128), F32),
        "e_att": ((enc, 128), BF),
        "e_hat2": ((enc, 128), F32),
        "e_inv2": ((enc, 128), F32),
        "e_n2": ((enc, 128), BF),
        "e_act": ((enc, 512), BF),
        "e_slope": ((enc, 512), F32),
        "e_gh": ((enc, 512), BF),
        "e_gn2": ((enc, 128), F32),
        "e_gm": ((enc, 128), F32),
        "e_gml": ((enc, 128), BF),
        "e_gqkv": ((enc, 384), BF),
    }
    for side in range(SETS):
        for name, entry in decoder_scratch(rows, slots).items():
            scratch[f"{name}@{side}"] = entry
    names = IN_NAMES + OUT_NAMES + tuple(scratch) + ("sems",)
    half = jax.ShapeDtypeStruct((grad_rows // 2, 128), BF)
    return pl.pallas_call(
        functools.partial(main_kernel, names, cap, extra, count, outs),
        out_shape=(jax.ShapeDtypeStruct((pixels, slots, width), F32), half, half)
        + (jax.ShapeDtypeStruct((count * cap // outs, VIS, width), BF),) * outs,
        in_specs=[smem] * 4 + [anywhere] * 2 + [vmem] * (len(IN_NAMES) - 6),
        out_specs=(anywhere,) * (3 + outs),
        scratch_shapes=[pltpu.VMEM(shape, kind) for shape, kind in scratch.values()]
        + [pltpu.SemaphoreType.DMA((5 + outs,))],
        compiler_params=pltpu.CompilerParams(vmem_limit_bytes=32 * MIB),
        name="layers",
    )(*args)


def fetch(pairs, sems):
    copies = [pltpu.make_async_copy(src, dst, sems.at[index]) for index, (src, dst) in enumerate(pairs)]
    for copy in copies:
        copy.start()
    return copies


def pair_sum_kernel(mine_ref, theirs_ref, out_ref, mine, theirs, sems):
    for copy in fetch([(mine_ref, mine), (theirs_ref, theirs)], sems):
        copy.wait()
    out_ref[...] = (mine[...].astype(F32) + theirs[...].astype(F32)).astype(BF)


def chunk_sum_kernel(parts_ref, out_ref, parts, low, sems):
    count = parts_ref.shape[0]
    (copy,) = fetch([(parts_ref, parts)], sems)
    copy.wait()
    total = parts[0].astype(F32)
    for part in range(1, count):
        total = total + parts[part].astype(F32)
    low[...] = total.astype(BF)
    for copy in fetch([(low, out_ref.at[part]) for part in range(count)], sems):
        copy.wait()


BIG = ("qkv", "out", "up", "down")


def unpack_kernel(slots, *refs):
    (core_ref, mine_ref, theirs_ref, gain_ref, bias_ref, b_up_ref, b_down_ref, mask_ref, pos_ref) = refs[:9]
    outs = dict(zip(BIG, refs[9:13]))
    held = dict(zip(BIG, refs[13:17]))
    full, sems = refs[17:]
    core = core_ref[0]
    for copy in fetch([(mine_ref, full.at[core]), (theirs_ref, full.at[1 - core])], sems):
        copy.wait()
    half = full.shape[1]

    def rows(start, size):
        side, at = start // half, start % half
        if at + size <= half:
            return full[side, at : at + size].astype(F32)
        cut = half - at
        return jnp.concatenate(
            [full[side, at:half].astype(F32), full[side + 1, 0 : size - cut].astype(F32)], axis=0
        )

    offset = 0
    copies = []

    def leave(name, layer):
        copy = pltpu.make_async_copy(held[name].at[layer], outs[name].at[layer], sems.at[2 + len(copies)])
        copy.start()
        copies.append(copy)

    for layer in range(2):
        for start in range(0, 384, 128):
            held["qkv"][layer, :, start : start + 128] = rows(offset, 128)
            offset += 128
        leave("qkv", layer)
        held["out"][layer] = rows(offset, 128)
        offset += 128
        leave("out", layer)
        for start in range(0, 512, 128):
            held["up"][layer, :, start : start + 128] = rows(offset, 128)
            offset += 128
        leave("up", layer)
        for start in range(0, 512, 128):
            held["down"][layer, start : start + 128, :] = rows(offset, 128)
            offset += 128
        leave("down", layer)
    count = small_rows(slots)
    small = rows(offset, count + (-count % 16))
    gain_ref[...] = small[0:4]
    bias_ref[...] = small[4:8]
    for layer in range(2):
        for part in range(4):
            at = 8 + 4 * layer + part
            b_up_ref[layer : layer + 1, part * 128 : (part + 1) * 128] = small[at : at + 1]
    b_down_ref[...] = small[16:18]
    mask_ref[...] = small[18:19]
    pos_ref[...] = small[19 : 19 + slots]
    for copy in copies:
        copy.wait()


def restore_kernel(cap, count, place_ref, pos_ref, *refs):
    blocks, (out_ref, rows, held, out, sems) = refs[:count], refs[count:]
    size = rows.shape[0] // count
    copies = fetch([(ref, rows.at[pl.ds(index * size, size)]) for index, ref in enumerate(blocks)], sems)
    groups = pos_ref.shape[0]
    wide = out.shape[0] // groups
    slots = wide // GROUP
    lane = iota((1, 128), 1)
    for copy in copies:
        copy.wait()
    for group in range(groups):
        for member in range(GROUP):
            block = rows[place_ref[group * GROUP + member]]
            held[pl.ds((group % 2) * 128 + member * VIS, VIS)] = block.astype(F32)
        pos_row = pos_ref[group : group + 1]
        target = jnp.where(pos_row > 0, (lane // VIS * slots).astype(F32) + pos_row - 1.0, -1.0)
        hot = jnp.where(iota((wide, 128), 0).astype(F32) == target, 1.0, 0.0).astype(BF)
        where = pl.ds(group * wide, wide)
        out[where] = nn(hot, held[pl.ds((group % 2) * 128, 128)].astype(BF))
        pltpu.make_async_copy(out.at[where], out_ref.at[where], sems.at[count]).start()
    pltpu.make_async_copy(out, out_ref, sems.at[count]).wait()


def shards(
    tokens, lengths, masked, route_dev, route_slot, norm_gain, norm_bias, w_qkv, w_out, w_up, b_up, w_down,
    b_down, mask_token, pos_table, cotangent,
):
    count = lax.axis_size("pix")
    reps = lax.axis_size("rep")
    devices = count * reps
    pixels, slots, width = tokens.shape
    cap = max(2, (2 * pixels + count - 1) // count)
    extra = 2
    smem = pl.BlockSpec(memory_space=pltpu.SMEM)
    vmem = pl.BlockSpec(memory_space=pltpu.VMEM)
    anywhere = pl.BlockSpec(memory_space=pl.ANY)
    pix = lax.axis_index("pix")
    me = pix.reshape(1).astype(jnp.int32)
    flat = pix * reps + lax.axis_index("rep")
    core = (flat % 2).reshape(1).astype(jnp.int32)
    payload, pos_rows, take, back_at = prep(tokens, lengths, masked, route_dev, count, cap, extra, me)
    block = cap + extra
    recv = lax.all_to_all(
        payload.reshape(count, block, VIS, width), "pix", split_axis=0, concat_axis=0, tiled=True
    ).reshape(count * block, VIS, width)
    chunk = -(-(3072 + small_rows(slots)) // devices)
    chunk += -chunk % 8
    half = devices // 2
    direct = count <= 8
    dec, keep, send, *back = main_call(
        (
            core, take, back_at, route_slot, recv, cotangent, w_qkv, w_out, w_up, w_down, b_up, b_down,
            norm_gain.reshape(4, width), norm_bias.reshape(4, width), mask_token.reshape(1, width), pos_table,
        ),
        cap,
        extra,
        count,
        devices * chunk,
        count if direct else 1,
    )
    axes = ("pix", "rep")
    swap = [(i, i ^ 1) for i in range(devices)]
    groups = [[2 * i + side for i in range(half)] for side in range(2)]

    def exchange(values):
        return lax.all_to_all(
            values, axes, split_axis=0, concat_axis=0, axis_index_groups=groups, tiled=True
        )

    theirs = lax.ppermute(send, axes, swap)
    piece = jax.ShapeDtypeStruct((half, chunk, 128), BF)
    line = pltpu.VMEM((half, chunk, 128), BF)
    paired = pl.pallas_call(
        pair_sum_kernel,
        out_shape=piece,
        in_specs=[anywhere, anywhere],
        out_specs=vmem,
        scratch_shapes=[line, line, pltpu.SemaphoreType.DMA((2,))],
        compiler_params=pltpu.CompilerParams(vmem_limit_bytes=4 * MIB),
        name="pair_sum",
    )(keep.reshape(half, chunk, 128), theirs.reshape(half, chunk, 128))
    if direct:
        returned = back[:1]
        for step in range(1, count):
            returned.append(lax.ppermute(back[step], "pix", [(i, (i - step) % count) for i in range(count)]))
    else:
        turn = (pix - jnp.arange(count)) % count
        blocks = lax.all_to_all(
            back[0].reshape(count, cap, VIS, width)[turn], "pix", split_axis=0, concat_axis=0, tiled=True
        )
        returned = [blocks[(pix + jnp.arange(count)) % count].reshape(count * cap, VIS, width)]
    spread = pl.pallas_call(
        chunk_sum_kernel,
        out_shape=piece,
        in_specs=[anywhere],
        out_specs=anywhere,
        scratch_shapes=[line, pltpu.VMEM((chunk, 128), BF), pltpu.SemaphoreType.DMA((half,))],
        compiler_params=pltpu.CompilerParams(vmem_limit_bytes=4 * MIB),
        name="chunk_sum",
    )(exchange(paired))
    spread, *returned = lax.optimization_barrier((spread, *returned))
    summed = exchange(spread).reshape(half * chunk, 128)
    other = lax.ppermute(summed, axes, swap)
    small = ((4, width), (4, width), b_up.shape, b_down.shape, (1, width), pos_table.shape)
    large = tuple(w.shape for w in (w_qkv, w_out, w_up, w_down))
    gain, bias, bup, bdown, mask, pos, qkv, out, up, down = pl.pallas_call(
        functools.partial(unpack_kernel, slots),
        out_shape=tuple(jax.ShapeDtypeStruct(shape, F32) for shape in small + large),
        in_specs=[smem, anywhere, anywhere],
        out_specs=(vmem,) * 6 + (anywhere,) * 4,
        scratch_shapes=[pltpu.VMEM(shape, F32) for shape in large]
        + [pltpu.VMEM((2, half * chunk, 128), BF), pltpu.SemaphoreType.DMA((10,))],
        compiler_params=pltpu.CompilerParams(vmem_limit_bytes=8 * MIB),
        name="unpack",
    )(core, summed, other)
    grad_tokens = pl.pallas_call(
        functools.partial(restore_kernel, cap, len(returned)),
        out_shape=jax.ShapeDtypeStruct((pixels * slots, width), F32),
        in_specs=[smem, vmem] + [anywhere] * len(returned),
        out_specs=anywhere,
        scratch_shapes=[
            pltpu.VMEM((count * cap, VIS, width), BF),
            pltpu.VMEM((2 * GROUP * VIS, width), F32),
            pltpu.VMEM((pixels * slots, width), F32),
            pltpu.SemaphoreType.DMA((len(returned) + 1,)),
        ],
        compiler_params=pltpu.CompilerParams(vmem_limit_bytes=8 * MIB),
        name="restore",
    )(back_at, pos_rows, *returned)
    return (
        dec,
        grad_tokens.reshape(pixels, slots, width),
        gain.reshape(norm_gain.shape),
        bias.reshape(norm_bias.shape),
        qkv,
        out,
        up,
        bup,
        down,
        bdown,
        mask.reshape(width),
        pos,
    )


def solution(mesh):
    rows = P(("pix", "rep"))
    in_specs = (rows,) * 5 + (P(),) * 10 + (rows,)
    out_specs = (rows, rows) + (P(),) * 10
    return jax.shard_map(shards, mesh=mesh, in_specs=in_specs, out_specs=out_specs, check_vma=False)
```

```python
import functools

import jax
import jax.numpy as jnp
from jax import lax
from jax.experimental import pallas as pl
from jax.experimental.pallas import tpu as pltpu
from jax.sharding import PartitionSpec as P

HEADS = 8
HEAD_DIM = 16
FOLD = 4
BATCH = 16
PAIRS = 16
ENC_ROWS = 256
SETS = 2
PLACES = (0.0, 1.0, 2.0, 3.0, 4.0)
VIS = 8
GROUP = 16
PAD = 32
CHUNK = 48
FIRST = (4,)
MIDDLE = (1, 2, 3, 5, 6, 7)
LAST = ()
EPS = 1e-05
NEG = -1e30
BF = jnp.bfloat16
F32 = jnp.float32
MIB = 1024 * 1024


def nn(left, right):
    return jnp.dot(left, right, preferred_element_type=F32)


def nt(left, right):
    return lax.dot_general(left, right, (((1,), (1,)), ((), ())), preferred_element_type=F32)


def tn(left, right):
    return lax.dot_general(left, right, (((0,), (0,)), ((), ())), preferred_element_type=F32)


def iota(shape, dim):
    return lax.broadcasted_iota(jnp.int32, shape, dim)


def fold_rows(values):
    rows = values.shape[0]
    return jnp.sum(values.reshape(rows // 8, 8, values.shape[1]), axis=0)


def erf_parts(hidden):
    size = jnp.abs(hidden)
    base = 1.0 + size * (0.3275911 * 0.7071067811865476)
    t = 1.0 / base
    bell = jnp.exp2(hidden * hidden * (-0.5 * 1.4426950408889634))
    poly = t * (
        0.5 * 0.254829592
        + t * (0.5 * -0.284496736 + t * (0.5 * 1.421413741 + t * (0.5 * -1.453152027 + t * (0.5 * 1.061405429))))
    )
    tail = poly * bell
    return jnp.where(hidden >= 0, 1.0 - tail, tail), bell


def expand(rows, masks):
    count = rows.shape[0]
    return jnp.concatenate([rows * masks[h, :count, :] for h in range(HEADS)], axis=0)


def fold_heads(rows, step, count):
    lane = iota((count, 128), 1)
    picked = rows[0:count]
    for head in range(1, HEADS):
        picked = jnp.where(lane >= head * HEAD_DIM, rows[head * step : head * step + count], picked)
    return picked


def fold_halves(rows, step, count):
    lane = iota((count, 128), 1) // HEAD_DIM % FOLD
    picked = rows[0:count]
    for head in range(1, FOLD):
        picked = jnp.where(lane == head, rows[head * step : head * step + count], picked)
    return picked


def expand_halves(rows, masks):
    return jnp.concatenate([rows * masks[h] for h in range(FOLD)], axis=0)


def stack_halves(values):
    low = iota(values.shape, 1) < 64
    return jnp.concatenate([jnp.where(low, values, 0.0), jnp.where(low, 0.0, values)], axis=0).astype(BF)


def join_halves(values):
    count = values.shape[0] // 2
    return jnp.where(iota((count, 128), 1) < 64, values[:count], values[count:])


def both_diagonals(values, rows):
    return values[:rows, :128], values[rows:, 128:]


def block_diagonal(first, second):
    low = jnp.concatenate([first, jnp.zeros_like(first)], axis=1)
    return jnp.concatenate([low, jnp.concatenate([jnp.zeros_like(second), second], axis=1)], axis=0)


def pair_nt(rows, columns):
    full = nt(jnp.concatenate(rows, axis=0), jnp.concatenate(columns, axis=0))
    return both_diagonals(full, rows[0].shape[0])


def pair_nn(rows, columns):
    full = nn(jnp.concatenate(rows, axis=0), jnp.concatenate(columns, axis=1))
    return both_diagonals(full, rows[0].shape[0])


def pair_tn(rows, columns):
    full = tn(jnp.concatenate(rows, axis=0), block_diagonal(*columns))
    return full[:, :128], full[:, 128:]


def with_bias(rows, grad):
    full = nn(jnp.concatenate([rows.T, jnp.ones((16, rows.shape[0]), BF)], axis=0), grad)
    return full[:-16], full[-8:]


def softmax_halves(scores, keep):
    count = scores.shape[0] // 2
    scores = jnp.where(keep[None], scores.reshape(2, count, 128), NEG)
    powers = jnp.exp(scores - jnp.max(scores, axis=1, keepdims=True))
    probs = powers * (1.0 / jnp.sum(powers, axis=1, keepdims=True))
    return probs.reshape(2 * count, 128)


def soft_bwd_halves(probs, grad):
    count = probs.shape[0] // 2
    both = (grad * probs).reshape(2, count, 128)
    lean = jnp.sum(both, axis=1, keepdims=True)
    return (probs.reshape(2, count, 128) * (grad.reshape(2, count, 128) - lean)).reshape(2 * count, 128).astype(BF)


def ln_fwd(values, gain, bias, hat, inv, low, where):
    centred = values - jnp.mean(values, axis=-1, keepdims=True)
    scale = lax.rsqrt(jnp.mean(centred * centred, axis=-1, keepdims=True) + EPS)
    unit = centred * scale
    hat[where] = unit
    inv[where] = jnp.broadcast_to(scale, unit.shape)
    low[where] = (unit * gain + bias).astype(BF)


def ln_bwd(grad, gain, hat, inv, where):
    unit = hat[where]
    inner = grad * gain
    lean = jnp.sum(inner, axis=-1, keepdims=True)
    tilt = jnp.sum(inner * unit, axis=-1, keepdims=True)
    return inv[where] * (inner - (lean + unit * tilt) * (1.0 / unit.shape[-1])), fold_rows(grad * unit), fold_rows(grad)


def prep_kernel(
    cap, extra, count, me_ref, dest_ref, tokens_ref, len_ref, masked_ref, dest_row_ref,
    payload_ref, pos_ref, route_ref, tally,
):
    slots, pixels = masked_ref.shape
    groups = pixels // GROUP
    block = cap + extra
    wide = GROUP * slots
    lanes = GROUP * VIS
    lens = len_ref[...].astype(F32)
    seen = (masked_ref[...] == 0) & (iota((slots, pixels), 0).astype(F32) < lens)
    seen_low = jnp.where(seen, 1.0, 0.0).astype(BF)
    earlier = jnp.where(iota((slots, slots), 1) < iota((slots, slots), 0), 1.0, 0.0).astype(BF)
    member = iota((slots, pixels), 1) % GROUP
    code = jnp.where(seen, nn(earlier, seen_low) + (member * VIS).astype(F32), -1.0)
    spread = jnp.where(iota((slots, wide), 0) == iota((slots, wide), 1) % slots, 1.0, 0.0).astype(BF)
    code_wide = tn(code.astype(BF), spread)
    own = iota((pixels, wide), 0) % GROUP == iota((pixels, wide), 1) // slots
    code_row = jnp.sum(jnp.where(own, code_wide, 0.0).reshape(groups, GROUP, wide), axis=1)
    in_group = iota((groups, pixels), 1) // GROUP == iota((groups, pixels), 0)
    fan = iota((pixels, lanes), 0) % GROUP == iota((pixels, lanes), 1) // VIS
    fan = jnp.where(fan, 1.0, 0.0).astype(BF)
    len_rows = nn(jnp.where(in_group, lens, 0.0).astype(BF), fan)
    dest_rows = nn(jnp.where(in_group, dest_row_ref[...].astype(F32), 0.0).astype(BF), fan)
    me = me_ref[0]
    for dev in range(count):
        tally[dev] = 0
    order = iota((lanes, wide), 0).astype(F32)
    steps = (iota((GROUP, wide), 1) % slots + 1).astype(F32).astype(BF)
    found = []
    for group in range(groups):
        select = jnp.where(order == code_row[group : group + 1, :], 1.0, 0.0).astype(BF)
        rows = nn(select, tokens_ref[group * wide : (group + 1) * wide, :]).reshape(GROUP, VIS, 128)
        found.append(nt(steps, select)[0:1, :])
        for member_id in range(GROUP):
            series = group * GROUP + member_id
            dest = dest_ref[series]
            rank = tally[dest]
            tally[dest] = rank + 1
            sender = lax.rem(2 * me - dest + 2 * count, count)
            route_ref[series] = sender * 256 + rank
            payload_ref[dest * block + rank] = rows[member_id].astype(BF)
    pos_rows = jnp.concatenate(found, axis=0)
    pos_ref[...] = pos_rows

    def label(dev, carry):
        mine = dest_rows == dev.astype(F32)
        payload_ref[dev * block + cap] = jnp.where(mine, pos_rows, 0.0).astype(BF)
        payload_ref[dev * block + cap + 1] = jnp.where(mine, len_rows, 0.0).astype(BF)
        return carry

    lax.fori_loop(0, count, label, 0)


def prep(tokens, lengths, masked, route_dev, count, cap, extra, me):
    pixels, slots, width = tokens.shape
    smem = pl.BlockSpec(memory_space=pltpu.SMEM)
    vmem = pl.BlockSpec(memory_space=pltpu.VMEM)
    index = jax.ShapeDtypeStruct((pixels,), jnp.int32)
    return pl.pallas_call(
        functools.partial(prep_kernel, cap, extra, count),
        out_shape=(
            jax.ShapeDtypeStruct((count * (cap + extra), VIS, width), BF),
            jax.ShapeDtypeStruct((pixels // GROUP, GROUP * VIS), F32),
            index,
        ),
        in_specs=[smem, smem, vmem, vmem, vmem, vmem],
        out_specs=(vmem, vmem, smem),
        scratch_shapes=[pltpu.SMEM((count,), jnp.int32)],
        compiler_params=pltpu.CompilerParams(vmem_limit_bytes=56 * MIB),
        name="prep",
    )(
        me, route_dev, tokens.reshape(pixels * slots, width), lengths.reshape(1, pixels), masked.T,
        route_dev.reshape(1, pixels),
    )


class Box:
    pass


def offset_place(route, me, count, cap):
    return lax.rem(me - (route >> 8) + count, count) * cap + (route & 255)


def gelu_stage(hidden, b_up, act, slope, base, rows):
    for start in range(0, rows, 16):
        value = hidden[start : start + 16] + b_up
        cdf, bell = erf_parts(value)
        where = pl.ds(base + start, 16)
        act[where] = (value * cdf).astype(BF)
        slope[where] = cdf + value * bell * 0.3989422804014327


def slope_stage(grad_act, slope, out, base, rows):
    total = None
    for start in range(0, rows, 16):
        part = (grad_act[start : start + 16] * slope[pl.ds(base + start, 16)]).astype(BF)
        out[pl.ds(start, 16)] = part
        summed = fold_rows(part.astype(F32))
        total = summed if total is None else total + summed
    return total


def softmax_rows(scores, keep):
    scores = jnp.where(keep, scores, NEG)
    powers = jnp.exp(scores - jnp.max(scores, axis=0, keepdims=True))
    return powers / jnp.sum(powers, axis=0, keepdims=True)


def soft_bwd(probs, grad):
    return (probs * (grad - jnp.sum(grad * probs, axis=0, keepdims=True))).astype(BF)


class Encoder:
    def __init__(self, b, base, rows):
        self.b, self.base, self.rows = b, base, rows
        self.whole = slice(base, base + rows)

    def chunks(self):
        return [slice(start, start + 32) for start in range(self.base, self.base + self.rows, 32)]

    def part(self, values, where):
        return values[where.start - self.base : where.stop - self.base]

    def attend(self):
        b, w, whole = self.b, self.b.w, self.whole
        v = Box()
        same = iota((16, 128), 0) // VIS == (iota((16, 128), 1) % 16) // VIS

        def load(series):
            b.e_x[series * VIS : (series + 1) * VIS] = b.recv[b.take(series)].astype(F32)

        steps = [functools.partial(load, series) for series in range(self.base // VIS, (self.base + self.rows) // VIS)]

        def norm(where):
            ln_fwd(b.e_x[where], w.gain[0:1], w.bias[0:1], b.e_hat1, b.e_inv1, b.e_n1, where)

        steps += [functools.partial(norm, where) for where in self.chunks()]

        def project():
            v.qkv = nn(b.e_n1[whole], w.qkv[0])
            v.score, v.prob, v.mixed = {}, {}, {}

        steps.append(project)

        def split(where):
            part = self.part(v.qkv, where)
            b.e_qkv[where, 0:128] = (part[:, 0:128] * 0.25).astype(BF)
            b.e_qkv[where, 128:384] = part[:, 128:384].astype(BF)

        steps += [functools.partial(split, where) for where in self.chunks()]

        def score(at):
            pair = (at, at + 16)
            queries = [expand(b.e_qkv[one : one + 16, 0:128], b.masks) for one in pair]
            keys = [b.e_qkv[one : one + 16, 128:256] for one in pair]
            v.score[at], v.score[at + 16] = pair_nt(keys, queries)

        def soft(at):
            v.prob[at] = softmax_rows(v.score[at], same & (b.pos_col[at : at + 16] > 0))
            b.e_probs[at : at + 16] = v.prob[at]

        def mix(at):
            pair = (at, at + 16)
            values = [b.e_qkv[one : one + 16, 256:384] for one in pair]
            v.mixed[at], v.mixed[at + 16] = pair_tn([v.prob[one].astype(BF) for one in pair], values)

        def gather(at):
            b.e_att[at : at + 16] = fold_heads(v.mixed[at], 16, 16).astype(BF)

        for first in range(self.base, self.base + self.rows, 16 * PAIRS):
            for stage, stride in ((score, 32), (soft, 16), (mix, 32), (gather, 16)):
                steps += [functools.partial(stage, at) for at in range(first, first + 16 * PAIRS, stride)]

        def out():
            v.proj = nn(b.e_att[whole], w.out[0])

        steps.append(out)

        def second(where):
            middle = b.e_x[where] + self.part(v.proj, where)
            b.e_x[where] = middle
            ln_fwd(middle, w.gain[1:2], w.bias[1:2], b.e_hat2, b.e_inv2, b.e_n2, where)

        steps += [functools.partial(second, where) for where in self.chunks()]
        return steps

    def bend(self):
        b, w, whole = self.b, self.b.w, self.whole
        v = Box()

        def up():
            v.hidden = nn(b.e_n2[whole], w.up[0])

        def curve(start):
            value = v.hidden[start : start + 16] + w.b_up[0:1]
            cdf, bell = erf_parts(value)
            where = slice(self.base + start, self.base + start + 16)
            b.e_act[where] = (value * cdf).astype(BF)
            b.e_slope[where] = cdf + value * bell * 0.3989422804014327

        def down():
            v.down = nn(b.e_act[whole], w.down[0])

        def finish(where):
            b.sent[where] = (b.e_x[where] + self.part(v.down, where) + w.b_down[0:1]).astype(BF)

        return (
            [up]
            + [functools.partial(curve, start) for start in range(0, self.rows, 16)]
            + [down]
            + [functools.partial(finish, where) for where in self.chunks()]
        )

    def feed(self):
        b, whole = self.b, self.whole
        v = Box()

        def back():
            grad_low = b.g_sent[whole]
            b.d_down[0] += tn(grad_low, b.e_act[whole])
            b.d_b_down[0] += fold_rows(grad_low.astype(F32))
            v.grad_act = nn(grad_low, b.down_t[0])

        def unbend(start):
            where = slice(self.base + start, self.base + start + 16)
            b.e_gh[where] = (v.grad_act[start : start + 16] * b.e_slope[where]).astype(BF)

        def end():
            weights, bias = with_bias(b.e_n2[whole], b.e_gh[whole])
            b.d_up[0] += weights
            b.d_b_up[0] += bias
            b.e_gn2[whole] = nn(b.e_gh[whole], b.up_t[0])

        return [back] + [functools.partial(unbend, start) for start in range(0, self.rows, 16)] + [end]

    def retreat(self):
        b, w, whole = self.b, self.b.w, self.whole
        v = Box()

        def norm(where):
            grad, gain_part, bias_part = ln_bwd(b.e_gn2[where], w.gain[1:2], b.e_hat2, b.e_inv2, where)
            b.d_gain[1] += gain_part
            b.d_bias[1] += bias_part
            grad = grad + b.g_sent[where].astype(F32)
            b.e_gm[where] = grad
            b.e_gml[where] = grad.astype(BF)

        steps = [functools.partial(norm, where) for where in self.chunks()]

        def out():
            b.d_out[0] += tn(b.e_att[whole], b.e_gml[whole])
            v.grad_att = nn(b.e_gml[whole], b.out_t[0])
            v.grad, v.grad_p, v.grad_s, v.grad_v, v.grad_k, v.grad_q = ({} for _ in range(6))

        steps.append(out)

        def spread(at):
            pair = (at, at + 16)
            for one in pair:
                low = v.grad_att[one - self.base : one - self.base + 16].astype(BF)
                v.grad[one] = expand(low, b.masks)
            values = [b.e_qkv[one : one + 16, 256:384] for one in pair]
            v.grad_p[at], v.grad_p[at + 16] = pair_nt(values, [v.grad[one] for one in pair])

        def values(at):
            pair = (at, at + 16)
            probs = [b.e_probs[one : one + 16].astype(BF) for one in pair]
            v.grad_v[at], v.grad_v[at + 16] = pair_nn(probs, [v.grad[one] for one in pair])

        def soft(at):
            v.grad_s[at] = soft_bwd(b.e_probs[at : at + 16], v.grad_p[at])

        def keys(at):
            pair = (at, at + 16)
            columns = [expand(b.e_qkv[one : one + 16, 0:128], b.masks) for one in pair]
            v.grad_k[at], v.grad_k[at + 16] = pair_nn([v.grad_s[one] for one in pair], columns)

        def queries(at):
            pair = (at, at + 16)
            keys = [b.e_qkv[one : one + 16, 128:256] for one in pair]
            v.grad_q[at], v.grad_q[at + 16] = pair_tn([v.grad_s[one] for one in pair], keys)

        def gather(at):
            b.e_gqkv[at : at + 16, 256:384] = v.grad_v[at].astype(BF)
            b.e_gqkv[at : at + 16, 128:256] = v.grad_k[at].astype(BF)
            b.e_gqkv[at : at + 16, 0:128] = (fold_heads(v.grad_q[at], 16, 16) * 0.25).astype(BF)

        for first in range(self.base, self.base + self.rows, 16 * PAIRS):
            for stage, stride in ((spread, 32), (values, 32), (soft, 16), (keys, 32), (queries, 32), (gather, 16)):
                steps += [functools.partial(stage, at) for at in range(first, first + 16 * PAIRS, stride)]

        def project():
            b.d_qkv[0] += tn(b.e_n1[whole], b.e_gqkv[whole])
            v.grad_n1 = nn(b.e_gqkv[whole], b.qkv_t[0])

        steps.append(project)

        def first_norm(where):
            grad, gain_part, bias_part = ln_bwd(
                self.part(v.grad_n1, where), w.gain[0:1], b.e_hat1, b.e_inv1, where
            )
            b.d_gain[0] += gain_part
            b.d_bias[0] += bias_part
            grad = grad + b.e_gm[where]
            for series in range(where.start // VIS, where.stop // VIS):
                at = series * VIS - where.start
                b.back[b.back_at(series)] = grad[at : at + VIS].astype(BF)

        steps += [functools.partial(first_norm, where) for where in self.chunks()]
        return steps


def weave(timeline):
    order = []
    for which, (start, length, steps) in enumerate(timeline):
        order += [(start + length * (index + 0.5) / len(steps), which, step) for index, step in enumerate(steps)]
    for _, _, step in sorted(order, key=lambda entry: entry[:2]):
        step()


class Decoder:
    def __init__(self, b, d, group):
        self.b, self.d, self.group = b, d, group
        self.slots = b.slots
        self.rows = GROUP * b.slots
        self.sent_rows = pl.ds(pl.multiple_of(group * 128, 128), 128)
        self.zeros = jnp.zeros((PAD - b.slots, 128), F32)
        self.step = iota((b.slots, 128), 0).astype(F32)

    def span(self, member):
        return pl.ds(member * self.slots, self.slots)

    def cut(self, member):
        return slice(member * self.slots, (member + 1) * self.slots)

    def inside(self, member):
        lens = self.b.len_col[pl.ds(pl.multiple_of(self.group * 128, 128) + member * VIS, VIS)]
        return self.step < jnp.concatenate([lens] * (self.slots // VIS), axis=0)

    def padded(self, values):
        return jnp.concatenate([values, self.zeros], axis=0).astype(BF)

    def chunks(self):
        return range(0, self.rows, CHUNK)

    def attend(self):
        b, d, w, slots = self.b, self.d, self.b.w, self.slots
        v = Box()
        steps = []

        def begin():
            pos_row = b.pos_row[self.group]
            lane = iota((1, 128), 1)
            target = jnp.where(pos_row > 0, (lane // VIS * slots).astype(F32) + pos_row - 1.0, -1.0)
            for start in self.chunks():
                spot = (iota((CHUNK, 128), 0) + start).astype(F32)
                d.hot[pl.ds(start, CHUNK)] = jnp.where(spot == target, 1.0, 0.0).astype(BF)
            both = jnp.concatenate([b.sent[self.sent_rows], jnp.ones((128, 128), BF)], axis=1)
            full = nn(d.hot[...], both)
            v.placed, v.shown = full[:, 0:128], full[:, 128:256]

        steps.append(begin)

        def assemble(member):
            at = self.cut(member)
            hidden_part = 1.0 - v.shown[at]
            d.unseen[self.span(member)] = hidden_part
            d.x[self.span(member)] = v.placed[at] + hidden_part * w.mask[...] + w.pos[...]
            cot = b.cot[b.slot[self.group * GROUP + member]].astype(F32)
            d.g[self.span(member)] = jnp.where(self.inside(member), cot, 0.0)

        steps += [functools.partial(assemble, member) for member in range(GROUP)]

        def norm(start):
            where = pl.ds(start, CHUNK)
            ln_fwd(d.x[where], w.gain[2:3], w.bias[2:3], d.hat1, d.inv1, d.n1, where)

        steps += [functools.partial(norm, start) for start in self.chunks()]

        def project():
            v.qkv = nn(d.n1[...], w.qkv[1])
            v.score, v.prob, v.mixed = {}, {}, {}

        steps.append(project)

        def split(member):
            at = self.cut(member)
            d.q[member] = self.padded(v.qkv[at, 0:128] * 0.25)
            d.k[member] = stack_halves(v.qkv[at, 128:256])
            d.v[member] = stack_halves(v.qkv[at, 256:384])

        def score(member):
            pair = (member, member + 1)
            queries = [expand_halves(d.q[one], b.masks_half) for one in pair]
            v.score[member], v.score[member + 1] = pair_nt([d.k[one] for one in pair], queries)

        def soft(member):
            v.prob[member] = softmax_halves(v.score[member], self.inside(member))
            d.probs[member] = v.prob[member]

        def mix(member):
            pair = (member, member + 1)
            mixed = pair_tn([v.prob[one].astype(BF) for one in pair], [d.v[one] for one in pair])
            v.mixed[member], v.mixed[member + 1] = mixed

        def gather(member):
            d.att32[self.span(member)] = fold_halves(v.mixed[member], PAD, slots)

        for first in range(0, GROUP, BATCH):
            for stage, stride in ((split, 1), (score, 2), (soft, 1), (mix, 2), (gather, 1)):
                steps += [functools.partial(stage, member) for member in range(first, first + BATCH, stride)]

        def low(start):
            where = pl.ds(start, CHUNK)
            d.att[where] = d.att32[where].astype(BF)

        steps += [functools.partial(low, start) for start in self.chunks()]

        def out():
            v.proj = nn(d.att[...], w.out[1])

        steps.append(out)

        def second(start):
            where = pl.ds(start, CHUNK)
            middle = d.x[where] + v.proj[start : start + CHUNK]
            d.x[where] = middle
            ln_fwd(middle, w.gain[3:4], w.bias[3:4], d.hat2, d.inv2, d.n2, where)

        steps += [functools.partial(second, start) for start in self.chunks()]
        return steps

    def bend(self):
        b, d, w = self.b, self.d, self.b.w
        v = Box()
        steps = []

        def up():
            v.hidden = nn(d.n2[...], w.up[1])

        steps.append(up)

        def curve(start):
            value = v.hidden[start : start + 16] + w.b_up[1:2]
            cdf, bell = erf_parts(value)
            where = pl.ds(start, 16)
            d.act[where] = (value * cdf).astype(BF)
            d.slope[where] = cdf + value * bell * 0.3989422804014327

        steps += [functools.partial(curve, start) for start in range(0, self.rows, 16)]
        return steps

    def feed(self):
        b, d, w = self.b, self.d, self.b.w
        v = Box()
        steps = []

        def down():
            v.down = nn(d.act[...], w.down[1])

        steps.append(down)

        def finish(member):
            value = d.x[self.span(member)] + v.down[self.cut(member)] + w.b_down[1:2]
            slot = b.slot[self.group * GROUP + member]
            b.dec[slot] = jnp.where(self.inside(member), value, 0.0)
            pltpu.make_async_copy(b.dec.at[slot], b.dec_out.at[slot], b.sems.at[1]).start()

        steps += [functools.partial(finish, member) for member in range(GROUP)]

        def low(start):
            where = pl.ds(start, CHUNK)
            d.gl[where] = d.g[where].astype(BF)

        steps += [functools.partial(low, start) for start in self.chunks()]

        def back():
            b.d_down[1] += tn(d.gl[...], d.act[...])
            b.d_b_down[1] += fold_rows(d.g[...])
            v.grad_act = nn(d.gl[...], b.down_t[1])

        steps.append(back)

        def unbend(start):
            d.gh[pl.ds(start, 16)] = (v.grad_act[start : start + 16] * d.slope[pl.ds(start, 16)]).astype(BF)

        steps += [functools.partial(unbend, start) for start in range(0, self.rows, 16)]

        def end():
            weights, bias = with_bias(d.n2[...], d.gh[...])
            b.d_up[1] += weights
            b.d_b_up[1] += bias
            d.gn2[...] = nn(d.gh[...], b.up_t[1])

        steps.append(end)
        return steps

    def retreat(self):
        b, d, w, slots = self.b, self.d, self.b.w, self.slots
        v = Box()
        steps = []

        def norm(start):
            where = pl.ds(start, CHUNK)
            grad, gain_part, bias_part = ln_bwd(d.gn2[where], w.gain[3:4], d.hat2, d.inv2, where)
            b.d_gain[3] += gain_part
            b.d_bias[3] += bias_part
            grad = grad + d.g[where]
            d.g[where] = grad
            d.gl[where] = grad.astype(BF)

        steps += [functools.partial(norm, start) for start in self.chunks()]

        def out():
            b.d_out[1] += tn(d.att[...], d.gl[...])
            v.grad_att = nn(d.gl[...], b.out_t[1])
            v.grad, v.prob, v.grad_p, v.grad_s, v.grad_v, v.grad_k, v.grad_q = ({} for _ in range(7))

        steps.append(out)

        def spread(member):
            pair = (member, member + 1)
            for one in pair:
                v.grad[one] = expand_halves(self.padded(v.grad_att[self.cut(one)]), b.masks_half)
            grads = [v.grad[one] for one in pair]
            v.grad_p[member], v.grad_p[member + 1] = pair_nt([d.v[one] for one in pair], grads)

        def values(member):
            pair = (member, member + 1)
            probs = [d.probs[one].astype(BF) for one in pair]
            v.grad_v[member], v.grad_v[member + 1] = pair_nn(probs, [v.grad[one] for one in pair])

        def soft(member):
            v.grad_s[member] = soft_bwd_halves(d.probs[member], v.grad_p[member])

        def keys(member):
            pair = (member, member + 1)
            columns = [expand_halves(d.q[one], b.masks_half) for one in pair]
            v.grad_k[member], v.grad_k[member + 1] = pair_nn([v.grad_s[one] for one in pair], columns)

        def queries(member):
            pair = (member, member + 1)
            grads = pair_tn([v.grad_s[one] for one in pair], [d.k[one] for one in pair])
            v.grad_q[member], v.grad_q[member + 1] = grads

        def gather(member):
            d.gqkv32[self.span(member), 256:384] = join_halves(v.grad_v[member])
            d.gqkv32[self.span(member), 128:256] = join_halves(v.grad_k[member])
            d.gqkv32[self.span(member), 0:128] = fold_halves(v.grad_q[member], PAD, slots) * 0.25

        for first in range(0, GROUP, BATCH):
            for stage, stride in ((spread, 2), (values, 2), (soft, 1), (keys, 2), (queries, 2), (gather, 1)):
                steps += [functools.partial(stage, member) for member in range(first, first + BATCH, stride)]

        def low(start):
            where = pl.ds(start, CHUNK)
            d.gqkv[where] = d.gqkv32[where].astype(BF)

        steps += [functools.partial(low, start) for start in self.chunks()]

        def project():
            b.d_qkv[1] += tn(d.n1[...], d.gqkv[...])
            v.grad_n1 = nn(d.gqkv[...], b.qkv_t[1])
            v.pos = None

        steps.append(project)

        def first_norm(start):
            where = pl.ds(start, CHUNK)
            grad, gain_part, bias_part = ln_bwd(
                v.grad_n1[start : start + CHUNK], w.gain[2:3], d.hat1, d.inv1, where
            )
            b.d_gain[2] += gain_part
            b.d_bias[2] += bias_part
            grad = grad + d.g[where]
            d.gl[where] = grad.astype(BF)
            part = jnp.sum(grad.reshape(CHUNK // slots, slots, 128), axis=0)
            v.pos = part if v.pos is None else v.pos + part
            b.d_mask[...] += fold_rows(grad * d.unseen[where])

        steps += [functools.partial(first_norm, start) for start in self.chunks()]

        def end():
            b.d_pos[...] += v.pos
            b.g_sent[self.sent_rows] = tn(d.hot[...], d.gl[...]).astype(BF)

        steps.append(end)
        return steps


def plan(b, groups, encoders, before_first):
    timeline = []
    for index in range(groups):
        decoder = Decoder(b, b.sets[index % SETS], index)
        phases = (decoder.attend, decoder.bend, decoder.feed, decoder.retreat)
        for start, stop, phase in zip(PLACES, PLACES[1:], phases):
            timeline.append((2 * index + start, stop - start, phase()))
    timeline.append((-0.01, 0.01, [before_first]))
    for chunk in encoders:
        first, last = chunk.base // (GROUP * VIS), (chunk.base + chunk.rows) // (GROUP * VIS) - 1
        early = 2 * first - (4 if first else 2)
        room = (2 * first - early) / 2
        timeline.append((early, room, chunk.attend()))
        timeline.append((early + room, room, chunk.bend()))
        late = 2 * last + PLACES[-1]
        room = 2 if last < groups - 1 else 1
        timeline.append((late, room, chunk.feed()))
        timeline.append((late + room, room, chunk.retreat()))
    return timeline


IN_NAMES = (
    "core", "me", "route", "slot", "recv_in", "cot_in", "w_qkv", "w_out", "w_up", "w_down", "b_up", "b_down",
    "gain", "bias", "mask", "pos",
)
OUT_NAMES = ("dec_out", "keep", "send")


def small_rows(slots):
    return 18 + 1 + slots


def main_kernel(names, cap, extra, count, outs, *refs):
    b = Box()
    b.sets = tuple(Box() for _ in range(SETS))
    b.back_out = refs[len(IN_NAMES) + len(OUT_NAMES) : len(IN_NAMES) + len(OUT_NAMES) + outs]
    refs = refs[: len(IN_NAMES) + len(OUT_NAMES)] + refs[len(IN_NAMES) + len(OUT_NAMES) + outs :]
    for name, ref in zip(names, refs, strict=True):
        name, _, side = name.partition("@")
        setattr(b.sets[int(side)] if side else b, name, ref)
    b.w = Box()
    for name in ("qkv", "out", "up", "down"):
        setattr(b.w, name, getattr(b, "w_" + name))
    for name in ("b_up", "b_down", "gain", "bias", "mask", "pos"):
        setattr(b.w, name, getattr(b, name))
    b.slots = b.cot.shape[1]
    pixels = b.cot.shape[0]
    groups = pixels // GROUP
    block = cap + extra
    b.take = lambda series: (b.route[series] >> 8) * block + (b.route[series] & 255)
    b.back_at = lambda series: offset_place(b.route[series], b.me[0], count, cap)
    recv_copy = pltpu.make_async_copy(b.recv_in, b.recv, b.sems.at[0])
    recv_copy.start()
    cot_copy = pltpu.make_async_copy(b.cot_in, b.cot, b.sems.at[2])
    cot_copy.start()
    for head in range(HEADS):
        lane = iota((PAD, 128), 1) // HEAD_DIM
        b.masks[head] = jnp.where(lane == head, 1.0, 0.0).astype(BF)
    for head in range(FOLD):
        lane = iota((PAD, 128), 1) // HEAD_DIM % FOLD
        b.masks_half[head] = jnp.where(lane == head, 1.0, 0.0).astype(BF)
    for layer in range(2):
        b.qkv_t[layer] = b.w_qkv[layer].T
        b.out_t[layer] = b.w_out[layer].T
        b.up_t[layer] = b.w_up[layer].T
        b.down_t[layer] = b.w_down[layer].T
    for ref in (b.d_qkv, b.d_out, b.d_up, b.d_down, b.d_gain, b.d_bias, b.d_b_up, b.d_b_down, b.d_mask, b.d_pos):
        ref[...] = jnp.zeros(ref.shape, F32)

    def gather(dev, carry):
        pos, lens = carry
        return (
            pos + b.recv[dev * block + cap].astype(F32),
            lens + b.recv[dev * block + cap + 1].astype(F32),
        )

    empty = jnp.zeros((groups, 128), F32)
    recv_copy.wait()
    pos, lens = lax.fori_loop(0, count, gather, (empty, empty))
    for group in range(groups):
        where = pl.ds(group * 128, 128)
        b.pos_row[group] = pos[group : group + 1]
        b.pos_col[where] = jnp.broadcast_to(pos[group : group + 1], (128, 128)).T
        b.len_col[where] = jnp.broadcast_to(lens[group : group + 1], (128, 128)).T

    encoders = [Encoder(b, base, ENC_ROWS) for base in range(0, pixels * VIS, ENC_ROWS)]
    weave(plan(b, groups, encoders, cot_copy.wait))
    copies = []
    size = b.back.shape[0] // outs
    for index, ref in enumerate(b.back_out):
        copies.append(pltpu.make_async_copy(b.back.at[pl.ds(index * size, size)], ref, b.sems.at[5 + index]))
        copies[-1].start()

    offset = 0
    for layer in range(2):
        for start in range(0, 384, 128):
            b.grads[offset : offset + 128] = b.d_qkv[layer, :, start : start + 128].astype(BF)
            offset += 128
        b.grads[offset : offset + 128] = b.d_out[layer].astype(BF)
        offset += 128
        for start in range(0, 512, 128):
            b.grads[offset : offset + 128] = b.d_up[layer, :, start : start + 128].astype(BF)
            offset += 128
        for start in range(0, 512, 128):
            b.grads[offset : offset + 128] = b.d_down[layer, :, start : start + 128].T.astype(BF)
            offset += 128

    def total(ref, index):
        return jnp.sum(ref[index], axis=0, keepdims=True)

    small = [total(b.d_gain, i) for i in range(4)] + [total(b.d_bias, i) for i in range(4)]
    for layer in range(2):
        row = b.d_b_up[layer, 0:1]
        small += [row[:, start : start + 128] for start in range(0, 512, 128)]
    small += [total(b.d_b_down, layer) for layer in range(2)]
    small.append(jnp.sum(b.d_mask[...], axis=0, keepdims=True))
    small.append(b.d_pos[...])
    tail = jnp.concatenate(small, axis=0)
    fill = -tail.shape[0] % 16
    tail = jnp.concatenate([tail, jnp.zeros((fill, 128), F32)], axis=0)
    b.grads[offset : offset + tail.shape[0]] = tail.astype(BF)
    half = b.grads.shape[0] // 2
    mine = b.core[0]
    for side, ref, sem in ((mine, b.keep, 3), (1 - mine, b.send, 4)):
        rows = pl.ds(pl.multiple_of(side * half, half), half)
        copies.append(pltpu.make_async_copy(b.grads.at[rows], ref, b.sems.at[sem]))
        copies[-1].start()
    for copy in copies:
        copy.wait()
    pltpu.make_async_copy(b.dec, b.dec_out, b.sems.at[1]).wait()


def decoder_scratch(rows, slots):
    return {
        "hot": ((rows, 128), BF),
        "unseen": ((rows, 128), F32),
        "x": ((rows, 128), F32),
        "g": ((rows, 128), F32),
        "gl": ((rows, 128), BF),
        "hat1": ((rows, 128), F32),
        "inv1": ((rows, 128), F32),
        "n1": ((rows, 128), BF),
        "q": ((GROUP, PAD, 128), BF),
        "k": ((GROUP, 2 * slots, 128), BF),
        "v": ((GROUP, 2 * slots, 128), BF),
        "probs": ((GROUP, 2 * slots, 128), F32),
        "att32": ((rows, 128), F32),
        "att": ((rows, 128), BF),
        "hat2": ((rows, 128), F32),
        "inv2": ((rows, 128), F32),
        "n2": ((rows, 128), BF),
        "act": ((rows, 512), BF),
        "slope": ((rows, 512), F32),
        "gh": ((rows, 512), BF),
        "gn2": ((rows, 128), F32),
        "gqkv32": ((rows, 384), F32),
        "gqkv": ((rows, 384), BF),
    }


def main_call(args, cap, extra, count, grad_rows, outs):
    recv, cot = args[4], args[5]
    pixels, slots, width = cot.shape
    enc = pixels * VIS
    rows = GROUP * slots
    smem = pl.BlockSpec(memory_space=pltpu.SMEM)
    vmem = pl.BlockSpec(memory_space=pltpu.VMEM)
    anywhere = pl.BlockSpec(memory_space=pl.ANY)
    scratch = {
        "recv": (recv.shape, BF),
        "cot": (cot.shape, BF),
        "dec": (cot.shape, F32),
        "back": ((count * cap, VIS, width), BF),
        "grads": ((grad_rows, 128), BF),
        "masks": ((HEADS, PAD, 128), BF),
        "masks_half": ((FOLD, PAD, 128), BF),
        "qkv_t": ((2, 384, 128), BF),
        "out_t": ((2, 128, 128), BF),
        "up_t": ((2, 512, 128), BF),
        "down_t": ((2, 128, 512), BF),
        "d_qkv": ((2, 128, 384), F32),
        "d_out": ((2, 128, 128), F32),
        "d_up": ((2, 128, 512), F32),
        "d_down": ((2, 128, 512), F32),
        "d_gain": ((4, 8, 128), F32),
        "d_bias": ((4, 8, 128), F32),
        "d_b_up": ((2, 8, 512), F32),
        "d_b_down": ((2, 8, 128), F32),
        "d_mask": ((8, 128), F32),
        "d_pos": ((slots, 128), F32),
        "pos_row": ((pixels // GROUP, 1, 128), F32),
        "pos_col": ((enc, 128), F32),
        "len_col": ((enc, 128), F32),
        "sent": ((enc, 128), BF),
        "g_sent": ((enc, 128), BF),
        "e_x": ((enc, 128), F32),
        "e_hat1": ((enc, 128), F32),
        "e_inv1": ((enc, 128), F32),
        "e_n1": ((enc, 128), BF),
        "e_qkv": ((enc, 384), BF),
        "e_probs": ((enc, 128), F32),
        "e_att": ((enc, 128), BF),
        "e_hat2": ((enc, 128), F32),
        "e_inv2": ((enc, 128), F32),
        "e_n2": ((enc, 128), BF),
        "e_act": ((enc, 512), BF),
        "e_slope": ((enc, 512), F32),
        "e_gh": ((enc, 512), BF),
        "e_gn2": ((enc, 128), F32),
        "e_gm": ((enc, 128), F32),
        "e_gml": ((enc, 128), BF),
        "e_gqkv": ((enc, 384), BF),
    }
    for side in range(SETS):
        for name, entry in decoder_scratch(rows, slots).items():
            scratch[f"{name}@{side}"] = entry
    names = IN_NAMES + OUT_NAMES + tuple(scratch) + ("sems",)
    half = jax.ShapeDtypeStruct((grad_rows // 2, 128), BF)
    return pl.pallas_call(
        functools.partial(main_kernel, names, cap, extra, count, outs),
        out_shape=(jax.ShapeDtypeStruct((pixels, slots, width), F32), half, half)
        + (jax.ShapeDtypeStruct((count * cap // outs, VIS, width), BF),) * outs,
        in_specs=[smem] * 4 + [anywhere] * 2 + [vmem] * (len(IN_NAMES) - 6),
        out_specs=(anywhere,) * (3 + outs),
        scratch_shapes=[pltpu.VMEM(shape, kind) for shape, kind in scratch.values()]
        + [pltpu.SemaphoreType.DMA((5 + outs,))],
        compiler_params=pltpu.CompilerParams(vmem_limit_bytes=32 * MIB),
        name="layers",
    )(*args)


def fetch(pairs, sems):
    copies = [pltpu.make_async_copy(src, dst, sems.at[index]) for index, (src, dst) in enumerate(pairs)]
    for copy in copies:
        copy.start()
    return copies


def pair_sum_kernel(spot_ref, mine_ref, theirs_ref, keep_ref, send_ref, mine, theirs, sems):
    for copy in fetch([(mine_ref, mine), (theirs_ref, theirs)], sems):
        copy.wait()
    side = spot_ref[0]
    for ref, which in ((send_ref, 1 - side), (keep_ref, side)):
        ref[...] = (mine[:, which].astype(F32) + theirs[:, which].astype(F32)).astype(BF)


def quad_sum_kernel(mine_ref, theirs_ref, out_ref, mine, theirs, sems):
    for copy in fetch([(mine_ref, mine), (theirs_ref, theirs)], sems):
        copy.wait()
    out_ref[...] = (mine[...].astype(F32) + theirs[...].astype(F32)).astype(BF)


def chunk_sum_kernel(parts_ref, out_ref, parts, low, sems):
    count = parts_ref.shape[0]
    (copy,) = fetch([(parts_ref, parts)], sems)
    copy.wait()
    total = parts[0].astype(F32)
    for part in range(1, count):
        total = total + parts[part].astype(F32)
    low[...] = total.astype(BF)
    for copy in fetch([(low, out_ref.at[part]) for part in range(out_ref.shape[0])], sems):
        copy.wait()


BIG = ("qkv", "out", "up", "down")


def unpack_kernel(slots, *refs):
    (core_ref, mine_ref, theirs_ref, gain_ref, bias_ref, b_up_ref, b_down_ref, mask_ref, pos_ref) = refs[:9]
    outs = dict(zip(BIG, refs[9:13]))
    held = dict(zip(BIG, refs[13:17]))
    full, sems = refs[17:]
    core = core_ref[0]
    for copy in fetch([(mine_ref, full.at[core]), (theirs_ref, full.at[1 - core])], sems):
        copy.wait()
    half = full.shape[1]

    def rows(start, size):
        side, at = start // half, start % half
        if at + size <= half:
            return full[side, at : at + size].astype(F32)
        cut = half - at
        return jnp.concatenate(
            [full[side, at:half].astype(F32), full[side + 1, 0 : size - cut].astype(F32)], axis=0
        )

    offset = 0
    copies = []

    def leave(name, layer):
        copy = pltpu.make_async_copy(held[name].at[layer], outs[name].at[layer], sems.at[2 + len(copies)])
        copy.start()
        copies.append(copy)

    for layer in range(2):
        for start in range(0, 384, 128):
            held["qkv"][layer, :, start : start + 128] = rows(offset, 128)
            offset += 128
        leave("qkv", layer)
        held["out"][layer] = rows(offset, 128)
        offset += 128
        leave("out", layer)
        for start in range(0, 512, 128):
            held["up"][layer, :, start : start + 128] = rows(offset, 128)
            offset += 128
        leave("up", layer)
        for start in range(0, 512, 128):
            held["down"][layer, start : start + 128, :] = rows(offset, 128)
            offset += 128
        leave("down", layer)
    count = small_rows(slots)
    small = rows(offset, count + (-count % 16))
    gain_ref[...] = small[0:4]
    bias_ref[...] = small[4:8]
    for layer in range(2):
        for part in range(4):
            at = 8 + 4 * layer + part
            b_up_ref[layer : layer + 1, part * 128 : (part + 1) * 128] = small[at : at + 1]
    b_down_ref[...] = small[16:18]
    mask_ref[...] = small[18:19]
    pos_ref[...] = small[19 : 19 + slots]
    for copy in copies:
        copy.wait()


def restore_kernel(cap, steps, count, spot_ref, route_ref, pos_ref, *refs):
    blocks, (out_ref, rows, held, out, sems) = refs[:count], refs[count:]
    size = rows.shape[0] // count
    copies = fetch([(ref, rows.at[pl.ds(index * size, size)]) for index, ref in enumerate(blocks)], sems)
    groups = pos_ref.shape[0]
    wide = out.shape[0] // groups
    slots = wide // GROUP
    lane = iota((1, 128), 1)
    for copy in copies:
        copy.wait()
    for group in range(groups):
        for member in range(GROUP):
            block = rows[offset_place(route_ref[group * GROUP + member], spot_ref[0], steps, cap)]
            held[pl.ds((group % 2) * 128 + member * VIS, VIS)] = block.astype(F32)
        pos_row = pos_ref[group : group + 1]
        target = jnp.where(pos_row > 0, (lane // VIS * slots).astype(F32) + pos_row - 1.0, -1.0)
        hot = jnp.where(iota((wide, 128), 0).astype(F32) == target, 1.0, 0.0).astype(BF)
        where = pl.ds(group * wide, wide)
        out[where] = nn(hot, held[pl.ds((group % 2) * 128, 128)].astype(BF))
        pltpu.make_async_copy(out.at[where], out_ref.at[where], sems.at[count]).start()
    pltpu.make_async_copy(out, out_ref, sems.at[count]).wait()


def shards(
    tokens, lengths, masked, route_dev, route_slot, norm_gain, norm_bias, w_qkv, w_out, w_up, b_up, w_down,
    b_down, mask_token, pos_table, cotangent,
):
    count = lax.axis_size("pix")
    reps = lax.axis_size("rep")
    devices = count * reps
    pixels, slots, width = tokens.shape
    cap = max(2, (2 * pixels + count - 1) // count)
    extra = 2
    smem = pl.BlockSpec(memory_space=pltpu.SMEM)
    vmem = pl.BlockSpec(memory_space=pltpu.VMEM)
    anywhere = pl.BlockSpec(memory_space=pl.ANY)
    pix = lax.axis_index("pix")
    rep = lax.axis_index("rep")
    core, side, me = (value.reshape(1).astype(jnp.int32) for value in (rep % 2, rep // 2 % 2, pix))
    payload, pos_rows, route = prep(tokens, lengths, masked, route_dev, count, cap, extra, me)
    block = cap + extra
    recv = lax.all_to_all(
        payload.reshape(count, block, VIS, width), "pix", split_axis=0, concat_axis=0, tiled=True
    ).reshape(count * block, VIS, width)
    chunk = -(-(3072 + small_rows(slots)) // devices)
    chunk += -chunk % 8
    half = devices // 2
    direct = count <= 8
    dec, keep, send, *back = main_call(
        (
            core, me, route, route_slot, recv, cotangent, w_qkv, w_out, w_up, w_down, b_up, b_down,
            norm_gain.reshape(4, width), norm_bias.reshape(4, width), mask_token.reshape(1, width), pos_table,
        ),
        cap,
        extra,
        count,
        devices * chunk,
        count if direct else 1,
    )
    axes = ("pix", "rep")
    swap = [(i, i ^ 1) for i in range(devices)]
    groups = [[2 * i + side for i in range(half)] for side in range(2)]

    def exchange(values):
        return lax.all_to_all(
            values, axes, split_axis=0, concat_axis=0, axis_index_groups=groups, tiled=True
        )

    theirs = lax.ppermute(send, axes, swap)
    quarter = jax.ShapeDtypeStruct((count, chunk, 128), BF)
    line = pltpu.VMEM((count, 2, chunk, 128), BF)
    keep, send = pl.pallas_call(
        pair_sum_kernel,
        out_shape=(quarter, quarter),
        in_specs=[smem, anywhere, anywhere],
        out_specs=(vmem, vmem),
        scratch_shapes=[line, line, pltpu.SemaphoreType.DMA((2,))],
        compiler_params=pltpu.CompilerParams(vmem_limit_bytes=4 * MIB),
        name="pair_sum",
    )(side, keep.reshape(count, 2, chunk, 128), theirs.reshape(count, 2, chunk, 128))
    theirs = lax.ppermute(send, axes, [(i, i ^ 2) for i in range(devices)])
    gone = {}

    def tie(values, steps):
        tied, *some = lax.optimization_barrier((values, *[gone[step] for step in steps if step in gone]))
        gone.update(zip([step for step in steps if step in gone], some))
        return tied

    if direct:
        for step in range(1, count):
            gone[step] = lax.ppermute(back[step], "pix", [(i, (i - step) % count) for i in range(count)])
    theirs = tie(theirs, FIRST)
    line = pltpu.VMEM((count, chunk, 128), BF)
    paired = pl.pallas_call(
        quad_sum_kernel,
        out_shape=quarter,
        in_specs=[anywhere, anywhere],
        out_specs=vmem,
        scratch_shapes=[line, line, pltpu.SemaphoreType.DMA((2,))],
        compiler_params=pltpu.CompilerParams(vmem_limit_bytes=4 * MIB),
        name="quad_sum",
    )(keep, theirs)
    if direct:
        returned = []
    else:
        turn = (pix - jnp.arange(count)) % count
        blocks = lax.all_to_all(
            back[0].reshape(count, cap, VIS, width)[turn], "pix", split_axis=0, concat_axis=0, tiled=True
        )
        returned = [blocks[(pix + jnp.arange(count)) % count].reshape(count * cap, VIS, width)]
    parts = lax.all_to_all(paired, "pix", split_axis=0, concat_axis=0, tiled=True)
    spread = pl.pallas_call(
        chunk_sum_kernel,
        out_shape=jax.ShapeDtypeStruct((half, chunk, 128), BF),
        in_specs=[anywhere],
        out_specs=anywhere,
        scratch_shapes=[line, pltpu.VMEM((chunk, 128), BF), pltpu.SemaphoreType.DMA((half,))],
        compiler_params=pltpu.CompilerParams(vmem_limit_bytes=4 * MIB),
        name="chunk_sum",
    )(parts)
    spread = tie(spread, MIDDLE)
    summed = tie(exchange(spread).reshape(half * chunk, 128), LAST)
    if direct:
        returned = [back[0]] + [gone[step] for step in range(1, count)]
    other = lax.ppermute(summed, axes, swap)
    small = ((4, width), (4, width), b_up.shape, b_down.shape, (1, width), pos_table.shape)
    large = tuple(w.shape for w in (w_qkv, w_out, w_up, w_down))
    gain, bias, bup, bdown, mask, pos, qkv, out, up, down = pl.pallas_call(
        functools.partial(unpack_kernel, slots),
        out_shape=tuple(jax.ShapeDtypeStruct(shape, F32) for shape in small + large),
        in_specs=[smem, anywhere, anywhere],
        out_specs=(vmem,) * 6 + (anywhere,) * 4,
        scratch_shapes=[pltpu.VMEM(shape, F32) for shape in large]
        + [pltpu.VMEM((2, half * chunk, 128), BF), pltpu.SemaphoreType.DMA((10,))],
        compiler_params=pltpu.CompilerParams(vmem_limit_bytes=8 * MIB),
        name="unpack",
    )(core, summed, other)
    grad_tokens = pl.pallas_call(
        functools.partial(restore_kernel, cap, count, len(returned)),
        out_shape=jax.ShapeDtypeStruct((pixels * slots, width), F32),
        in_specs=[smem, smem, vmem] + [anywhere] * len(returned),
        out_specs=anywhere,
        scratch_shapes=[
            pltpu.VMEM((count * cap, VIS, width), BF),
            pltpu.VMEM((2 * GROUP * VIS, width), F32),
            pltpu.VMEM((pixels * slots, width), F32),
            pltpu.SemaphoreType.DMA((len(returned) + 1,)),
        ],
        compiler_params=pltpu.CompilerParams(vmem_limit_bytes=8 * MIB),
        name="restore",
    )(me, route, pos_rows, *returned)
    return (
        dec,
        grad_tokens.reshape(pixels, slots, width),
        gain.reshape(norm_gain.shape),
        bias.reshape(norm_bias.shape),
        qkv,
        out,
        up,
        bup,
        down,
        bdown,
        mask.reshape(width),
        pos,
    )


def solution(mesh):
    rows = P(("pix", "rep"))
    in_specs = (rows,) * 5 + (P(),) * 10 + (rows,)
    out_specs = (rows, rows) + (P(),) * 10
    return jax.shard_map(shards, mesh=mesh, in_specs=in_specs, out_specs=out_specs, check_vma=False)
```

```python
import functools

import jax
import jax.numpy as jnp
from jax import lax
from jax.experimental import pallas as pl
from jax.experimental.pallas import tpu as pltpu
from jax.sharding import PartitionSpec as P

HEADS = 8
HEAD_DIM = 16
FOLD = 4
BATCH = 16
PAIRS = 16
ENC_ROWS = 256
SETS = 2
PLACES = (0.0, 1.0, 2.0, 3.0, 4.0)
VIS = 8
GROUP = 16
PAD = 32
CHUNK = 48
FIRST = (4,)
MIDDLE = (1, 2, 3, 5, 6, 7)
LAST = ()
EPS = 1e-05
NEG = -1e30
BF = jnp.bfloat16
F32 = jnp.float32
MIB = 1024 * 1024


def nn(left, right):
    return jnp.dot(left, right, preferred_element_type=F32)


def nt(left, right):
    return lax.dot_general(left, right, (((1,), (1,)), ((), ())), preferred_element_type=F32)


def tn(left, right):
    return lax.dot_general(left, right, (((0,), (0,)), ((), ())), preferred_element_type=F32)


def iota(shape, dim):
    return lax.broadcasted_iota(jnp.int32, shape, dim)


def fold_rows(values):
    rows = values.shape[0]
    return jnp.sum(values.reshape(rows // 8, 8, values.shape[1]), axis=0)


def erf_parts(hidden):
    size = jnp.abs(hidden)
    base = 1.0 + size * (0.3275911 * 0.7071067811865476)
    t = 1.0 / base
    bell = jnp.exp2(hidden * hidden * (-0.5 * 1.4426950408889634))
    poly = t * (
        0.5 * 0.254829592
        + t * (0.5 * -0.284496736 + t * (0.5 * 1.421413741 + t * (0.5 * -1.453152027 + t * (0.5 * 1.061405429))))
    )
    tail = poly * bell
    return jnp.where(hidden >= 0, 1.0 - tail, tail), bell


def expand(rows, masks):
    count = rows.shape[0]
    return jnp.concatenate([rows * masks[h, :count, :] for h in range(HEADS)], axis=0)


def fold_heads(rows, step, count):
    lane = iota((count, 128), 1)
    picked = rows[0:count]
    for head in range(1, HEADS):
        picked = jnp.where(lane >= head * HEAD_DIM, rows[head * step : head * step + count], picked)
    return picked


def fold_halves(rows, step, count):
    lane = iota((count, 128), 1) // HEAD_DIM % FOLD
    picked = rows[0:count]
    for head in range(1, FOLD):
        picked = jnp.where(lane == head, rows[head * step : head * step + count], picked)
    return picked


def expand_halves(rows, masks):
    return jnp.concatenate([rows * masks[h] for h in range(FOLD)], axis=0)


def stack_halves(values):
    low = iota(values.shape, 1) < 64
    return jnp.concatenate([jnp.where(low, values, 0.0), jnp.where(low, 0.0, values)], axis=0).astype(BF)


def join_halves(values):
    count = values.shape[0] // 2
    return jnp.where(iota((count, 128), 1) < 64, values[:count], values[count:])


def both_diagonals(values, rows):
    return values[:rows, :128], values[rows:, 128:]


def block_diagonal(first, second):
    low = jnp.concatenate([first, jnp.zeros_like(first)], axis=1)
    return jnp.concatenate([low, jnp.concatenate([jnp.zeros_like(second), second], axis=1)], axis=0)


def pair_nt(rows, columns):
    full = nt(jnp.concatenate(rows, axis=0), jnp.concatenate(columns, axis=0))
    return both_diagonals(full, rows[0].shape[0])


def pair_nn(rows, columns):
    full = nn(jnp.concatenate(rows, axis=0), jnp.concatenate(columns, axis=1))
    return both_diagonals(full, rows[0].shape[0])


def pair_tn(rows, columns):
    full = tn(jnp.concatenate(rows, axis=0), block_diagonal(*columns))
    return full[:, :128], full[:, 128:]


def with_bias(rows, grad):
    full = nn(jnp.concatenate([rows.T, jnp.ones((16, rows.shape[0]), BF)], axis=0), grad)
    return full[:-16], full[-8:]


def softmax_halves(scores, keep):
    count = scores.shape[0] // 2
    scores = jnp.where(keep[None], scores.reshape(2, count, 128), NEG)
    powers = jnp.exp(scores - jnp.max(scores, axis=1, keepdims=True))
    probs = powers * (1.0 / jnp.sum(powers, axis=1, keepdims=True))
    return probs.reshape(2 * count, 128)


def soft_bwd_halves(probs, grad):
    count = probs.shape[0] // 2
    both = (grad * probs).reshape(2, count, 128)
    lean = jnp.sum(both, axis=1, keepdims=True)
    return (probs.reshape(2, count, 128) * (grad.reshape(2, count, 128) - lean)).reshape(2 * count, 128).astype(BF)


def ln_fwd(values, gain, bias, hat, inv, low, where):
    centred = values - jnp.mean(values, axis=-1, keepdims=True)
    scale = lax.rsqrt(jnp.mean(centred * centred, axis=-1, keepdims=True) + EPS)
    unit = centred * scale
    hat[where] = unit
    inv[where] = jnp.broadcast_to(scale, unit.shape)
    low[where] = (unit * gain + bias).astype(BF)


def ln_bwd(grad, gain, hat, inv, where):
    unit = hat[where]
    inner = grad * gain
    lean = jnp.sum(inner, axis=-1, keepdims=True)
    tilt = jnp.sum(inner * unit, axis=-1, keepdims=True)
    return inv[where] * (inner - (lean + unit * tilt) * (1.0 / unit.shape[-1])), fold_rows(grad * unit), fold_rows(grad)


def prep_kernel(
    cap, extra, count, me_ref, dest_ref, tokens_ref, len_ref, masked_ref, dest_row_ref,
    payload_ref, pos_ref, route_ref, tally,
):
    slots, pixels = masked_ref.shape
    groups = pixels // GROUP
    block = cap + extra
    wide = GROUP * slots
    lanes = GROUP * VIS
    lens = len_ref[...].astype(F32)
    seen = (masked_ref[...] == 0) & (iota((slots, pixels), 0).astype(F32) < lens)
    seen_low = jnp.where(seen, 1.0, 0.0).astype(BF)
    earlier = jnp.where(iota((slots, slots), 1) < iota((slots, slots), 0), 1.0, 0.0).astype(BF)
    member = iota((slots, pixels), 1) % GROUP
    code = jnp.where(seen, nn(earlier, seen_low) + (member * VIS).astype(F32), -1.0)
    spread = jnp.where(iota((slots, wide), 0) == iota((slots, wide), 1) % slots, 1.0, 0.0).astype(BF)
    code_wide = tn(code.astype(BF), spread)
    own = iota((pixels, wide), 0) % GROUP == iota((pixels, wide), 1) // slots
    code_row = jnp.sum(jnp.where(own, code_wide, 0.0).reshape(groups, GROUP, wide), axis=1)
    in_group = iota((groups, pixels), 1) // GROUP == iota((groups, pixels), 0)
    fan = iota((pixels, lanes), 0) % GROUP == iota((pixels, lanes), 1) // VIS
    fan = jnp.where(fan, 1.0, 0.0).astype(BF)
    len_rows = nn(jnp.where(in_group, lens, 0.0).astype(BF), fan)
    dest_rows = nn(jnp.where(in_group, dest_row_ref[...].astype(F32), 0.0).astype(BF), fan)
    me = me_ref[0]
    for dev in range(count):
        tally[dev] = 0
    order = iota((lanes, wide), 0).astype(F32)
    steps = (iota((GROUP, wide), 1) % slots + 1).astype(F32).astype(BF)
    found = []
    for group in range(groups):
        select = jnp.where(order == code_row[group : group + 1, :], 1.0, 0.0).astype(BF)
        rows = nn(select, tokens_ref[group * wide : (group + 1) * wide, :]).reshape(GROUP, VIS, 128)
        found.append(nt(steps, select)[0:1, :])
        for member_id in range(GROUP):
            series = group * GROUP + member_id
            dest = dest_ref[series]
            rank = tally[dest]
            tally[dest] = rank + 1
            sender = lax.rem(2 * me - dest + 2 * count, count)
            route_ref[series] = sender * 256 + rank
            payload_ref[dest * block + rank] = rows[member_id].astype(BF)
    pos_rows = jnp.concatenate(found, axis=0)
    pos_ref[...] = pos_rows

    def label(dev, carry):
        mine = dest_rows == dev.astype(F32)
        payload_ref[dev * block + cap] = jnp.where(mine, pos_rows, 0.0).astype(BF)
        payload_ref[dev * block + cap + 1] = jnp.where(mine, len_rows, 0.0).astype(BF)
        return carry

    lax.fori_loop(0, count, label, 0)


def prep(tokens, lengths, masked, route_dev, count, cap, extra, me):
    pixels, slots, width = tokens.shape
    smem = pl.BlockSpec(memory_space=pltpu.SMEM)
    vmem = pl.BlockSpec(memory_space=pltpu.VMEM)
    index = jax.ShapeDtypeStruct((pixels,), jnp.int32)
    return pl.pallas_call(
        functools.partial(prep_kernel, cap, extra, count),
        out_shape=(
            jax.ShapeDtypeStruct((count * (cap + extra), VIS, width), BF),
            jax.ShapeDtypeStruct((pixels // GROUP, GROUP * VIS), F32),
            index,
        ),
        in_specs=[smem, smem, vmem, vmem, vmem, vmem],
        out_specs=(vmem, vmem, smem),
        scratch_shapes=[pltpu.SMEM((count,), jnp.int32)],
        compiler_params=pltpu.CompilerParams(vmem_limit_bytes=56 * MIB),
        name="prep",
    )(
        me, route_dev, tokens.reshape(pixels * slots, width), lengths.reshape(1, pixels), masked.T,
        route_dev.reshape(1, pixels),
    )


class Box:
    pass


def offset_place(route, me, count, cap):
    return lax.rem(me - (route >> 8) + count, count) * cap + (route & 255)


def gelu_stage(hidden, b_up, act, slope, base, rows):
    for start in range(0, rows, 16):
        value = hidden[start : start + 16] + b_up
        cdf, bell = erf_parts(value)
        where = pl.ds(base + start, 16)
        act[where] = (value * cdf).astype(BF)
        slope[where] = cdf + value * bell * 0.3989422804014327


def slope_stage(grad_act, slope, out, base, rows):
    total = None
    for start in range(0, rows, 16):
        part = (grad_act[start : start + 16] * slope[pl.ds(base + start, 16)]).astype(BF)
        out[pl.ds(start, 16)] = part
        summed = fold_rows(part.astype(F32))
        total = summed if total is None else total + summed
    return total


def softmax_rows(scores, keep):
    scores = jnp.where(keep, scores, NEG)
    powers = jnp.exp(scores - jnp.max(scores, axis=0, keepdims=True))
    return powers / jnp.sum(powers, axis=0, keepdims=True)


def soft_bwd(probs, grad):
    return (probs * (grad - jnp.sum(grad * probs, axis=0, keepdims=True))).astype(BF)


class Encoder:
    def __init__(self, b, base, rows):
        self.b, self.base, self.rows = b, base, rows
        self.whole = slice(base, base + rows)

    def chunks(self):
        return [slice(start, start + 32) for start in range(self.base, self.base + self.rows, 32)]

    def part(self, values, where):
        return values[where.start - self.base : where.stop - self.base]

    def attend(self):
        b, w, whole = self.b, self.b.w, self.whole
        v = Box()
        same = iota((16, 128), 0) // VIS == (iota((16, 128), 1) % 16) // VIS

        def load(series):
            b.e_x[series * VIS : (series + 1) * VIS] = b.recv[b.take(series)].astype(F32)

        steps = [functools.partial(load, series) for series in range(self.base // VIS, (self.base + self.rows) // VIS)]

        def norm(where):
            ln_fwd(b.e_x[where], w.gain[0:1], w.bias[0:1], b.e_hat1, b.e_inv1, b.e_n1, where)

        steps += [functools.partial(norm, where) for where in self.chunks()]

        def project():
            v.qkv = nn(b.e_n1[whole], w.qkv[0])
            v.score, v.prob, v.mixed = {}, {}, {}

        steps.append(project)

        def split(where):
            part = self.part(v.qkv, where)
            b.e_qkv[where, 0:128] = (part[:, 0:128] * 0.25).astype(BF)
            b.e_qkv[where, 128:384] = part[:, 128:384].astype(BF)

        steps += [functools.partial(split, where) for where in self.chunks()]

        def score(at):
            pair = (at, at + 16)
            queries = [expand(b.e_qkv[one : one + 16, 0:128], b.masks) for one in pair]
            keys = [b.e_qkv[one : one + 16, 128:256] for one in pair]
            v.score[at], v.score[at + 16] = pair_nt(keys, queries)

        def soft(at):
            v.prob[at] = softmax_rows(v.score[at], same & (b.pos_col[at : at + 16] > 0))
            b.e_probs[at : at + 16] = v.prob[at]

        def mix(at):
            pair = (at, at + 16)
            values = [b.e_qkv[one : one + 16, 256:384] for one in pair]
            v.mixed[at], v.mixed[at + 16] = pair_tn([v.prob[one].astype(BF) for one in pair], values)

        def gather(at):
            b.e_att[at : at + 16] = fold_heads(v.mixed[at], 16, 16).astype(BF)

        for first in range(self.base, self.base + self.rows, 16 * PAIRS):
            for stage, stride in ((score, 32), (soft, 16), (mix, 32), (gather, 16)):
                steps += [functools.partial(stage, at) for at in range(first, first + 16 * PAIRS, stride)]

        def out():
            v.proj = nn(b.e_att[whole], w.out[0])

        steps.append(out)

        def second(where):
            middle = b.e_x[where] + self.part(v.proj, where)
            b.e_x[where] = middle
            ln_fwd(middle, w.gain[1:2], w.bias[1:2], b.e_hat2, b.e_inv2, b.e_n2, where)

        steps += [functools.partial(second, where) for where in self.chunks()]
        return steps

    def bend(self):
        b, w, whole = self.b, self.b.w, self.whole
        v = Box()

        def up():
            v.hidden = nn(b.e_n2[whole], w.up[0])

        def curve(start):
            value = v.hidden[start : start + 16] + w.b_up[0:1]
            cdf, bell = erf_parts(value)
            where = slice(self.base + start, self.base + start + 16)
            b.e_act[where] = (value * cdf).astype(BF)
            b.e_slope[where] = cdf + value * bell * 0.3989422804014327

        def down():
            v.down = nn(b.e_act[whole], w.down[0])

        def finish(where):
            b.sent[where] = (b.e_x[where] + self.part(v.down, where) + w.b_down[0:1]).astype(BF)

        return (
            [up]
            + [functools.partial(curve, start) for start in range(0, self.rows, 16)]
            + [down]
            + [functools.partial(finish, where) for where in self.chunks()]
        )

    def feed(self):
        b, whole = self.b, self.whole
        v = Box()

        def back():
            grad_low = b.g_sent[whole]
            b.d_down[0] += tn(grad_low, b.e_act[whole])
            b.d_b_down[0] += fold_rows(grad_low.astype(F32))
            v.grad_act = nn(grad_low, b.down_t[0])

        def unbend(start):
            where = slice(self.base + start, self.base + start + 16)
            b.e_gh[where] = (v.grad_act[start : start + 16] * b.e_slope[where]).astype(BF)

        def end():
            weights, bias = with_bias(b.e_n2[whole], b.e_gh[whole])
            b.d_up[0] += weights
            b.d_b_up[0] += bias
            b.e_gn2[whole] = nn(b.e_gh[whole], b.up_t[0])

        return [back] + [functools.partial(unbend, start) for start in range(0, self.rows, 16)] + [end]

    def retreat(self):
        b, w, whole = self.b, self.b.w, self.whole
        v = Box()

        def norm(where):
            grad, gain_part, bias_part = ln_bwd(b.e_gn2[where], w.gain[1:2], b.e_hat2, b.e_inv2, where)
            b.d_gain[1] += gain_part
            b.d_bias[1] += bias_part
            grad = grad + b.g_sent[where].astype(F32)
            b.e_gm[where] = grad
            b.e_gml[where] = grad.astype(BF)

        steps = [functools.partial(norm, where) for where in self.chunks()]

        def out():
            b.d_out[0] += tn(b.e_att[whole], b.e_gml[whole])
            v.grad_att = nn(b.e_gml[whole], b.out_t[0])
            v.grad, v.grad_p, v.grad_s, v.grad_v, v.grad_k, v.grad_q = ({} for _ in range(6))

        steps.append(out)

        def spread(at):
            pair = (at, at + 16)
            for one in pair:
                low = v.grad_att[one - self.base : one - self.base + 16].astype(BF)
                v.grad[one] = expand(low, b.masks)
            values = [b.e_qkv[one : one + 16, 256:384] for one in pair]
            v.grad_p[at], v.grad_p[at + 16] = pair_nt(values, [v.grad[one] for one in pair])

        def values(at):
            pair = (at, at + 16)
            probs = [b.e_probs[one : one + 16].astype(BF) for one in pair]
            v.grad_v[at], v.grad_v[at + 16] = pair_nn(probs, [v.grad[one] for one in pair])

        def soft(at):
            v.grad_s[at] = soft_bwd(b.e_probs[at : at + 16], v.grad_p[at])

        def keys(at):
            pair = (at, at + 16)
            columns = [expand(b.e_qkv[one : one + 16, 0:128], b.masks) for one in pair]
            v.grad_k[at], v.grad_k[at + 16] = pair_nn([v.grad_s[one] for one in pair], columns)

        def queries(at):
            pair = (at, at + 16)
            keys = [b.e_qkv[one : one + 16, 128:256] for one in pair]
            v.grad_q[at], v.grad_q[at + 16] = pair_tn([v.grad_s[one] for one in pair], keys)

        def gather(at):
            b.e_gqkv[at : at + 16, 256:384] = v.grad_v[at].astype(BF)
            b.e_gqkv[at : at + 16, 128:256] = v.grad_k[at].astype(BF)
            b.e_gqkv[at : at + 16, 0:128] = (fold_heads(v.grad_q[at], 16, 16) * 0.25).astype(BF)

        for first in range(self.base, self.base + self.rows, 16 * PAIRS):
            for stage, stride in ((spread, 32), (values, 32), (soft, 16), (keys, 32), (queries, 32), (gather, 16)):
                steps += [functools.partial(stage, at) for at in range(first, first + 16 * PAIRS, stride)]

        def project():
            b.d_qkv[0] += tn(b.e_n1[whole], b.e_gqkv[whole])
            v.grad_n1 = nn(b.e_gqkv[whole], b.qkv_t[0])

        steps.append(project)

        def first_norm(where):
            grad, gain_part, bias_part = ln_bwd(
                self.part(v.grad_n1, where), w.gain[0:1], b.e_hat1, b.e_inv1, where
            )
            b.d_gain[0] += gain_part
            b.d_bias[0] += bias_part
            grad = grad + b.e_gm[where]
            for series in range(where.start // VIS, where.stop // VIS):
                at = series * VIS - where.start
                b.back[b.back_at(series)] = grad[at : at + VIS].astype(BF)

        steps += [functools.partial(first_norm, where) for where in self.chunks()]
        return steps


def weave(timeline):
    order = []
    for which, (start, length, steps) in enumerate(timeline):
        order += [(start + length * (index + 0.5) / len(steps), which, step) for index, step in enumerate(steps)]
    for _, _, step in sorted(order, key=lambda entry: entry[:2]):
        step()


class Decoder:
    def __init__(self, b, d, group):
        self.b, self.d, self.group = b, d, group
        self.slots = b.slots
        self.rows = GROUP * b.slots
        self.sent_rows = pl.ds(pl.multiple_of(group * 128, 128), 128)
        self.zeros = jnp.zeros((PAD - b.slots, 128), F32)
        self.step = iota((b.slots, 128), 0).astype(F32)

    def span(self, member):
        return pl.ds(member * self.slots, self.slots)

    def cut(self, member):
        return slice(member * self.slots, (member + 1) * self.slots)

    def inside(self, member):
        lens = self.b.len_col[pl.ds(pl.multiple_of(self.group * 128, 128) + member * VIS, VIS)]
        return self.step < jnp.concatenate([lens] * (self.slots // VIS), axis=0)

    def padded(self, values):
        return jnp.concatenate([values, self.zeros], axis=0).astype(BF)

    def chunks(self):
        return range(0, self.rows, CHUNK)

    def attend(self):
        b, d, w, slots = self.b, self.d, self.b.w, self.slots
        v = Box()
        steps = []

        def begin():
            pos_row = b.pos_row[self.group]
            lane = iota((1, 128), 1)
            target = jnp.where(pos_row > 0, (lane // VIS * slots).astype(F32) + pos_row - 1.0, -1.0)
            for start in self.chunks():
                spot = (iota((CHUNK, 128), 0) + start).astype(F32)
                d.hot[pl.ds(start, CHUNK)] = jnp.where(spot == target, 1.0, 0.0).astype(BF)
            both = jnp.concatenate([b.sent[self.sent_rows], jnp.ones((128, 128), BF)], axis=1)
            full = nn(d.hot[...], both)
            v.placed, v.shown = full[:, 0:128], full[:, 128:256]

        steps.append(begin)

        def assemble(member):
            at = self.cut(member)
            hidden_part = 1.0 - v.shown[at]
            d.unseen[self.span(member)] = hidden_part
            d.x[self.span(member)] = v.placed[at] + hidden_part * w.mask[...] + w.pos[...]
            cot = b.cot[b.slot[self.group * GROUP + member]].astype(F32)
            d.g[self.span(member)] = jnp.where(self.inside(member), cot, 0.0)

        steps += [functools.partial(assemble, member) for member in range(GROUP)]

        def norm(start):
            where = pl.ds(start, CHUNK)
            ln_fwd(d.x[where], w.gain[2:3], w.bias[2:3], d.hat1, d.inv1, d.n1, where)

        steps += [functools.partial(norm, start) for start in self.chunks()]

        def project():
            v.qkv = nn(d.n1[...], w.qkv[1])
            v.score, v.prob, v.mixed = {}, {}, {}

        steps.append(project)

        def split(member):
            at = self.cut(member)
            d.q[member] = self.padded(v.qkv[at, 0:128] * 0.25)
            d.k[member] = stack_halves(v.qkv[at, 128:256])
            d.v[member] = stack_halves(v.qkv[at, 256:384])

        def score(member):
            pair = (member, member + 1)
            queries = [expand_halves(d.q[one], b.masks_half) for one in pair]
            v.score[member], v.score[member + 1] = pair_nt([d.k[one] for one in pair], queries)

        def soft(member):
            v.prob[member] = softmax_halves(v.score[member], self.inside(member))
            d.probs[member] = v.prob[member]

        def mix(member):
            pair = (member, member + 1)
            mixed = pair_tn([v.prob[one].astype(BF) for one in pair], [d.v[one] for one in pair])
            v.mixed[member], v.mixed[member + 1] = mixed

        def gather(member):
            d.att32[self.span(member)] = fold_halves(v.mixed[member], PAD, slots)

        for first in range(0, GROUP, BATCH):
            for stage, stride in ((split, 1), (score, 2), (soft, 1), (mix, 2), (gather, 1)):
                steps += [functools.partial(stage, member) for member in range(first, first + BATCH, stride)]

        def low(start):
            where = pl.ds(start, CHUNK)
            d.att[where] = d.att32[where].astype(BF)

        steps += [functools.partial(low, start) for start in self.chunks()]

        def out():
            v.proj = nn(d.att[...], w.out[1])

        steps.append(out)

        def second(start):
            where = pl.ds(start, CHUNK)
            middle = d.x[where] + v.proj[start : start + CHUNK]
            d.x[where] = middle
            ln_fwd(middle, w.gain[3:4], w.bias[3:4], d.hat2, d.inv2, d.n2, where)

        steps += [functools.partial(second, start) for start in self.chunks()]
        return steps

    def bend(self):
        b, d, w = self.b, self.d, self.b.w
        v = Box()
        steps = []

        def up():
            v.hidden = nn(d.n2[...], w.up[1])

        steps.append(up)

        def curve(start):
            value = v.hidden[start : start + 16] + w.b_up[1:2]
            cdf, bell = erf_parts(value)
            where = pl.ds(start, 16)
            d.act[where] = (value * cdf).astype(BF)
            d.slope[where] = cdf + value * bell * 0.3989422804014327

        steps += [functools.partial(curve, start) for start in range(0, self.rows, 16)]
        return steps

    def feed(self):
        b, d, w = self.b, self.d, self.b.w
        v = Box()
        steps = []

        def down():
            v.down = nn(d.act[...], w.down[1])

        steps.append(down)

        def finish(member):
            value = d.x[self.span(member)] + v.down[self.cut(member)] + w.b_down[1:2]
            slot = b.slot[self.group * GROUP + member]
            b.dec[slot] = jnp.where(self.inside(member), value, 0.0)
            pltpu.make_async_copy(b.dec.at[slot], b.dec_out.at[slot], b.sems.at[1]).start()

        steps += [functools.partial(finish, member) for member in range(GROUP)]

        def low(start):
            where = pl.ds(start, CHUNK)
            d.gl[where] = d.g[where].astype(BF)

        steps += [functools.partial(low, start) for start in self.chunks()]

        def back():
            v.grad_act = nn(d.gl[...], b.down_t[1])

        def weights_down():
            b.d_down[1] += tn(d.gl[...], d.act[...])
            b.d_b_down[1] += fold_rows(d.g[...])

        steps.append(back)

        def unbend(start):
            d.gh[pl.ds(start, 16)] = (v.grad_act[start : start + 16] * d.slope[pl.ds(start, 16)]).astype(BF)

        bends = [functools.partial(unbend, start) for start in range(0, self.rows, 16)]
        steps += bends[:4] + [weights_down] + bends[4:]

        def end():
            d.gn2[...] = nn(d.gh[...], b.up_t[1])

        def weights_up():
            weights, bias = with_bias(d.n2[...], d.gh[...])
            b.d_up[1] += weights
            b.d_b_up[1] += bias

        steps += [end, weights_up]
        return steps

    def retreat(self):
        b, d, w, slots = self.b, self.d, self.b.w, self.slots
        v = Box()
        steps = []

        def norm(start):
            where = pl.ds(start, CHUNK)
            grad, gain_part, bias_part = ln_bwd(d.gn2[where], w.gain[3:4], d.hat2, d.inv2, where)
            b.d_gain[3] += gain_part
            b.d_bias[3] += bias_part
            grad = grad + d.g[where]
            d.g[where] = grad
            d.gl[where] = grad.astype(BF)

        steps += [functools.partial(norm, start) for start in self.chunks()]

        def weights_out():
            b.d_out[1] += tn(d.att[...], d.gl[...])

        def out():
            v.grad_att = nn(d.gl[...], b.out_t[1])
            v.grad, v.prob, v.grad_p, v.grad_s, v.grad_v, v.grad_k, v.grad_q = ({} for _ in range(7))

        steps.append(out)

        def spread(member):
            pair = (member, member + 1)
            for one in pair:
                v.grad[one] = expand_halves(self.padded(v.grad_att[self.cut(one)]), b.masks_half)
            grads = [v.grad[one] for one in pair]
            v.grad_p[member], v.grad_p[member + 1] = pair_nt([d.v[one] for one in pair], grads)

        def values(member):
            pair = (member, member + 1)
            probs = [d.probs[one].astype(BF) for one in pair]
            v.grad_v[member], v.grad_v[member + 1] = pair_nn(probs, [v.grad[one] for one in pair])

        def soft(member):
            v.grad_s[member] = soft_bwd_halves(d.probs[member], v.grad_p[member])

        def keys(member):
            pair = (member, member + 1)
            columns = [expand_halves(d.q[one], b.masks_half) for one in pair]
            v.grad_k[member], v.grad_k[member + 1] = pair_nn([v.grad_s[one] for one in pair], columns)

        def queries(member):
            pair = (member, member + 1)
            grads = pair_tn([v.grad_s[one] for one in pair], [d.k[one] for one in pair])
            v.grad_q[member], v.grad_q[member + 1] = grads

        def gather(member):
            d.gqkv32[self.span(member), 256:384] = join_halves(v.grad_v[member])
            d.gqkv32[self.span(member), 128:256] = join_halves(v.grad_k[member])
            d.gqkv32[self.span(member), 0:128] = fold_halves(v.grad_q[member], PAD, slots) * 0.25

        for first in range(0, GROUP, BATCH):
            for stage, stride in ((spread, 2), (values, 2), (soft, 1), (keys, 2), (queries, 2), (gather, 1)):
                steps += [functools.partial(stage, member) for member in range(first, first + BATCH, stride)]
                if stage is soft and first == 0:
                    steps.append(weights_out)

        def low(start):
            where = pl.ds(start, CHUNK)
            d.gqkv[where] = d.gqkv32[where].astype(BF)

        steps += [functools.partial(low, start) for start in self.chunks()]

        def weights_qkv():
            b.d_qkv[1] += tn(d.n1[...], d.gqkv[...])

        def project():
            v.grad_n1 = nn(d.gqkv[...], b.qkv_t[1])
            v.pos = None

        steps.append(project)

        def first_norm(start):
            where = pl.ds(start, CHUNK)
            grad, gain_part, bias_part = ln_bwd(
                v.grad_n1[start : start + CHUNK], w.gain[2:3], d.hat1, d.inv1, where
            )
            b.d_gain[2] += gain_part
            b.d_bias[2] += bias_part
            grad = grad + d.g[where]
            d.gl[where] = grad.astype(BF)
            part = jnp.sum(grad.reshape(CHUNK // slots, slots, 128), axis=0)
            v.pos = part if v.pos is None else v.pos + part
            b.d_mask[...] += fold_rows(grad * d.unseen[where])

        steps.append(weights_qkv)
        steps += [functools.partial(first_norm, start) for start in self.chunks()]

        def end():
            b.d_pos[...] += v.pos
            b.g_sent[self.sent_rows] = tn(d.hot[...], d.gl[...]).astype(BF)

        steps.append(end)
        return steps


def plan(b, groups, encoders, before_first):
    timeline = []
    for index in range(groups):
        decoder = Decoder(b, b.sets[index % SETS], index)
        phases = (decoder.attend, decoder.bend, decoder.feed, decoder.retreat)
        for start, stop, phase in zip(PLACES, PLACES[1:], phases):
            timeline.append((2 * index + start, stop - start, phase()))
    timeline.append((-0.01, 0.01, [before_first]))
    for chunk in encoders:
        first, last = chunk.base // (GROUP * VIS), (chunk.base + chunk.rows) // (GROUP * VIS) - 1
        early = 2 * first - (4 if first else 2)
        room = (2 * first - early) / 2
        timeline.append((early, room, chunk.attend()))
        timeline.append((early + room, room, chunk.bend()))
        late = 2 * last + PLACES[-1]
        room = 2 if last < groups - 1 else 1
        timeline.append((late, room, chunk.feed()))
        timeline.append((late + room, room, chunk.retreat()))
    return timeline


IN_NAMES = (
    "core", "me", "route", "slot", "recv_in", "cot_in", "w_qkv", "w_out", "w_up", "w_down", "b_up", "b_down",
    "gain", "bias", "mask", "pos",
)
OUT_NAMES = ("dec_out", "keep", "send")


def small_rows(slots):
    return 18 + 1 + slots


def main_kernel(names, cap, extra, count, outs, *refs):
    b = Box()
    b.sets = tuple(Box() for _ in range(SETS))
    b.back_out = refs[len(IN_NAMES) + len(OUT_NAMES) : len(IN_NAMES) + len(OUT_NAMES) + outs]
    refs = refs[: len(IN_NAMES) + len(OUT_NAMES)] + refs[len(IN_NAMES) + len(OUT_NAMES) + outs :]
    for name, ref in zip(names, refs, strict=True):
        name, _, side = name.partition("@")
        setattr(b.sets[int(side)] if side else b, name, ref)
    b.w = Box()
    for name in ("qkv", "out", "up", "down"):
        setattr(b.w, name, getattr(b, "w_" + name))
    for name in ("b_up", "b_down", "gain", "bias", "mask", "pos"):
        setattr(b.w, name, getattr(b, name))
    b.slots = b.cot.shape[1]
    pixels = b.cot.shape[0]
    groups = pixels // GROUP
    block = cap + extra
    b.take = lambda series: (b.route[series] >> 8) * block + (b.route[series] & 255)
    b.back_at = lambda series: offset_place(b.route[series], b.me[0], count, cap)
    recv_copy = pltpu.make_async_copy(b.recv_in, b.recv, b.sems.at[0])
    recv_copy.start()
    cot_copy = pltpu.make_async_copy(b.cot_in, b.cot, b.sems.at[2])
    cot_copy.start()
    for head in range(HEADS):
        lane = iota((PAD, 128), 1) // HEAD_DIM
        b.masks[head] = jnp.where(lane == head, 1.0, 0.0).astype(BF)
    for head in range(FOLD):
        lane = iota((PAD, 128), 1) // HEAD_DIM % FOLD
        b.masks_half[head] = jnp.where(lane == head, 1.0, 0.0).astype(BF)
    for layer in range(2):
        b.qkv_t[layer] = b.w_qkv[layer].T
        b.out_t[layer] = b.w_out[layer].T
        b.up_t[layer] = b.w_up[layer].T
        b.down_t[layer] = b.w_down[layer].T
    for ref in (b.d_qkv, b.d_out, b.d_up, b.d_down, b.d_gain, b.d_bias, b.d_b_up, b.d_b_down, b.d_mask, b.d_pos):
        ref[...] = jnp.zeros(ref.shape, F32)

    def gather(dev, carry):
        pos, lens = carry
        return (
            pos + b.recv[dev * block + cap].astype(F32),
            lens + b.recv[dev * block + cap + 1].astype(F32),
        )

    empty = jnp.zeros((groups, 128), F32)
    recv_copy.wait()
    pos, lens = lax.fori_loop(0, count, gather, (empty, empty))
    for group in range(groups):
        where = pl.ds(group * 128, 128)
        b.pos_row[group] = pos[group : group + 1]
        b.pos_col[where] = jnp.broadcast_to(pos[group : group + 1], (128, 128)).T
        b.len_col[where] = jnp.broadcast_to(lens[group : group + 1], (128, 128)).T

    encoders = [Encoder(b, base, ENC_ROWS) for base in range(0, pixels * VIS, ENC_ROWS)]
    weave(plan(b, groups, encoders, cot_copy.wait))
    copies = []
    size = b.back.shape[0] // outs
    for index, ref in enumerate(b.back_out):
        copies.append(pltpu.make_async_copy(b.back.at[pl.ds(index * size, size)], ref, b.sems.at[5 + index]))
        copies[-1].start()

    offset = 0
    for layer in range(2):
        for start in range(0, 384, 128):
            b.grads[offset : offset + 128] = b.d_qkv[layer, :, start : start + 128].astype(BF)
            offset += 128
        b.grads[offset : offset + 128] = b.d_out[layer].astype(BF)
        offset += 128
        for start in range(0, 512, 128):
            b.grads[offset : offset + 128] = b.d_up[layer, :, start : start + 128].astype(BF)
            offset += 128
        for start in range(0, 512, 128):
            b.grads[offset : offset + 128] = b.d_down[layer, :, start : start + 128].T.astype(BF)
            offset += 128

    def total(ref, index):
        return jnp.sum(ref[index], axis=0, keepdims=True)

    small = [total(b.d_gain, i) for i in range(4)] + [total(b.d_bias, i) for i in range(4)]
    for layer in range(2):
        row = b.d_b_up[layer, 0:1]
        small += [row[:, start : start + 128] for start in range(0, 512, 128)]
    small += [total(b.d_b_down, layer) for layer in range(2)]
    small.append(jnp.sum(b.d_mask[...], axis=0, keepdims=True))
    small.append(b.d_pos[...])
    tail = jnp.concatenate(small, axis=0)
    fill = -tail.shape[0] % 16
    tail = jnp.concatenate([tail, jnp.zeros((fill, 128), F32)], axis=0)
    b.grads[offset : offset + tail.shape[0]] = tail.astype(BF)
    half = b.grads.shape[0] // 2
    mine = b.core[0]
    for side, ref, sem in ((mine, b.keep, 3), (1 - mine, b.send, 4)):
        rows = pl.ds(pl.multiple_of(side * half, half), half)
        copies.append(pltpu.make_async_copy(b.grads.at[rows], ref, b.sems.at[sem]))
        copies[-1].start()
    for copy in copies:
        copy.wait()
    pltpu.make_async_copy(b.dec, b.dec_out, b.sems.at[1]).wait()


def decoder_scratch(rows, slots):
    return {
        "hot": ((rows, 128), BF),
        "unseen": ((rows, 128), F32),
        "x": ((rows, 128), F32),
        "g": ((rows, 128), F32),
        "gl": ((rows, 128), BF),
        "hat1": ((rows, 128), F32),
        "inv1": ((rows, 128), F32),
        "n1": ((rows, 128), BF),
        "q": ((GROUP, PAD, 128), BF),
        "k": ((GROUP, 2 * slots, 128), BF),
        "v": ((GROUP, 2 * slots, 128), BF),
        "probs": ((GROUP, 2 * slots, 128), F32),
        "att32": ((rows, 128), F32),
        "att": ((rows, 128), BF),
        "hat2": ((rows, 128), F32),
        "inv2": ((rows, 128), F32),
        "n2": ((rows, 128), BF),
        "act": ((rows, 512), BF),
        "slope": ((rows, 512), F32),
        "gh": ((rows, 512), BF),
        "gn2": ((rows, 128), F32),
        "gqkv32": ((rows, 384), F32),
        "gqkv": ((rows, 384), BF),
    }


def main_call(args, cap, extra, count, grad_rows, outs):
    recv, cot = args[4], args[5]
    pixels, slots, width = cot.shape
    enc = pixels * VIS
    rows = GROUP * slots
    smem = pl.BlockSpec(memory_space=pltpu.SMEM)
    vmem = pl.BlockSpec(memory_space=pltpu.VMEM)
    anywhere = pl.BlockSpec(memory_space=pl.ANY)
    scratch = {
        "recv": (recv.shape, BF),
        "cot": (cot.shape, BF),
        "dec": (cot.shape, F32),
        "back": ((count * cap, VIS, width), BF),
        "grads": ((grad_rows, 128), BF),
        "masks": ((HEADS, PAD, 128), BF),
        "masks_half": ((FOLD, PAD, 128), BF),
        "qkv_t": ((2, 384, 128), BF),
        "out_t": ((2, 128, 128), BF),
        "up_t": ((2, 512, 128), BF),
        "down_t": ((2, 128, 512), BF),
        "d_qkv": ((2, 128, 384), F32),
        "d_out": ((2, 128, 128), F32),
        "d_up": ((2, 128, 512), F32),
        "d_down": ((2, 128, 512), F32),
        "d_gain": ((4, 8, 128), F32),
        "d_bias": ((4, 8, 128), F32),
        "d_b_up": ((2, 8, 512), F32),
        "d_b_down": ((2, 8, 128), F32),
        "d_mask": ((8, 128), F32),
        "d_pos": ((slots, 128), F32),
        "pos_row": ((pixels // GROUP, 1, 128), F32),
        "pos_col": ((enc, 128), F32),
        "len_col": ((enc, 128), F32),
        "sent": ((enc, 128), BF),
        "g_sent": ((enc, 128), BF),
        "e_x": ((enc, 128), F32),
        "e_hat1": ((enc, 128), F32),
        "e_inv1": ((enc, 128), F32),
        "e_n1": ((enc, 128), BF),
        "e_qkv": ((enc, 384), BF),
        "e_probs": ((enc, 128), F32),
        "e_att": ((enc, 128), BF),
        "e_hat2": ((enc, 128), F32),
        "e_inv2": ((enc, 128), F32),
        "e_n2": ((enc, 128), BF),
        "e_act": ((enc, 512), BF),
        "e_slope": ((enc, 512), F32),
        "e_gh": ((enc, 512), BF),
        "e_gn2": ((enc, 128), F32),
        "e_gm": ((enc, 128), F32),
        "e_gml": ((enc, 128), BF),
        "e_gqkv": ((enc, 384), BF),
    }
    for side in range(SETS):
        for name, entry in decoder_scratch(rows, slots).items():
            scratch[f"{name}@{side}"] = entry
    names = IN_NAMES + OUT_NAMES + tuple(scratch) + ("sems",)
    half = jax.ShapeDtypeStruct((grad_rows // 2, 128), BF)
    return pl.pallas_call(
        functools.partial(main_kernel, names, cap, extra, count, outs),
        out_shape=(jax.ShapeDtypeStruct((pixels, slots, width), F32), half, half)
        + (jax.ShapeDtypeStruct((count * cap // outs, VIS, width), BF),) * outs,
        in_specs=[smem] * 4 + [anywhere] * 2 + [vmem] * (len(IN_NAMES) - 6),
        out_specs=(anywhere,) * (3 + outs),
        scratch_shapes=[pltpu.VMEM(shape, kind) for shape, kind in scratch.values()]
        + [pltpu.SemaphoreType.DMA((5 + outs,))],
        compiler_params=pltpu.CompilerParams(vmem_limit_bytes=32 * MIB),
        name="layers",
    )(*args)


def fetch(pairs, sems):
    copies = [pltpu.make_async_copy(src, dst, sems.at[index]) for index, (src, dst) in enumerate(pairs)]
    for copy in copies:
        copy.start()
    return copies


def pair_sum_kernel(spot_ref, mine_ref, theirs_ref, keep_ref, send_ref, mine, theirs, sems):
    for copy in fetch([(mine_ref, mine), (theirs_ref, theirs)], sems):
        copy.wait()
    side = spot_ref[0]
    for ref, which in ((send_ref, 1 - side), (keep_ref, side)):
        ref[...] = (mine[:, which].astype(F32) + theirs[:, which].astype(F32)).astype(BF)


def quad_sum_kernel(mine_ref, theirs_ref, out_ref, mine, theirs, sems):
    for copy in fetch([(mine_ref, mine), (theirs_ref, theirs)], sems):
        copy.wait()
    out_ref[...] = (mine[...].astype(F32) + theirs[...].astype(F32)).astype(BF)


def chunk_sum_kernel(parts_ref, out_ref, parts, low, sems):
    count = parts_ref.shape[0]
    (copy,) = fetch([(parts_ref, parts)], sems)
    copy.wait()
    total = parts[0].astype(F32)
    for part in range(1, count):
        total = total + parts[part].astype(F32)
    low[...] = total.astype(BF)
    for copy in fetch([(low, out_ref.at[part]) for part in range(out_ref.shape[0])], sems):
        copy.wait()


BIG = ("qkv", "out", "up", "down")


def unpack_kernel(slots, *refs):
    (core_ref, mine_ref, theirs_ref, gain_ref, bias_ref, b_up_ref, b_down_ref, mask_ref, pos_ref) = refs[:9]
    outs = dict(zip(BIG, refs[9:13]))
    held = dict(zip(BIG, refs[13:17]))
    full, sems = refs[17:]
    core = core_ref[0]
    for copy in fetch([(mine_ref, full.at[core]), (theirs_ref, full.at[1 - core])], sems):
        copy.wait()
    half = full.shape[1]

    def rows(start, size):
        side, at = start // half, start % half
        if at + size <= half:
            return full[side, at : at + size].astype(F32)
        cut = half - at
        return jnp.concatenate(
            [full[side, at:half].astype(F32), full[side + 1, 0 : size - cut].astype(F32)], axis=0
        )

    offset = 0
    copies = []

    def leave(name, layer):
        copy = pltpu.make_async_copy(held[name].at[layer], outs[name].at[layer], sems.at[2 + len(copies)])
        copy.start()
        copies.append(copy)

    for layer in range(2):
        for start in range(0, 384, 128):
            held["qkv"][layer, :, start : start + 128] = rows(offset, 128)
            offset += 128
        leave("qkv", layer)
        held["out"][layer] = rows(offset, 128)
        offset += 128
        leave("out", layer)
        for start in range(0, 512, 128):
            held["up"][layer, :, start : start + 128] = rows(offset, 128)
            offset += 128
        leave("up", layer)
        for start in range(0, 512, 128):
            held["down"][layer, start : start + 128, :] = rows(offset, 128)
            offset += 128
        leave("down", layer)
    count = small_rows(slots)
    small = rows(offset, count + (-count % 16))
    gain_ref[...] = small[0:4]
    bias_ref[...] = small[4:8]
    for layer in range(2):
        for part in range(4):
            at = 8 + 4 * layer + part
            b_up_ref[layer : layer + 1, part * 128 : (part + 1) * 128] = small[at : at + 1]
    b_down_ref[...] = small[16:18]
    mask_ref[...] = small[18:19]
    pos_ref[...] = small[19 : 19 + slots]
    for copy in copies:
        copy.wait()


def restore_kernel(cap, steps, count, spot_ref, route_ref, pos_ref, *refs):
    blocks, (out_ref, rows, held, out, sems) = refs[:count], refs[count:]
    size = rows.shape[0] // count
    copies = fetch([(ref, rows.at[pl.ds(index * size, size)]) for index, ref in enumerate(blocks)], sems)
    groups = pos_ref.shape[0]
    wide = out.shape[0] // groups
    slots = wide // GROUP
    lane = iota((1, 128), 1)
    for copy in copies:
        copy.wait()
    for group in range(groups):
        for member in range(GROUP):
            block = rows[offset_place(route_ref[group * GROUP + member], spot_ref[0], steps, cap)]
            held[pl.ds((group % 2) * 128 + member * VIS, VIS)] = block.astype(F32)
        pos_row = pos_ref[group : group + 1]
        target = jnp.where(pos_row > 0, (lane // VIS * slots).astype(F32) + pos_row - 1.0, -1.0)
        hot = jnp.where(iota((wide, 128), 0).astype(F32) == target, 1.0, 0.0).astype(BF)
        where = pl.ds(group * wide, wide)
        out[where] = nn(hot, held[pl.ds((group % 2) * 128, 128)].astype(BF))
        pltpu.make_async_copy(out.at[where], out_ref.at[where], sems.at[count]).start()
    pltpu.make_async_copy(out, out_ref, sems.at[count]).wait()


def shards(
    tokens, lengths, masked, route_dev, route_slot, norm_gain, norm_bias, w_qkv, w_out, w_up, b_up, w_down,
    b_down, mask_token, pos_table, cotangent,
):
    count = lax.axis_size("pix")
    reps = lax.axis_size("rep")
    devices = count * reps
    pixels, slots, width = tokens.shape
    cap = max(2, (2 * pixels + count - 1) // count)
    extra = 2
    smem = pl.BlockSpec(memory_space=pltpu.SMEM)
    vmem = pl.BlockSpec(memory_space=pltpu.VMEM)
    anywhere = pl.BlockSpec(memory_space=pl.ANY)
    pix = lax.axis_index("pix")
    rep = lax.axis_index("rep")
    core, side, me = (value.reshape(1).astype(jnp.int32) for value in (rep % 2, rep // 2 % 2, pix))
    payload, pos_rows, route = prep(tokens, lengths, masked, route_dev, count, cap, extra, me)
    block = cap + extra
    recv = lax.all_to_all(
        payload.reshape(count, block, VIS, width), "pix", split_axis=0, concat_axis=0, tiled=True
    ).reshape(count * block, VIS, width)
    chunk = -(-(3072 + small_rows(slots)) // devices)
    chunk += -chunk % 8
    half = devices // 2
    direct = count <= 8
    dec, keep, send, *back = main_call(
        (
            core, me, route, route_slot, recv, cotangent, w_qkv, w_out, w_up, w_down, b_up, b_down,
            norm_gain.reshape(4, width), norm_bias.reshape(4, width), mask_token.reshape(1, width), pos_table,
        ),
        cap,
        extra,
        count,
        devices * chunk,
        count if direct else 1,
    )
    axes = ("pix", "rep")
    swap = [(i, i ^ 1) for i in range(devices)]
    groups = [[2 * i + side for i in range(half)] for side in range(2)]

    def exchange(values):
        return lax.all_to_all(
            values, axes, split_axis=0, concat_axis=0, axis_index_groups=groups, tiled=True
        )

    theirs = lax.ppermute(send, axes, swap)
    quarter = jax.ShapeDtypeStruct((count, chunk, 128), BF)
    line = pltpu.VMEM((count, 2, chunk, 128), BF)
    keep, send = pl.pallas_call(
        pair_sum_kernel,
        out_shape=(quarter, quarter),
        in_specs=[smem, anywhere, anywhere],
        out_specs=(vmem, vmem),
        scratch_shapes=[line, line, pltpu.SemaphoreType.DMA((2,))],
        compiler_params=pltpu.CompilerParams(vmem_limit_bytes=4 * MIB),
        name="pair_sum",
    )(side, keep.reshape(count, 2, chunk, 128), theirs.reshape(count, 2, chunk, 128))
    theirs = lax.ppermute(send, axes, [(i, i ^ 2) for i in range(devices)])
    gone = {}

    def tie(values, steps):
        tied, *some = lax.optimization_barrier((values, *[gone[step] for step in steps if step in gone]))
        gone.update(zip([step for step in steps if step in gone], some))
        return tied

    if direct:
        for step in range(1, count):
            gone[step] = lax.ppermute(back[step], "pix", [(i, (i - step) % count) for i in range(count)])
    theirs = tie(theirs, FIRST)
    line = pltpu.VMEM((count, chunk, 128), BF)
    paired = pl.pallas_call(
        quad_sum_kernel,
        out_shape=quarter,
        in_specs=[anywhere, anywhere],
        out_specs=vmem,
        scratch_shapes=[line, line, pltpu.SemaphoreType.DMA((2,))],
        compiler_params=pltpu.CompilerParams(vmem_limit_bytes=4 * MIB),
        name="quad_sum",
    )(keep, theirs)
    if direct:
        returned = []
    else:
        turn = (pix - jnp.arange(count)) % count
        blocks = lax.all_to_all(
            back[0].reshape(count, cap, VIS, width)[turn], "pix", split_axis=0, concat_axis=0, tiled=True
        )
        returned = [blocks[(pix + jnp.arange(count)) % count].reshape(count * cap, VIS, width)]
    parts = lax.all_to_all(paired, "pix", split_axis=0, concat_axis=0, tiled=True)
    spread = pl.pallas_call(
        chunk_sum_kernel,
        out_shape=jax.ShapeDtypeStruct((half, chunk, 128), BF),
        in_specs=[anywhere],
        out_specs=anywhere,
        scratch_shapes=[line, pltpu.VMEM((chunk, 128), BF), pltpu.SemaphoreType.DMA((half,))],
        compiler_params=pltpu.CompilerParams(vmem_limit_bytes=4 * MIB),
        name="chunk_sum",
    )(parts)
    spread = tie(spread, MIDDLE)
    summed = tie(exchange(spread).reshape(half * chunk, 128), LAST)
    if direct:
        returned = [back[0]] + [gone[step] for step in range(1, count)]
    other = lax.ppermute(summed, axes, swap)
    small = ((4, width), (4, width), b_up.shape, b_down.shape, (1, width), pos_table.shape)
    large = tuple(w.shape for w in (w_qkv, w_out, w_up, w_down))
    gain, bias, bup, bdown, mask, pos, qkv, out, up, down = pl.pallas_call(
        functools.partial(unpack_kernel, slots),
        out_shape=tuple(jax.ShapeDtypeStruct(shape, F32) for shape in small + large),
        in_specs=[smem, anywhere, anywhere],
        out_specs=(vmem,) * 6 + (anywhere,) * 4,
        scratch_shapes=[pltpu.VMEM(shape, F32) for shape in large]
        + [pltpu.VMEM((2, half * chunk, 128), BF), pltpu.SemaphoreType.DMA((10,))],
        compiler_params=pltpu.CompilerParams(vmem_limit_bytes=8 * MIB),
        name="unpack",
    )(core, summed, other)
    grad_tokens = pl.pallas_call(
        functools.partial(restore_kernel, cap, count, len(returned)),
        out_shape=jax.ShapeDtypeStruct((pixels * slots, width), F32),
        in_specs=[smem, smem, vmem] + [anywhere] * len(returned),
        out_specs=anywhere,
        scratch_shapes=[
            pltpu.VMEM((count * cap, VIS, width), BF),
            pltpu.VMEM((2 * GROUP * VIS, width), F32),
            pltpu.VMEM((pixels * slots, width), F32),
            pltpu.SemaphoreType.DMA((len(returned) + 1,)),
        ],
        compiler_params=pltpu.CompilerParams(vmem_limit_bytes=8 * MIB),
        name="restore",
    )(me, route, pos_rows, *returned)
    return (
        dec,
        grad_tokens.reshape(pixels, slots, width),
        gain.reshape(norm_gain.shape),
        bias.reshape(norm_bias.shape),
        qkv,
        out,
        up,
        bup,
        down,
        bdown,
        mask.reshape(width),
        pos,
    )


def solution(mesh):
    rows = P(("pix", "rep"))
    in_specs = (rows,) * 5 + (P(),) * 10 + (rows,)
    out_specs = (rows, rows) + (P(),) * 10
    return jax.shard_map(shards, mesh=mesh, in_specs=in_specs, out_specs=out_specs, check_vma=False)
```
